512 devices in a mesh: dp: 32 (over z, x), ctx: 16 (over y, core).
Axes of the slice: x: 4, y: 8, z: 8, core: 2. Of those that a mesh axis runs over, the one named last changes fastest.
Arguments:
- item_ids: int32 [2, 32, 2048], P(None, 'dp', 'ctx'), may hold values from 0 to 16383, as said below
- segments: int32 [32, 2048], P('dp', 'ctx'), may hold values from 0 to 31, never falling along the last dimension, each value on 1 to 512 neighbouring positions
- touched_rows: bfloat16 [16384, 512], P('dp'), may hold values from -6 to 6
- w_in: bfloat16 [512, 2048], replicated, may hold values from -0.25 to 0.25
- w_out: bfloat16 [512, 512], replicated, may hold values from -0.25 to 0.25
- out_grad: bfloat16 [32, 2048, 512], P('dp', 'ctx'), may hold values from -6 to 6
Outputs:
- layer_out: bfloat16 [32, 2048, 512], P('dp', 'ctx')
- table_grad: float32 [16384, 512], P('dp', 'ctx')
- w_in_grad: float32 [512, 2048], P('ctx', 'dp')
- w_out_grad: float32 [512, 512], P('ctx', 'dp')
The draws below stay inside these ranges and needn't reach their ends.
Inputs may be any that keep to these rules, and one draw needn't show every extreme that they name: `item_ids`: row r is held by owner r // 512. Among the 256 lookups of one device (both hashes of its events), no owner is named more than 32 times, and one owner exactly 32 times. `segments`: each user's events form one contiguous run of at most 512 events, and in every group one user has exactly 512.
All inputs are finite; a program needn't handle non-finite values.
Results may differ from the reference program's by a relative error of at most 0.034.
Values may be sent and summed in bfloat16 or wider, within the bound.
No kernel may reach another device: no remote copies, remote signals or barrier semaphores. Data moves between devices by JAX's collectives and lax.ppermute only.
A program may use at most 64 MiB of HBM per device.

```python
import math
import jax
import jax.numpy as jnp
import numpy as np
from jax import lax

D = 512
H = 8
DH = 64
EV_DEV = 128
TOUCH_DEV = 512
GROUPS = 32
SEQ = 2048
USERS = 32
MOST = 512
CAP = 32
ROWS = 16384


def draw_item_ids(key, part):
    key = jax.random.fold_in(key, 11)
    owners_count = ROWS // TOUCH_DEV
    ctx_count = SEQ // EV_DEV
    block_count = owners_count * ctx_count
    lookup_count = 2 * EV_DEV
    cold_count = lookup_count - CAP
    pool_count = cold_count + cold_count // 2
    block_key, scramble_key = jax.random.split(key)

    def one_block(this_key):
        hot_key, pick_key, order_key, top_key, low_key = jax.random.split(this_key, 5)
        hot_owner = jax.random.randint(hot_key, (), 0, owners_count)
        picks = jax.random.permutation(pick_key, pool_count)[:cold_count]
        cold_owner = (hot_owner + 1 + picks % (owners_count - 1)) % owners_count
        owner_list = jnp.concatenate([jnp.full((CAP,), hot_owner, jnp.int32), cold_owner.astype(jnp.int32)])
        owner_list = owner_list[jax.random.permutation(order_key, lookup_count)]
        tops = jax.random.randint(top_key, (lookup_count,), 1, TOUCH_DEV + 1)
        lows = jax.random.randint(low_key, (lookup_count,), 0, tops)
        return (owner_list, lows)
    owner_all, low_all = jax.vmap(one_block)(jax.random.split(block_key, block_count))
    mult_key, shift_key = jax.random.split(scramble_key)
    multiplier = 2 * jax.random.randint(mult_key, (), 0, max(TOUCH_DEV // 2, 1)) + 1
    shifted = jax.random.randint(shift_key, (), 0, TOUCH_DEV)
    local_rows = (low_all * multiplier + shifted) % TOUCH_DEV
    row_ids = owner_all * TOUCH_DEV + local_rows
    row_ids = row_ids.reshape(owners_count, ctx_count, 2, EV_DEV)
    row_ids = jnp.transpose(row_ids, (2, 0, 1, 3)).reshape(2, owners_count, SEQ)
    return row_ids.astype(jnp.int32)


def strengthened(array, key, source, target, shards_of, factor):
    def block_of(axis_at):
        return (jnp.arange(array.shape[axis_at]) // (array.shape[axis_at] // shards_of)).reshape((-1,) + (1,) * (array.ndim - 1 - axis_at))

    one_side = jax.random.permutation(key, shards_of)[block_of(target)]
    second = (block_of(target) + shards_of // 2) % shards_of
    return jnp.where((block_of(source) == one_side) | (block_of(source) == second), factor * array, array)


def level_of(rng, shape, shards, least, high):
    factor_of = 1.0
    for dim, parts in shards:
        steps = jax.random.uniform(jax.random.fold_in(jax.random.fold_in(rng, 6), dim), (parts,), jnp.float32, least / len(shards), high / len(shards))
        factor_of = factor_of * jnp.repeat(jnp.exp(steps), shape[dim] // parts).reshape((-1,) + (1,) * (len(shape) - 1 - dim))
    return factor_of


def length_profile(count, total, reach, skew):
    weights = [(1 << 20) // math.isqrt(rank ** skew) + 1 for rank in range(2, count + 1)]
    spare, given = total - reach - (count - 1), [1] * (count - 1)
    while spare > 0:
        free = [i for i in range(count - 1) if given[i] < reach]
        mass, remaining = sum([weights[i] for i in free]), spare
        for i in free:
            more = min(reach - given[i], max(1, remaining * weights[i] // mass), spare)
            given[i] = given[i] + more
            spare = spare - more
    return np.array([reach] + given)


def uneven(key, number_of, total, bound, skew):
    if number_of == 2:
        one = jax.random.randint(key, (), max(1, total - bound), min(bound, total - 1) + 1)
        return jnp.stack([one, total - one])
    lengths = jnp.asarray(length_profile(number_of, total, bound, skew), jnp.int32)
    twos = (number_of - 1) // 2
    donor, sink = lengths[1:1 + 2 * twos:2], lengths[2:2 + 2 * twos:2]
    slack = jnp.minimum(donor - 1, bound - sink)
    moved = jax.random.randint(jax.random.fold_in(key, 1), (twos,), 0, 1 << 20) % (slack + 1)
    lengths = lengths.at[1:1 + 2 * twos:2].set(donor - moved).at[2:2 + 2 * twos:2].set(sink + moved)
    return lengths[jax.random.permutation(jax.random.fold_in(key, 2), number_of)]


def gaussian(key, shape, spread, reach, cuts=(), held_as=jnp.bfloat16):
    array = spread * jax.random.normal(key, shape, jnp.float32)
    if cuts:
        array = array * level_of(key, shape, cuts, -0.22, 0.18)
    return jnp.clip(array, -reach, reach).astype(held_as)


def noise_with(own_key, dims, scale, most, cuts, heavy, kind=jnp.bfloat16):
    drawn = scale * jax.random.normal(own_key, dims, jnp.float32)
    if cuts:
        drawn = drawn * level_of(own_key, dims, cuts, -0.22, 0.18)
    return jnp.clip(strengthened(drawn, jax.random.fold_in(own_key, 3), *heavy), -most, most).astype(kind)


def setup_inputs(seed: int = 0) -> dict:
    streams_of = jax.random.split(jax.random.key(seed), 7)
    item_ids = draw_item_ids(jax.random.fold_in(streams_of[6], 71), 0)
    segments = jax.vmap(lambda own: jnp.searchsorted(jnp.cumsum(uneven(own, USERS, SEQ, MOST, 2)), jnp.arange(SEQ), side="right"))(jax.random.split(streams_of[1], GROUPS)).reshape((GROUPS, SEQ)).astype(jnp.int32)
    touched_rows = gaussian(streams_of[2], (ROWS, D), 1.0, 6.0, ((0, 32),))
    w_in = gaussian(streams_of[3], (D, 4 * D), D ** -0.5, 0.25)
    w_out = gaussian(streams_of[4], (D, D), D ** -0.5, 0.25)
    out_grad = noise_with(streams_of[5], (GROUPS, SEQ, D), 0.25, 6.0, ((0, 32), (1, 16)), (0, 2, 32, 2.75))
    return {"item_ids": item_ids, "segments": segments, "touched_rows": touched_rows, "w_in": w_in, "w_out": w_out, "out_grad": out_grad}


epsilon = 1e-05

def layer_norm(values):
    centered = values - lax.optimization_barrier(jnp.mean(values, axis=-1, keepdims=True))
    inverse = lax.rsqrt(lax.optimization_barrier(jnp.mean(centered * centered, axis=-1, keepdims=True)) + epsilon)
    return (centered * inverse, inverse)

def norm_backward(normed, inverse, upstream):
    first_mean = lax.optimization_barrier(jnp.mean(upstream, axis=-1, keepdims=True))
    second_mean = lax.optimization_barrier(jnp.mean(upstream * normed, axis=-1, keepdims=True))
    return inverse * (upstream - first_mean - normed * second_mean)

def silu_slope(values):
    sigmoid = jax.nn.sigmoid(values)
    return sigmoid * (1.0 + values * (1.0 - sigmoid))

def block_partials(left_rows, right_rows):
    blocks = SEQ // EV_DEV
    left_blocks = left_rows.reshape(blocks, EV_DEV, left_rows.shape[1])
    right_blocks = right_rows.reshape(blocks, EV_DEV, right_rows.shape[1])

    def one_block(both_blocks):
        return jnp.dot(both_blocks[0].T, both_blocks[1], preferred_element_type=jnp.float32).astype(jnp.bfloat16)
    pieces = lax.map(one_block, (left_blocks, right_blocks))
    pieces = lax.optimization_barrier(pieces)
    return lax.optimization_barrier(jnp.sum(pieces.astype(jnp.float32), axis=0))

def group_pass(touched_rows, w_in, w_out, group_data):
    lookup_ids, user_ids, grad_rows = group_data
    score_scale = 1.0 / math.sqrt(DH)
    back_blocks = MOST // EV_DEV
    margin = back_blocks * EV_DEV
    first_rows = jnp.take(touched_rows, lookup_ids[0], axis=0).astype(jnp.float32)
    second_rows = jnp.take(touched_rows, lookup_ids[1], axis=0).astype(jnp.float32)
    inputs = (first_rows + second_rows).astype(jnp.bfloat16)
    inputs_f = inputs.astype(jnp.float32)
    input_hat, input_inv = layer_norm(inputs_f)
    normed = input_hat.astype(jnp.bfloat16)
    projected = jnp.dot(normed, w_in, preferred_element_type=jnp.float32)
    activated = jax.nn.silu(projected).astype(jnp.bfloat16)
    gates = activated[:, :D].astype(jnp.float32)
    value_rows = activated[:, D:2 * D]
    query_rows = activated[:, 2 * D:3 * D]
    key_rows = activated[:, 3 * D:]
    user_plus = user_ids + 1
    pad_rows = jnp.zeros((margin, D), jnp.bfloat16)
    key_padded = jnp.concatenate([pad_rows, key_rows]).reshape(-1, H, DH)
    value_padded = jnp.concatenate([pad_rows, value_rows]).reshape(-1, H, DH)
    user_padded = jnp.concatenate([jnp.zeros((margin,), jnp.int32), user_plus])
    query_heads = query_rows.reshape(SEQ, H, DH)

    def window(block):
        block_start = (block * EV_DEV).astype(jnp.int32)
        query_block = lax.dynamic_slice_in_dim(query_heads, block_start, EV_DEV, 0)
        key_block = lax.dynamic_slice_in_dim(key_padded, block_start, EV_DEV + margin, 0)
        value_block = lax.dynamic_slice_in_dim(value_padded, block_start, EV_DEV + margin, 0)
        query_users = lax.dynamic_slice_in_dim(user_plus, block_start, EV_DEV, 0)
        key_users = lax.dynamic_slice_in_dim(user_padded, block_start, EV_DEV + margin, 0)
        row_index = jnp.arange(EV_DEV, dtype=jnp.int32)[:, None]
        col_index = jnp.arange(EV_DEV + margin, dtype=jnp.int32)[None, :]
        allowed = (query_users[:, None] == key_users[None, :]) & (col_index <= row_index + margin)
        scores = jnp.einsum('qhd,khd->hqk', query_block.astype(jnp.float32), key_block.astype(jnp.float32)) * score_scale
        weights = jnp.where(allowed[None], jax.nn.silu(scores), 0.0).astype(jnp.bfloat16)
        return (block_start, scores, allowed, weights, query_block, key_block, value_block)

    def attend(block):
        block_start, scores, allowed, weights, query_block, key_block, value_block = window(block)
        return jnp.einsum('hqk,khd->qhd', weights.astype(jnp.float32), value_block.astype(jnp.float32)).reshape(EV_DEV, D)
    blocks = SEQ // EV_DEV
    attended = lax.map(attend, jnp.arange(blocks, dtype=jnp.int32)).reshape(SEQ, D)
    att_hat, att_inv = layer_norm(attended)
    mixed = (att_hat * gates).astype(jnp.bfloat16)
    layer_out = (inputs_f + jnp.dot(mixed, w_out, preferred_element_type=jnp.float32)).astype(jnp.bfloat16)
    grad_f = grad_rows.astype(jnp.float32)
    mixed_grad = jnp.dot(grad_rows, w_out.T, preferred_element_type=jnp.float32)
    gate_grad = mixed_grad * att_hat
    attended_grad = norm_backward(att_hat, att_inv, mixed_grad * gates).astype(jnp.bfloat16)
    grad_heads = attended_grad.reshape(SEQ, H, DH)

    def backward_step(carry, block):
        key_acc, value_acc = carry
        block_start, scores, allowed, weights, query_block, key_block, value_block = window(block)
        grad_block = lax.dynamic_slice_in_dim(grad_heads, block_start, EV_DEV, 0)
        prob_grad = jnp.einsum('qhd,khd->hqk', grad_block.astype(jnp.float32), value_block.astype(jnp.float32))
        score_grad = jnp.where(allowed[None], prob_grad * silu_slope(scores), 0.0).astype(jnp.bfloat16)
        score_f = score_grad.astype(jnp.float32)
        query_part = jnp.einsum('hqk,khd->qhd', score_f, key_block.astype(jnp.float32)) * score_scale
        key_part = jnp.einsum('hqk,qhd->khd', score_f, query_block.astype(jnp.float32)) * score_scale
        value_part = jnp.einsum('hqk,qhd->khd', weights.astype(jnp.float32), grad_block.astype(jnp.float32))
        key_old = lax.dynamic_slice_in_dim(key_acc, block_start, EV_DEV + margin, 0)
        value_old = lax.dynamic_slice_in_dim(value_acc, block_start, EV_DEV + margin, 0)
        key_acc = lax.dynamic_update_slice_in_dim(key_acc, key_old + key_part, block_start, 0)
        value_acc = lax.dynamic_update_slice_in_dim(value_acc, value_old + value_part, block_start, 0)
        return ((key_acc, value_acc), query_part.reshape(EV_DEV, D))
    zero_acc = jnp.zeros((SEQ + margin, H, DH), jnp.float32)
    (key_acc, value_acc), query_parts = lax.scan(backward_step, (zero_acc, zero_acc), jnp.arange(blocks, dtype=jnp.int32))
    query_grad = query_parts.reshape(SEQ, D)
    key_grad = key_acc[margin:].reshape(SEQ, D)
    value_grad = value_acc[margin:].reshape(SEQ, D)
    joined = jnp.concatenate([gate_grad, value_grad, query_grad, key_grad], axis=1)
    projected_grad = (joined * silu_slope(projected)).astype(jnp.bfloat16)
    normed_grad = jnp.dot(projected_grad, w_in.T, preferred_element_type=jnp.float32)
    inputs_grad = (grad_f + norm_backward(input_hat, input_inv, normed_grad)).astype(jnp.bfloat16)
    w_in_grad = block_partials(normed, projected_grad)
    w_out_grad = block_partials(mixed, grad_rows)
    return (layer_out, inputs_grad, w_in_grad, w_out_grad)

def reference(item_ids, segments, touched_rows, w_in, w_out, out_grad):

    def run_group(group_data):
        return group_pass(touched_rows, w_in, w_out, group_data)
    layer_out, inputs_grad, w_in_grads, w_out_grads = lax.map(run_group, (jnp.transpose(item_ids, (1, 0, 2)), segments, out_grad))
    flat_grad = inputs_grad.reshape(-1, D).astype(jnp.float32)
    table_grad = jax.ops.segment_sum(flat_grad, item_ids[0].reshape(-1), num_segments=ROWS)
    table_grad = table_grad + jax.ops.segment_sum(flat_grad, item_ids[1].reshape(-1), num_segments=ROWS)
    w_in_grad = lax.optimization_barrier(jnp.sum(w_in_grads, axis=0))
    w_out_grad = lax.optimization_barrier(jnp.sum(w_out_grads, axis=0))
    return (layer_out, table_grad, w_in_grad, w_out_grad)
```

```python
import math

import jax
import jax.numpy as jnp
from jax import lax
from jax.sharding import PartitionSpec as P

H = 8
DH = 64


epsilon = 1e-05


def passed_along(block, axis, distance):
    devices = range(lax.axis_size(axis))
    route = [(i - distance, i) for i in devices if i - distance in devices]
    return lax.ppermute(block, axis, route)


def layer_norm(values):
    centered = values - jnp.mean(values, axis=-1, keepdims=True)
    inverse = lax.rsqrt(jnp.mean(centered * centered, axis=-1, keepdims=True) + epsilon)
    return (centered * inverse, inverse)


def norm_backward(normed, inverse, upstream):
    first_mean = jnp.mean(upstream, axis=-1, keepdims=True)
    second_mean = jnp.mean(upstream * normed, axis=-1, keepdims=True)
    return inverse * (upstream - first_mean - normed * second_mean)


def silu_slope(values):
    sigmoid = jax.nn.sigmoid(values)
    return sigmoid * (1.0 + values * (1.0 - sigmoid))


def scatter_ctx(terms, core):
    devices = lax.axis_size("ctx")
    chips = devices // 2
    rows = terms.shape[0] // devices
    slabs = terms.reshape(chips, 2, rows, terms.shape[1])
    kept = lax.dynamic_index_in_dim(slabs, core, 1, keepdims=False)
    sent = lax.dynamic_index_in_dim(slabs, 1 - core, 1, keepdims=False)
    got = lax.ppermute(sent, "ctx", [(i, i ^ 1) for i in range(devices)])
    chip_sum = (kept.astype(jnp.float32) + got.astype(jnp.float32)).astype(jnp.bfloat16)
    groups = [list(range(first, devices, 2)) for first in range(2)]
    spread = lax.all_to_all(
        chip_sum, "ctx", split_axis=0, concat_axis=0, tiled=True, axis_index_groups=groups
    )
    return jnp.sum(spread.astype(jnp.float32), axis=0)


def local(item_ids, segments, touched_rows, w_in, w_out, out_grad):
    rows_dev = segments.shape[1]
    model_width = w_in.shape[0]
    table_dev = touched_rows.shape[0]
    owners_count = lax.axis_size("dp")
    ctx_count = lax.axis_size("ctx")
    capacity = max(rows_dev // 4, 6 * rows_dev // owners_count + 2)
    reach_blocks = min(4, ctx_count // 2)
    margin = reach_blocks * rows_dev
    score_scale = 1.0 / math.sqrt(DH)
    lookups = item_ids.reshape(2 * rows_dev)
    owner_of = lookups // table_dev
    local_row = lookups % table_dev
    member = (owner_of[:, None] == jnp.arange(owners_count, dtype=jnp.int32)[None, :]).astype(
        jnp.int32
    )
    slot_rank = jnp.sum(jnp.cumsum(member, axis=0) * member, axis=1) - 1
    slot_index = owner_of * capacity + slot_rank
    requests = jnp.full((owners_count * capacity,), -1, jnp.int32).at[slot_index].set(local_row)
    requests = requests.reshape(owners_count, capacity)
    asked_rows = lax.all_to_all(requests, "dp", split_axis=0, concat_axis=0, tiled=True)
    present = asked_rows >= 0
    found_rows = jnp.take(touched_rows, jnp.maximum(asked_rows, 0), axis=0)
    found_rows = jnp.where(present[..., None], found_rows, jnp.zeros((), found_rows.dtype))
    fetched = lax.all_to_all(found_rows, "dp", split_axis=0, concat_axis=0, tiled=True)
    embedded = jnp.take(
        fetched.reshape(owners_count * capacity, model_width), slot_index, axis=0
    ).astype(jnp.float32)
    inputs = (embedded[:rows_dev] + embedded[rows_dev:]).astype(jnp.bfloat16)
    inputs_f = inputs.astype(jnp.float32)
    input_hat, input_inv = layer_norm(inputs_f)
    normed = input_hat.astype(jnp.bfloat16)
    projected = jnp.dot(normed, w_in, preferred_element_type=jnp.float32)
    activated = jax.nn.silu(projected).astype(jnp.bfloat16)
    gates = activated[:, :model_width].astype(jnp.float32)
    value_rows = activated[:, model_width : 2 * model_width]
    query_rows = activated[:, 2 * model_width : 3 * model_width]
    key_rows = activated[:, 3 * model_width :]
    user_plus = segments[0] + 1
    far_keys = []
    far_values = []
    far_users = []
    for offset in range(reach_blocks, 0, -1):
        got_keys, got_values, got_users = passed_along(
            (key_rows, value_rows, user_plus), "ctx", offset
        )
        far_keys.append(got_keys)
        far_values.append(got_values)
        far_users.append(got_users)
    key_heads = jnp.concatenate(far_keys + [key_rows]).reshape(-1, H, DH)
    value_heads = jnp.concatenate(far_values + [value_rows]).reshape(-1, H, DH)
    key_users = jnp.concatenate(far_users + [user_plus])
    query_heads = query_rows.reshape(rows_dev, H, DH)
    row_index = jnp.arange(rows_dev, dtype=jnp.int32)[:, None]
    col_index = jnp.arange(margin + rows_dev, dtype=jnp.int32)[None, :]
    allowed = (user_plus[:, None] == key_users[None, :]) & (col_index <= row_index + margin)
    scores = (
        jnp.einsum("qhd,khd->hqk", query_heads, key_heads, preferred_element_type=jnp.float32)
        * score_scale
    )
    weights = jnp.where(allowed[None], jax.nn.silu(scores), 0.0).astype(jnp.bfloat16)
    attended = jnp.einsum(
        "hqk,khd->qhd", weights, value_heads, preferred_element_type=jnp.float32
    ).reshape(rows_dev, model_width)
    att_hat, att_inv = layer_norm(attended)
    mixed = (att_hat * gates).astype(jnp.bfloat16)
    grad_rows = out_grad[0]
    layer_out = (inputs_f + jnp.dot(mixed, w_out, preferred_element_type=jnp.float32)).astype(
        jnp.bfloat16
    )
    mixed_grad = jnp.einsum("re,de->rd", grad_rows, w_out, preferred_element_type=jnp.float32)
    gate_grad = mixed_grad * att_hat
    attended_grad = norm_backward(att_hat, att_inv, mixed_grad * gates).astype(jnp.bfloat16)
    grad_heads = attended_grad.reshape(rows_dev, H, DH)
    prob_grad = jnp.einsum(
        "qhd,khd->hqk", grad_heads, value_heads, preferred_element_type=jnp.float32
    )
    score_grad = jnp.where(allowed[None], prob_grad * silu_slope(scores), 0.0).astype(jnp.bfloat16)
    query_grad = (
        jnp.einsum("hqk,khd->qhd", score_grad, key_heads, preferred_element_type=jnp.float32)
        * score_scale
    ).reshape(rows_dev, model_width)
    key_all = (
        jnp.einsum("hqk,qhd->khd", score_grad, query_heads, preferred_element_type=jnp.float32)
        * score_scale
    ).reshape(-1, model_width)
    value_all = jnp.einsum(
        "hqk,qhd->khd", weights, grad_heads, preferred_element_type=jnp.float32
    ).reshape(-1, model_width)
    key_grad = key_all[margin:]
    value_grad = value_all[margin:]
    for offset in range(1, reach_blocks + 1):
        block_start = (reach_blocks - offset) * rows_dev
        back_keys, back_values = (
            passed_along(
                key_all[block_start : block_start + rows_dev].astype(jnp.bfloat16), "ctx", -offset
            ).astype(jnp.float32),
            passed_along(
                value_all[block_start : block_start + rows_dev].astype(jnp.bfloat16), "ctx", -offset
            ).astype(jnp.float32),
        )
        key_grad = key_grad + back_keys
        value_grad = value_grad + back_values
    joined = jnp.concatenate([gate_grad, value_grad, query_grad, key_grad], axis=1)
    projected_grad = (joined * silu_slope(projected)).astype(jnp.bfloat16)
    normed_grad = jnp.einsum("re,de->rd", projected_grad, w_in, preferred_element_type=jnp.float32)
    inputs_grad = (
        grad_rows.astype(jnp.float32) + norm_backward(input_hat, input_inv, normed_grad)
    ).astype(jnp.bfloat16)
    w_in_part = jnp.einsum("rd,re->de", normed, projected_grad, preferred_element_type=jnp.float32)
    w_out_part = jnp.einsum("rd,re->de", mixed, grad_rows, preferred_element_type=jnp.float32)
    core = lax.axis_index("ctx") % 2
    w_part = jnp.concatenate([w_in_part, w_out_part], axis=1).astype(jnp.bfloat16)
    w_share = scatter_ctx(w_part, core)
    w_cols = w_share.astype(jnp.bfloat16)
    width = w_in.shape[1]
    dp_in = w_cols[:, :width].reshape(-1, owners_count, width // owners_count)
    dp_out = w_cols[:, width:].reshape(-1, owners_count, model_width // owners_count)
    dp_send = jnp.concatenate([dp_in, dp_out], axis=2).transpose(1, 0, 2)
    dp_got = lax.all_to_all(dp_send, "dp", split_axis=0, concat_axis=0, tiled=True)
    w_total = jnp.sum(dp_got.astype(jnp.float32), axis=0)
    w_in_grad = w_total[:, : width // owners_count]
    w_out_grad = w_total[:, width // owners_count :]
    lookup_grads = jnp.concatenate([inputs_grad, inputs_grad])
    outgoing = (
        jnp.zeros((owners_count * capacity, model_width), jnp.bfloat16)
        .at[slot_index]
        .set(lookup_grads)
    )
    outgoing = outgoing.reshape(owners_count, capacity, model_width)
    arrived = lax.all_to_all(outgoing, "dp", split_axis=0, concat_axis=0, tiled=True)
    row_of = jnp.arange(table_dev, dtype=jnp.int32)[None, :]
    hits = (asked_rows.reshape(-1)[:, None] == row_of).astype(jnp.bfloat16)
    accumulated = jnp.einsum(
        "sd,sr->dr", arrived.reshape(-1, model_width), hits, preferred_element_type=jnp.float32
    )
    table_grad = scatter_ctx(accumulated.astype(jnp.bfloat16), core).T
    return (layer_out[None], table_grad, w_in_grad, w_out_grad)


def solution(mesh):
    return jax.shard_map(
        local,
        mesh=mesh,
        in_specs=(
            P(None, "dp", "ctx"),
            P("dp", "ctx"),
            P("dp", None),
            P(),
            P(),
            P("dp", "ctx", None),
        ),
        out_specs=(P("dp", "ctx", None), P("dp", "ctx"), P("ctx", "dp"), P("ctx", "dp")),
        check_vma=False,
    )
```

```python
import math

import jax
import jax.numpy as jnp
from jax import lax
from jax.experimental import pallas as pl
from jax.experimental.pallas import tpu as pltpu
from jax.sharding import PartitionSpec as P

H = 8
DH = 64
X_CHIPS = 4
REACH = 4
USER_ROWS = 16

epsilon = 1e-05
f32 = jnp.float32
bf16 = jnp.bfloat16


def passed_along(block, axis, distance):
    devices = range(lax.axis_size(axis))
    route = [(i - distance, i) for i in devices if i - distance in devices]
    return lax.ppermute(block, axis, route)


def layer_norm(values):
    centered = values - jnp.mean(values, axis=-1, keepdims=True)
    inverse = lax.rsqrt(jnp.mean(centered * centered, axis=-1, keepdims=True) + epsilon)
    return (centered * inverse, inverse)


def norm_backward(normed, inverse, upstream):
    first_mean = jnp.mean(upstream, axis=-1, keepdims=True)
    second_mean = jnp.mean(upstream * normed, axis=-1, keepdims=True)
    return inverse * (upstream - first_mean - normed * second_mean)


def sigmoid(values):
    return 0.5 * jnp.tanh(0.5 * values) + 0.5


def silu_slope(values):
    sig = sigmoid(values)
    return sig * (1.0 + values * (1.0 - sig))


def iota(shape, dim):
    return lax.broadcasted_iota(jnp.int32, shape, dim)


def dot(left, right):
    return jnp.dot(left, right, preferred_element_type=f32)


def dot_nt(left, right):
    return lax.dot_general(left, right, (((1,), (1,)), ((), ())), preferred_element_type=f32)


def dot_tn(left, right):
    return lax.dot_general(left, right, (((0,), (0,)), ((), ())), preferred_element_type=f32)


def hot(condition):
    return condition.astype(f32).astype(bf16)


def as_column(row):
    length = row.shape[1]
    eye = iota((length, length), 0) == iota((length, length), 1)
    return jnp.sum(jnp.where(eye, jnp.broadcast_to(row, (length, length)), 0.0), axis=1, keepdims=True)


def both_heads(pair):
    low = iota(pair.shape, 1) < DH
    zero = jnp.zeros_like(pair)
    return jnp.concatenate([jnp.where(low, pair, zero), jnp.where(low, zero, pair)], axis=0)


def one_pair(stacked):
    rows = stacked.shape[0] // 2
    low = iota((rows, stacked.shape[1]), 1) < DH
    return jnp.where(low, stacked[:rows], stacked[rows:])


def call(body, outs, *operands, flops=0, moved=0):
    return pl.pallas_call(
        body,
        out_shape=[jax.ShapeDtypeStruct(shape, kind) for shape, kind in outs],
        compiler_params=pltpu.CompilerParams(vmem_limit_bytes=40 * 1024 * 1024),
        cost_estimate=pl.CostEstimate(flops=flops, bytes_accessed=moved, transcendentals=0),
    )(*operands)


def route_body(table_dev, ids_ref, request_ref, slot_ref):
    owners, capacity = request_ref.shape
    ids = ids_ref[...]
    count = ids.shape[0]
    shift = table_dev.bit_length() - 1
    owner = jnp.right_shift(ids, shift)
    row = jnp.bitwise_and(ids, table_dev - 1)
    member_f = (owner == iota((count, owners), 1)).astype(f32)
    member = member_f.astype(bf16)
    earlier = hot(iota((count, count), 0) > iota((count, count), 1))
    rank = jnp.sum(dot(earlier, member) * member_f, axis=1, keepdims=True).astype(jnp.int32)
    rank_hot = hot(rank == iota((count, capacity), 1))
    high = (member_f * jnp.right_shift(row, 4).astype(f32)).astype(bf16)
    low = (member_f * jnp.bitwise_and(row, 15).astype(f32)).astype(bf16)
    found = 16.0 * dot_tn(high, rank_hot) + dot_tn(low, rank_hot) + dot_tn(member, rank_hot)
    request_ref[...] = found.astype(jnp.int32) - 1
    slot_ref[...] = owner * capacity + rank


def gather_body(asked_ref, table_ref, found_ref):
    slots = asked_ref.shape[1]
    hits = hot(iota((table_ref.shape[0], slots), 0) == asked_ref[...])
    found_ref[...] = dot_tn(hits, table_ref[...]).astype(bf16)


def slot_matrix(slot, slots):
    events = slot.shape[0] // 2
    places = iota((events, slots), 1)
    return hot((slot[:events] == places) | (slot[events:] == places))


def embed_body(slot_ref, fetched_ref, user_ref, inputs_ref, packed_ref):
    rows = inputs_ref.shape[0]
    places = slot_matrix(slot_ref[...], fetched_ref.shape[0])
    inputs = dot(places, fetched_ref[...]).astype(bf16)
    inputs_ref[...] = inputs
    packed_ref[:rows, :] = layer_norm(inputs.astype(f32))[0].astype(bf16)
    packed_ref[rows:, :] = user_rows(user_ref[...], packed_ref.shape[1])


def user_rows(user, width):
    wide = jnp.concatenate([user, jnp.zeros((1, width - user.shape[1]), f32)], axis=1)
    return jnp.broadcast_to(wide, (USER_ROWS, width)).astype(bf16)


def project_body(
    packed_ref, w_in_ref, w_out_ref, grad_ref, user_ref,
    projected_ref, gates_ref, values_ref, queries_ref, keys_ref, mixed_grad_ref,
):
    rows = grad_ref.shape[0]
    width = grad_ref.shape[1]
    normed = packed_ref[:rows, :]
    for part, out_ref in enumerate((gates_ref, values_ref, queries_ref, keys_ref)):
        columns = slice(part * width, (part + 1) * width)
        projected = dot(normed, w_in_ref[:, columns])
        projected_ref[:, columns] = projected
        out_ref[:rows, :] = (projected * sigmoid(projected)).astype(bf16)
    queries_ref[rows:, :] = user_rows(user_ref[...], width)
    mixed_grad_ref[...] = dot_nt(grad_ref[...], w_out_ref[...])


def window_mask(user_row, key_user_row, margin):
    rows = user_row.shape[1]
    columns = key_user_row.shape[1]
    user_column = as_column(user_row)
    allowed = (user_column == key_user_row) & (
        iota((rows, columns), 1) <= iota((rows, columns), 0) + margin
    )
    weight = allowed.astype(f32)
    return jnp.concatenate([weight, weight], axis=0) > 0.0


def forward_body(
    halo4_ref, halo3_ref, halo2_ref, halo1_ref, values_ref, keys_ref, queries_ref, gates_ref,
    inputs_ref, mixed_grad_ref, w_in_ref, w_out_ref, user_ref,
    out_ref, mixed_ref, gate_grad_ref, att_grad_ref, all_keys_ref, all_values_ref, key_user_ref,
):
    rows, width = inputs_ref.shape
    score_scale = 1.0 / math.sqrt(DH)
    halos = (halo4_ref, halo3_ref, halo2_ref, halo1_ref)
    far = jnp.concatenate([halo[:rows, :] for halo in halos], axis=0)
    margin = far.shape[0]
    for part, own_ref, all_ref in ((1, values_ref, all_values_ref), (3, keys_ref, all_keys_ref)):
        projected = dot(far, w_in_ref[:, part * width : (part + 1) * width])
        all_ref[:margin, :] = (projected * sigmoid(projected)).astype(bf16)
        all_ref[margin:, :] = own_ref[...]
    user_row = user_ref[...]
    key_user = jnp.concatenate(
        [halo[rows : rows + 1, :rows].astype(f32) for halo in halos] + [user_row], axis=1
    )
    key_user_ref[...] = key_user
    allowed = window_mask(user_row, key_user, margin)
    parts = []
    for pair in range(H // 2):
        columns = slice(2 * DH * pair, 2 * DH * (pair + 1))
        scores = dot_nt(both_heads(queries_ref[:rows, columns]), all_keys_ref[:, columns]) * score_scale
        weights = jnp.where(allowed, scores * sigmoid(scores), 0.0).astype(bf16)
        parts.append(one_pair(dot(weights, all_values_ref[:, columns])))
    att_hat, att_inv = layer_norm(jnp.concatenate(parts, axis=1))
    gates = gates_ref[...].astype(f32)
    mixed = (att_hat * gates).astype(bf16)
    mixed_ref[...] = mixed
    out_ref[...] = (inputs_ref[...].astype(f32) + dot(mixed, w_out_ref[...])).astype(bf16)
    mixed_grad = mixed_grad_ref[...]
    gate_grad_ref[...] = mixed_grad * att_hat
    att_grad_ref[...] = norm_backward(att_hat, att_inv, mixed_grad * gates).astype(bf16)


def split_by_core(core, section, terms, kept_ref, sent_ref):
    devices = 2 * kept_ref.shape[1]
    rows = terms.shape[0] // devices
    lanes = terms.shape[1] // X_CHIPS
    even = core == 0
    for x in range(X_CHIPS):
        for chip in range(devices // 2):
            first = terms[2 * chip * rows : (2 * chip + 1) * rows, x * lanes : (x + 1) * lanes]
            second = terms[(2 * chip + 1) * rows : (2 * chip + 2) * rows, x * lanes : (x + 1) * lanes]
            place = (x, chip, slice(None), slice(section * lanes, (section + 1) * lanes))
            kept_ref[place] = jnp.where(even, first, second).astype(bf16)
            sent_ref[place] = jnp.where(even, second, first).astype(bf16)


def order_by_x(block, piece):
    width = block.shape[1]
    old = iota((width, width), 0)
    new = iota((width, width), 1)
    per_x = width // X_CHIPS
    inner = jnp.bitwise_and(old, piece - 1)
    owner = jnp.right_shift(old, piece.bit_length() - 1)
    x = jnp.bitwise_and(owner, X_CHIPS - 1)
    z = jnp.right_shift(owner, X_CHIPS.bit_length() - 1)
    return dot(block, hot(new == x * per_x + z * piece + inner)).astype(bf16)


def query_body(
    piece_in, piece_out, core_ref, queries_ref, all_keys_ref, all_values_ref, att_grad_ref, gate_grad_ref,
    projected_ref, user_ref, key_user_ref, packed_ref, mixed_ref, grad_ref,
    gate_query_ref, kept_ref, sent_ref,
):
    rows, width = grad_ref.shape
    score_scale = 1.0 / math.sqrt(DH)
    margin = all_keys_ref.shape[0] - rows
    allowed = window_mask(user_ref[...], key_user_ref[...], margin)
    parts = []
    for pair in range(H // 2):
        columns = slice(2 * DH * pair, 2 * DH * (pair + 1))
        keys = all_keys_ref[:, columns]
        scores = dot_nt(both_heads(queries_ref[:rows, columns]), keys) * score_scale
        prob_grad = dot_nt(both_heads(att_grad_ref[:, columns]), all_values_ref[:, columns])
        score_grad = jnp.where(allowed, prob_grad * silu_slope(scores), 0.0).astype(bf16)
        parts.append(one_pair(dot(score_grad, keys)) * score_scale)
    query_grad = jnp.concatenate(parts, axis=1)
    core = core_ref[0]
    normed = packed_ref[:rows, :]
    gate_part = (gate_grad_ref[...] * silu_slope(projected_ref[:, :width])).astype(bf16)
    query_part = (query_grad * silu_slope(projected_ref[:, 2 * width : 3 * width])).astype(bf16)
    gate_query_ref[:, :width] = gate_part
    gate_query_ref[:, width:] = query_part
    split_by_core(core, 0, dot_tn(normed, order_by_x(gate_part, piece_in)), kept_ref, sent_ref)
    split_by_core(core, 1, dot_tn(normed, order_by_x(query_part, piece_in)), kept_ref, sent_ref)
    split_by_core(core, 2, dot_tn(mixed_ref[...], order_by_x(grad_ref[...], piece_out)), kept_ref, sent_ref)


def key_body(
    query0_ref, query1_ref, query2_ref, query3_ref, query4_ref,
    grad0_ref, grad1_ref, grad2_ref, grad3_ref, grad4_ref,
    keys_ref, values_ref, projected_ref, gate_query_ref, w_in_ref, inputs_ref, out_grad_ref, slot_ref, user_ref,
    value_key_ref, outgoing_ref,
):
    rows, width = inputs_ref.shape
    score_scale = 1.0 / math.sqrt(DH)
    query_refs = (query0_ref, query1_ref, query2_ref, query3_ref, query4_ref)
    grad_refs = (grad0_ref, grad1_ref, grad2_ref, grad3_ref, grad4_ref)
    user_row = user_ref[...]
    query_user = jnp.concatenate(
        [as_column(ref[rows : rows + 1, :rows].astype(f32)) for ref in query_refs], axis=0
    )
    total = query_user.shape[0]
    allowed = (query_user == user_row) & (iota((total, rows), 1) <= iota((total, rows), 0))
    weight = allowed.astype(f32)
    allowed = jnp.concatenate([weight, weight], axis=0) > 0.0
    key_parts = []
    value_parts = []
    for pair in range(H // 2):
        columns = slice(2 * DH * pair, 2 * DH * (pair + 1))
        queries = both_heads(jnp.concatenate([ref[:rows, columns] for ref in query_refs], axis=0))
        grads = both_heads(jnp.concatenate([ref[:, columns] for ref in grad_refs], axis=0))
        scores = dot_nt(queries, keys_ref[:, columns]) * score_scale
        sig = sigmoid(scores)
        raw = scores * sig
        weights = jnp.where(allowed, raw, 0.0).astype(bf16)
        prob_grad = dot_nt(grads, values_ref[:, columns])
        score_grad = jnp.where(allowed, prob_grad * (sig + raw * (1.0 - sig)), 0.0).astype(bf16)
        key_parts.append(dot_tn(score_grad, queries) * score_scale)
        value_parts.append(dot_tn(weights, grads))
    key_grad = jnp.concatenate(key_parts, axis=1)
    value_grad = jnp.concatenate(value_parts, axis=1)
    value_part = (value_grad * silu_slope(projected_ref[:, width : 2 * width])).astype(bf16)
    key_part = (key_grad * silu_slope(projected_ref[:, 3 * width :])).astype(bf16)
    value_key_ref[:, :width] = value_part
    value_key_ref[:, width:] = key_part
    joined = jnp.concatenate(
        [gate_query_ref[:, :width], value_part, gate_query_ref[:, width:], key_part], axis=1
    )
    normed_grad = dot_nt(joined, w_in_ref[...])
    input_hat, input_inv = layer_norm(inputs_ref[...].astype(f32))
    inputs_grad = (
        out_grad_ref[...].astype(f32) + norm_backward(input_hat, input_inv, normed_grad)
    ).astype(bf16)
    places = slot_matrix(slot_ref[...], outgoing_ref.shape[0])
    outgoing_ref[...] = dot_tn(places, inputs_grad).astype(bf16)


def late_weights_body(piece_in, core_ref, packed_ref, value_key_ref, kept_ref, sent_ref):
    rows = value_key_ref.shape[0]
    width = value_key_ref.shape[1] // 2
    core = core_ref[0]
    normed = packed_ref[:rows, :]
    for section in range(2):
        part = value_key_ref[:, section * width : (section + 1) * width]
        split_by_core(core, section, dot_tn(normed, order_by_x(part, piece_in)), kept_ref, sent_ref)


def table_body(core_ref, asked_ref, arrived_ref, kept_ref, sent_ref):
    slots = asked_ref.shape[1]
    table_dev = kept_ref.shape[2]
    hits = hot(iota((table_dev, slots), 0) == asked_ref[...])
    sums = dot(hits, arrived_ref[...]).T
    rows = kept_ref.shape[1]
    even = core_ref[0] == 0
    for chip in range(kept_ref.shape[0]):
        first = sums[2 * chip * rows : (2 * chip + 1) * rows]
        second = sums[(2 * chip + 1) * rows : (2 * chip + 2) * rows]
        kept_ref[chip] = jnp.where(even, first, second).astype(bf16)
        sent_ref[chip] = jnp.where(even, second, first).astype(bf16)


def pair_sum(kept, sent):
    devices = lax.axis_size("ctx")
    got = lax.ppermute(sent, "ctx", [(i, i ^ 1) for i in range(devices)])
    return (kept.astype(f32) + got.astype(f32)).astype(bf16)


def chips_along_y():
    devices = lax.axis_size("ctx")
    return [list(range(first, devices, 2)) for first in range(2)]


def spread(block, axis, groups):
    return lax.all_to_all(
        block, axis, split_axis=0, concat_axis=0, tiled=True, axis_index_groups=groups
    )


def total_of(blocks):
    return jnp.sum(blocks.astype(f32), axis=0)


def sum_along_x(block):
    count = lax.axis_size("dp")
    me = lax.axis_index("dp") % X_CHIPS
    own = lax.dynamic_index_in_dim(block, me, 0, keepdims=False).astype(f32)
    for step in range(1, X_CHIPS):
        route = [(i, i - i % X_CHIPS + (i + step) % X_CHIPS) for i in range(count)]
        piece = lax.dynamic_index_in_dim(block, (me + step) % X_CHIPS, 0, keepdims=False)
        own = own + lax.ppermute(piece, "dp", route).astype(f32)
    return own.astype(bf16)


def reduce_weights(early, late, owners):
    xs = [list(range(first, first + X_CHIPS)) for first in range(0, owners, X_CHIPS)]
    zs = [list(range(first, owners, X_CHIPS)) for first in range(X_CHIPS)]
    z_chips = owners // X_CHIPS
    early_x = total_of(spread(early, "dp", xs)).astype(bf16)
    late_x = sum_along_x(late)
    both = jnp.concatenate([early_x, late_x], axis=2)
    along_y = total_of(spread(both, "ctx", chips_along_y())).astype(bf16)
    rows = along_y.shape[0]
    gate, query, out, value, key = jnp.split(along_y, 5, axis=1)
    wide = jnp.concatenate([gate, value, query, key], axis=1).reshape(rows, z_chips, -1)
    thin = out.reshape(rows, z_chips, -1)
    send = jnp.concatenate([wide, thin], axis=2).transpose(1, 0, 2)
    summed = total_of(spread(send, "dp", zs))
    return (summed[:, : wide.shape[2]], summed[:, wide.shape[2] :])


def local(item_ids, segments, touched_rows, w_in, w_out, out_grad):
    rows_dev = segments.shape[1]
    model_width = w_in.shape[0]
    table_dev = touched_rows.shape[0]
    owners = lax.axis_size("dp")
    capacity = max(rows_dev // 4, 6 * rows_dev // owners + 2)
    slots = owners * capacity
    core = (lax.axis_index("ctx") % 2).astype(jnp.int32).reshape(1)
    piece_in = w_in.shape[1] // owners
    piece_out = model_width // owners
    block = (rows_dev, model_width)
    packed_block = (rows_dev + USER_ROWS, model_width)
    reach_block = ((REACH + 1) * rows_dev, model_width)
    chips = lax.axis_size("ctx") // 2
    weight_rows = model_width // (2 * chips)

    user = (segments + 1).astype(f32)
    grad_rows = out_grad[0]
    requests, slot = call(
        lambda *refs: route_body(table_dev, *refs),
        [((owners, capacity), jnp.int32), ((2 * rows_dev, 1), jnp.int32)],
        item_ids.reshape(2 * rows_dev, 1),
    )
    asked = lax.all_to_all(requests, "dp", split_axis=0, concat_axis=0, tiled=True).reshape(1, slots)
    (found,) = call(gather_body, [((slots, model_width), bf16)], asked, touched_rows)
    fetched = lax.all_to_all(
        found.reshape(owners, capacity, model_width), "dp", split_axis=0, concat_axis=0, tiled=True
    ).reshape(slots, model_width)
    inputs, packed = call(
        embed_body, [(block, bf16), (packed_block, bf16)], slot, fetched, user
    )
    halos = [passed_along(packed, "ctx", offset) for offset in range(REACH, 0, -1)]
    projected, gates, values, queries, keys, mixed_grad = call(
        project_body,
        [
            ((rows_dev, 4 * model_width), f32), (block, bf16), (block, bf16),
            (packed_block, bf16), (block, bf16), (block, f32),
        ],
        packed, w_in, w_out, grad_rows, user,
        flops=400_000_000, moved=6_000_000,
    )
    later_queries = [passed_along(queries, "ctx", -offset) for offset in range(1, REACH + 1)]
    layer_out, mixed, gate_grad, att_grad, all_keys, all_values, key_user = call(
        forward_body,
        [
            (block, bf16), (block, bf16), (block, f32), (block, bf16),
            (reach_block, bf16), (reach_block, bf16), ((1, (REACH + 1) * rows_dev), f32),
        ],
        *halos, values, keys, queries, gates, inputs, mixed_grad, w_in, w_out, user,
        flops=1_000_000_000, moved=8_000_000,
    )
    later_grads = [passed_along(att_grad, "ctx", -offset) for offset in range(1, REACH + 1)]
    early_block = (X_CHIPS, chips, weight_rows, 3 * model_width // X_CHIPS)
    gate_query, early_kept, early_sent = call(
        lambda *refs: query_body(piece_in, piece_out, *refs),
        [((rows_dev, 2 * model_width), bf16), (early_block, bf16), (early_block, bf16)],
        core, queries, all_keys, all_values, att_grad, gate_grad, projected, user, key_user,
        packed, mixed, grad_rows,
        flops=1_000_000_000, moved=8_000_000,
    )
    early = pair_sum(early_kept, early_sent)
    value_key, outgoing = call(
        key_body,
        [((rows_dev, 2 * model_width), bf16), ((slots, model_width), bf16)],
        queries, *later_queries, att_grad, *later_grads, keys, values, projected, gate_query,
        w_in, inputs, grad_rows, slot, user,
        flops=1_000_000_000, moved=8_000_000,
    )
    arrived = lax.all_to_all(
        outgoing.reshape(owners, capacity, model_width), "dp", split_axis=0, concat_axis=0, tiled=True
    ).reshape(slots, model_width)
    late_block = (X_CHIPS, chips, weight_rows, 2 * model_width // X_CHIPS)
    late_kept, late_sent = call(
        lambda *refs: late_weights_body(piece_in, *refs),
        [(late_block, bf16), (late_block, bf16)],
        core, packed, value_key,
        flops=400_000_000, moved=3_000_000,
    )
    late = pair_sum(late_kept, late_sent)
    w_in_grad, w_out_grad = reduce_weights(early, late, owners)
    table_block = (chips, model_width // (2 * chips), table_dev)
    table_kept, table_sent = call(
        table_body, [(table_block, bf16), (table_block, bf16)], core, asked, arrived
    )
    table_sum = pair_sum(table_kept, table_sent)
    table_grad = total_of(spread(table_sum, "ctx", chips_along_y())).T
    return (layer_out[None], table_grad, w_in_grad, w_out_grad)


def solution(mesh):
    return jax.shard_map(
        local,
        mesh=mesh,
        in_specs=(
            P(None, "dp", "ctx"),
            P("dp", "ctx"),
            P("dp", None),
            P(),
            P(),
            P("dp", "ctx", None),
        ),
        out_specs=(P("dp", "ctx", None), P("dp", "ctx"), P("ctx", "dp"), P("ctx", "dp")),
        check_vma=False,
    )
```

```python
import math

import jax
import jax.numpy as jnp
from jax import lax
from jax.experimental import pallas as pl
from jax.experimental.pallas import tpu as pltpu
from jax.sharding import PartitionSpec as P

H = 8
DH = 64
X_CHIPS = 4
REACH = 4
USER_ROWS = 16

epsilon = 1e-05
f32 = jnp.float32
bf16 = jnp.bfloat16


def passed_along(block, axis, distance):
    devices = range(lax.axis_size(axis))
    route = [(i - distance, i) for i in devices if i - distance in devices]
    return lax.ppermute(block, axis, route)


def layer_norm(values):
    centered = values - jnp.mean(values, axis=-1, keepdims=True)
    inverse = lax.rsqrt(jnp.mean(centered * centered, axis=-1, keepdims=True) + epsilon)
    return (centered * inverse, inverse)


def norm_backward(normed, inverse, upstream):
    first_mean = jnp.mean(upstream, axis=-1, keepdims=True)
    second_mean = jnp.mean(upstream * normed, axis=-1, keepdims=True)
    return inverse * (upstream - first_mean - normed * second_mean)


def sigmoid(values):
    return 0.5 * jnp.tanh(0.5 * values) + 0.5


def silu_slope(values):
    sig = sigmoid(values)
    return sig * (1.0 + values * (1.0 - sig))


def iota(shape, dim):
    return lax.broadcasted_iota(jnp.int32, shape, dim)


def dot(left, right):
    return jnp.dot(left, right, preferred_element_type=f32)


def dot_nt(left, right):
    return lax.dot_general(left, right, (((1,), (1,)), ((), ())), preferred_element_type=f32)


def dot_tn(left, right):
    return lax.dot_general(left, right, (((0,), (0,)), ((), ())), preferred_element_type=f32)


def hot(condition):
    return condition.astype(f32).astype(bf16)


def as_column(row):
    length = row.shape[1]
    eye = iota((length, length), 0) == iota((length, length), 1)
    return jnp.sum(jnp.where(eye, jnp.broadcast_to(row, (length, length)), 0.0), axis=1, keepdims=True)


def both_heads(pair):
    low = iota(pair.shape, 1) < DH
    zero = jnp.zeros_like(pair)
    return jnp.concatenate([jnp.where(low, pair, zero), jnp.where(low, zero, pair)], axis=0)


def one_pair(stacked):
    rows = stacked.shape[0] // 2
    low = iota((rows, stacked.shape[1]), 1) < DH
    return jnp.where(low, stacked[:rows], stacked[rows:])


def call(body, outs, *operands, flops=0, moved=0):
    return pl.pallas_call(
        body,
        out_shape=[jax.ShapeDtypeStruct(shape, kind) for shape, kind in outs],
        compiler_params=pltpu.CompilerParams(vmem_limit_bytes=16 * 1024 * 1024),
        cost_estimate=pl.CostEstimate(flops=flops, bytes_accessed=moved, transcendentals=0),
    )(*operands)


def route_body(table_dev, ids_ref, request_ref, slot_ref):
    owners, capacity = request_ref.shape
    ids = jnp.concatenate([as_column(ids_ref[h : h + 1, :].astype(f32)) for h in range(2)], axis=0)
    ids = ids.astype(jnp.int32)
    count = ids.shape[0]
    shift = table_dev.bit_length() - 1
    owner = jnp.right_shift(ids, shift)
    row = jnp.bitwise_and(ids, table_dev - 1)
    member_f = (owner == iota((count, owners), 1)).astype(f32)
    member = member_f.astype(bf16)
    earlier = hot(iota((count, count), 0) > iota((count, count), 1))
    rank = jnp.sum(dot(earlier, member) * member_f, axis=1, keepdims=True).astype(jnp.int32)
    rank_hot = hot(rank == iota((count, capacity), 1))
    high = (member_f * jnp.right_shift(row, 4).astype(f32)).astype(bf16)
    low = (member_f * jnp.bitwise_and(row, 15).astype(f32)).astype(bf16)
    found = 16.0 * dot_tn(high, rank_hot) + dot_tn(low, rank_hot) + dot_tn(member, rank_hot)
    request_ref[...] = found.astype(jnp.int32) - 1
    slot_ref[...] = owner * capacity + rank


def gather_body(asked_ref, table_ref, found_ref, asked_row_ref):
    asked_rows = asked_ref[...]
    asked_row = jnp.concatenate(
        [asked_rows[g : g + 1, :] for g in range(asked_rows.shape[0])], axis=1
    )
    asked_row_ref[...] = asked_row
    slots = asked_row.shape[1]
    hits = hot(iota((table_ref.shape[0], slots), 0) == asked_row)
    found_ref[...] = dot_tn(hits, table_ref[...]).astype(bf16)


def slot_matrix(slot, slots):
    events = slot.shape[0] // 2
    places = iota((events, slots), 1)
    return hot((slot[:events] == places) | (slot[events:] == places))


def embed_body(slot_ref, fetched_ref, user_ref, inputs_ref, packed_ref):
    rows = inputs_ref.shape[0]
    places = slot_matrix(slot_ref[...], fetched_ref.shape[0])
    inputs = dot(places, fetched_ref[...]).astype(bf16)
    inputs_ref[...] = inputs
    packed_ref[:rows, :] = layer_norm(inputs.astype(f32))[0].astype(bf16)
    packed_ref[rows:, :] = user_rows(user_ref[...], packed_ref.shape[1])


def user_rows(user, width):
    wide = jnp.concatenate([user, jnp.zeros((1, width - user.shape[1]), f32)], axis=1)
    return jnp.broadcast_to(wide, (USER_ROWS, width)).astype(bf16)


def project_body(
    packed_ref, w_in_ref, w_out_ref, grad_ref, user_ref,
    projected_ref, gates_ref, values_ref, queries_ref, keys_ref, mixed_grad_ref,
):
    rows = grad_ref.shape[0]
    width = grad_ref.shape[1]
    normed = packed_ref[:rows, :]
    for part, out_ref in enumerate((gates_ref, values_ref, queries_ref, keys_ref)):
        columns = slice(part * width, (part + 1) * width)
        projected = dot(normed, w_in_ref[:, columns])
        projected_ref[:, columns] = projected
        out_ref[:rows, :] = (projected * sigmoid(projected)).astype(bf16)
    queries_ref[rows:, :] = user_rows(user_ref[...], width)
    mixed_grad_ref[...] = dot_nt(grad_ref[...], w_out_ref[...])


def window_mask(user_row, key_user_row, margin):
    rows = user_row.shape[1]
    columns = key_user_row.shape[1]
    user_column = as_column(user_row)
    allowed = (user_column == key_user_row) & (
        iota((rows, columns), 1) <= iota((rows, columns), 0) + margin
    )
    weight = allowed.astype(f32)
    return jnp.concatenate([weight, weight], axis=0) > 0.0


def forward_body(
    halo4_ref, halo3_ref, halo2_ref, halo1_ref, values_ref, keys_ref, queries_ref, gates_ref,
    inputs_ref, mixed_grad_ref, w_in_ref, w_out_ref, user_ref,
    out_ref, mixed_ref, gate_grad_ref, att_grad_ref, all_keys_ref, all_values_ref, key_user_ref,
):
    rows, width = inputs_ref.shape
    score_scale = 1.0 / math.sqrt(DH)
    halos = (halo4_ref, halo3_ref, halo2_ref, halo1_ref)
    far = jnp.concatenate([halo[:rows, :] for halo in halos], axis=0)
    margin = far.shape[0]
    for part, own_ref, all_ref in ((1, values_ref, all_values_ref), (3, keys_ref, all_keys_ref)):
        projected = dot(far, w_in_ref[:, part * width : (part + 1) * width])
        all_ref[:margin, :] = (projected * sigmoid(projected)).astype(bf16)
        all_ref[margin:, :] = own_ref[...]
    user_row = user_ref[...]
    key_user = jnp.concatenate(
        [halo[rows : rows + 1, :rows].astype(f32) for halo in halos] + [user_row], axis=1
    )
    key_user_ref[...] = key_user
    allowed = window_mask(user_row, key_user, margin)
    parts = []
    for pair in range(H // 2):
        columns = slice(2 * DH * pair, 2 * DH * (pair + 1))
        scores = dot_nt(both_heads(queries_ref[:rows, columns]), all_keys_ref[:, columns]) * score_scale
        weights = jnp.where(allowed, scores * sigmoid(scores), 0.0).astype(bf16)
        parts.append(one_pair(dot(weights, all_values_ref[:, columns])))
    att_hat, att_inv = layer_norm(jnp.concatenate(parts, axis=1))
    gates = gates_ref[...].astype(f32)
    mixed = (att_hat * gates).astype(bf16)
    mixed_ref[...] = mixed
    out_ref[...] = (inputs_ref[...].astype(f32) + dot(mixed, w_out_ref[...])).astype(bf16)
    mixed_grad = mixed_grad_ref[...]
    gate_grad_ref[...] = mixed_grad * att_hat
    att_grad_ref[...] = norm_backward(att_hat, att_inv, mixed_grad * gates).astype(bf16)


def halving_place(chip, chips):
    place = 0
    while chips > 1:
        place = 2 * place + chip % 2
        chip //= 2
        chips //= 2
    return place


def split_by_core(core, section, terms, kept_ref, sent_ref):
    devices = 2 * kept_ref.shape[1]
    rows = terms.shape[0] // devices
    lanes = terms.shape[1] // X_CHIPS
    even = core == 0
    for x in range(X_CHIPS):
        for chip in range(devices // 2):
            first = terms[2 * chip * rows : (2 * chip + 1) * rows, x * lanes : (x + 1) * lanes]
            second = terms[(2 * chip + 1) * rows : (2 * chip + 2) * rows, x * lanes : (x + 1) * lanes]
            place = (x, halving_place(chip, devices // 2), slice(None), slice(section * lanes, (section + 1) * lanes))
            kept_ref[place] = jnp.where(even, first, second).astype(bf16)
            sent_ref[place] = jnp.where(even, second, first).astype(bf16)


def order_by_x(block, piece):
    width = block.shape[1]
    old = iota((width, width), 0)
    new = iota((width, width), 1)
    per_x = width // X_CHIPS
    inner = jnp.bitwise_and(old, piece - 1)
    owner = jnp.right_shift(old, piece.bit_length() - 1)
    x = jnp.bitwise_and(owner, X_CHIPS - 1)
    z = jnp.right_shift(owner, X_CHIPS.bit_length() - 1)
    return dot(block, hot(new == x * per_x + z * piece + inner)).astype(bf16)


def query_body(
    queries_ref, all_keys_ref, all_values_ref, att_grad_ref, gate_grad_ref,
    projected_ref, user_ref, key_user_ref, gate_query_ref,
):
    rows, width = gate_grad_ref.shape
    score_scale = 1.0 / math.sqrt(DH)
    margin = all_keys_ref.shape[0] - rows
    allowed = window_mask(user_ref[...], key_user_ref[...], margin)
    parts = []
    for pair in range(H // 2):
        columns = slice(2 * DH * pair, 2 * DH * (pair + 1))
        keys = all_keys_ref[:, columns]
        scores = dot_nt(both_heads(queries_ref[:rows, columns]), keys) * score_scale
        prob_grad = dot_nt(both_heads(att_grad_ref[:, columns]), all_values_ref[:, columns])
        score_grad = jnp.where(allowed, prob_grad * silu_slope(scores), 0.0).astype(bf16)
        parts.append(one_pair(dot(score_grad, keys)) * score_scale)
    query_grad = jnp.concatenate(parts, axis=1)
    gate_part = gate_grad_ref[...] * silu_slope(projected_ref[:, :width])
    query_part = query_grad * silu_slope(projected_ref[:, 2 * width : 3 * width])
    gate_query_ref[:, :width] = gate_part.astype(bf16)
    gate_query_ref[:, width:] = query_part.astype(bf16)


def key_body(
    query0_ref, query1_ref, query2_ref, query3_ref, query4_ref,
    grad0_ref, grad1_ref, grad2_ref, grad3_ref, grad4_ref,
    keys_ref, values_ref, projected_ref, gate_query_ref, w_in_ref, inputs_ref, out_grad_ref, slot_ref, user_ref,
    value_key_ref, outgoing_ref,
):
    rows, width = inputs_ref.shape
    score_scale = 1.0 / math.sqrt(DH)
    query_refs = (query0_ref, query1_ref, query2_ref, query3_ref, query4_ref)
    grad_refs = (grad0_ref, grad1_ref, grad2_ref, grad3_ref, grad4_ref)
    user_row = user_ref[...]
    query_user = jnp.concatenate(
        [as_column(ref[rows : rows + 1, :rows].astype(f32)) for ref in query_refs], axis=0
    )
    total = query_user.shape[0]
    allowed = (query_user == user_row) & (iota((total, rows), 1) <= iota((total, rows), 0))
    weight = allowed.astype(f32)
    allowed = jnp.concatenate([weight, weight], axis=0) > 0.0
    key_parts = []
    value_parts = []
    for pair in range(H // 2):
        columns = slice(2 * DH * pair, 2 * DH * (pair + 1))
        queries = both_heads(jnp.concatenate([ref[:rows, columns] for ref in query_refs], axis=0))
        grads = both_heads(jnp.concatenate([ref[:, columns] for ref in grad_refs], axis=0))
        scores = dot_nt(queries, keys_ref[:, columns]) * score_scale
        sig = sigmoid(scores)
        raw = scores * sig
        weights = jnp.where(allowed, raw, 0.0).astype(bf16)
        prob_grad = dot_nt(grads, values_ref[:, columns])
        score_grad = jnp.where(allowed, prob_grad * (sig + raw * (1.0 - sig)), 0.0).astype(bf16)
        key_parts.append(dot_tn(score_grad, queries) * score_scale)
        value_parts.append(dot_tn(weights, grads))
    key_grad = jnp.concatenate(key_parts, axis=1)
    value_grad = jnp.concatenate(value_parts, axis=1)
    value_part = (value_grad * silu_slope(projected_ref[:, width : 2 * width])).astype(bf16)
    key_part = (key_grad * silu_slope(projected_ref[:, 3 * width :])).astype(bf16)
    value_key_ref[:, :width] = value_part
    value_key_ref[:, width:] = key_part
    joined = jnp.concatenate(
        [gate_query_ref[:, :width], value_part, gate_query_ref[:, width:], key_part], axis=1
    )
    normed_grad = dot_nt(joined, w_in_ref[...])
    input_hat, input_inv = layer_norm(inputs_ref[...].astype(f32))
    inputs_grad = (
        out_grad_ref[...].astype(f32) + norm_backward(input_hat, input_inv, normed_grad)
    ).astype(bf16)
    places = slot_matrix(slot_ref[...], outgoing_ref.shape[0])
    outgoing_ref[...] = dot_tn(places, inputs_grad).astype(bf16)


def weights_body(
    piece_in, piece_out, core_ref, packed_ref, gate_query_ref, value_key_ref, mixed_ref, grad_ref,
    kept_ref, sent_ref,
):
    rows, width = grad_ref.shape
    core = core_ref[0]
    normed = packed_ref[:rows, :]
    parts = (
        gate_query_ref[:, :width], value_key_ref[:, :width],
        gate_query_ref[:, width:], value_key_ref[:, width:],
    )
    for section, part in enumerate(parts):
        split_by_core(core, section, dot_tn(normed, order_by_x(part, piece_in)), kept_ref, sent_ref)
    last = dot_tn(mixed_ref[...], order_by_x(grad_ref[...], piece_out))
    split_by_core(core, len(parts), last, kept_ref, sent_ref)


def table_body(core_ref, asked_ref, arrived_ref, kept_ref, sent_ref):
    slots = asked_ref.shape[1]
    table_dev = kept_ref.shape[2]
    hits = hot(iota((table_dev, slots), 0) == asked_ref[...])
    sums = dot(hits, arrived_ref[...]).T
    rows = kept_ref.shape[1]
    even = core_ref[0] == 0
    for chip in range(kept_ref.shape[0]):
        first = sums[2 * chip * rows : (2 * chip + 1) * rows]
        second = sums[(2 * chip + 1) * rows : (2 * chip + 2) * rows]
        kept_ref[chip] = jnp.where(even, first, second).astype(bf16)
        sent_ref[chip] = jnp.where(even, second, first).astype(bf16)


def pair_sum(kept, sent):
    devices = lax.axis_size("ctx")
    got = lax.ppermute(sent, "ctx", [(i, i ^ 1) for i in range(devices)])
    return (kept.astype(f32) + got.astype(f32)).astype(bf16)


def chips_along_y():
    devices = lax.axis_size("ctx")
    return [list(range(first, devices, 2)) for first in range(2)]


def spread(block, axis, groups):
    return lax.all_to_all(
        block, axis, split_axis=0, concat_axis=0, tiled=True, axis_index_groups=groups
    )


def total_of(blocks):
    return jnp.sum(blocks.astype(f32), axis=0)


def sum_along_x(block):
    count = lax.axis_size("dp")
    me = lax.axis_index("dp") % X_CHIPS
    own = lax.dynamic_index_in_dim(block, me, 0, keepdims=False).astype(f32)
    for step in range(1, X_CHIPS):
        route = [(i, i - i % X_CHIPS + (i + step) % X_CHIPS) for i in range(count)]
        piece = lax.dynamic_index_in_dim(block, (me + step) % X_CHIPS, 0, keepdims=False)
        own = own + lax.ppermute(piece, "dp", route).astype(f32)
    return own.astype(bf16)


def sum_along_y(block):
    count = lax.axis_size("ctx")
    me = lax.axis_index("ctx")
    distance = 2
    while block.shape[0] > 1:
        half = block.shape[0] // 2
        bit = (me // distance) % 2
        sent = lax.dynamic_slice_in_dim(block, (1 - bit) * half, half, 0)
        kept = lax.dynamic_slice_in_dim(block, bit * half, half, 0)
        got = lax.ppermute(sent, "ctx", [(i, i ^ distance) for i in range(count)])
        block = (kept.astype(f32) + got.astype(f32)).astype(bf16)
        distance *= 2
    return block[0]


def weights_to_z(along_y, owners):
    rows = along_y.shape[0]
    z_chips = owners // X_CHIPS
    wide_width = along_y.shape[1] * 4 // 5
    wide = along_y[:, :wide_width].reshape(rows, z_chips, -1)
    thin = along_y[:, wide_width:].reshape(rows, z_chips, -1)
    return jnp.concatenate([wide, thin], axis=2).transpose(1, 0, 2), wide.shape[2]


def sum_along_z(send, owners):
    zs = [list(range(first, owners, X_CHIPS)) for first in range(X_CHIPS)]
    return total_of(spread(send, "dp", zs))


def local(item_ids, segments, touched_rows, w_in, w_out, out_grad):
    rows_dev = segments.shape[1]
    model_width = w_in.shape[0]
    table_dev = touched_rows.shape[0]
    owners = lax.axis_size("dp")
    capacity = max(rows_dev // 4, 6 * rows_dev // owners + 2)
    slots = owners * capacity
    core = (lax.axis_index("ctx") % 2).astype(jnp.int32).reshape(1)
    piece_in = w_in.shape[1] // owners
    piece_out = model_width // owners
    block = (rows_dev, model_width)
    packed_block = (rows_dev + USER_ROWS, model_width)
    reach_block = ((REACH + 1) * rows_dev, model_width)
    chips = lax.axis_size("ctx") // 2
    weight_rows = model_width // (2 * chips)

    user = (segments + 1).astype(f32)
    grad_rows = out_grad[0]
    requests, slot = call(
        lambda *refs: route_body(table_dev, *refs),
        [((owners, capacity), jnp.int32), ((2 * rows_dev, 1), jnp.int32)],
        item_ids.reshape(2, rows_dev),
    )
    asked = lax.all_to_all(requests, "dp", split_axis=0, concat_axis=0, tiled=True)
    found, asked_row = call(
        gather_body, [((slots, model_width), bf16), ((1, slots), jnp.int32)], asked, touched_rows
    )
    fetched = lax.all_to_all(
        found.reshape(owners, capacity, model_width), "dp", split_axis=0, concat_axis=0, tiled=True
    ).reshape(slots, model_width)
    inputs, packed = call(
        embed_body, [(block, bf16), (packed_block, bf16)], slot, fetched, user
    )
    halos = [passed_along(packed, "ctx", offset) for offset in range(REACH, 0, -1)]
    projected, gates, values, queries, keys, mixed_grad = call(
        project_body,
        [
            ((rows_dev, 4 * model_width), f32), (block, bf16), (block, bf16),
            (packed_block, bf16), (block, bf16), (block, f32),
        ],
        packed, w_in, w_out, grad_rows, user,
        flops=1_500_000_000, moved=6_000_000,
    )
    later_queries = [passed_along(queries, "ctx", -offset) for offset in range(1, REACH + 1)]
    halos, later_queries = lax.optimization_barrier((halos, later_queries))
    layer_out, mixed, gate_grad, att_grad, all_keys, all_values, key_user = call(
        forward_body,
        [
            (block, bf16), (block, bf16), (block, f32), (block, bf16),
            (reach_block, bf16), (reach_block, bf16), ((1, (REACH + 1) * rows_dev), f32),
        ],
        *halos, values, keys, queries, gates, inputs, mixed_grad, w_in, w_out, user,
        flops=4_000_000_000, moved=8_000_000,
    )
    later_grads = [passed_along(att_grad, "ctx", -offset) for offset in range(1, REACH + 1)]
    (gate_query,) = call(
        query_body, [((rows_dev, 2 * model_width), bf16)],
        queries, all_keys, all_values, att_grad, gate_grad, projected, user, key_user,
        flops=4_000_000_000, moved=8_000_000,
    )
    value_key, outgoing = call(
        key_body,
        [((rows_dev, 2 * model_width), bf16), ((slots, model_width), bf16)],
        queries, *later_queries, att_grad, *later_grads, keys, values, projected, gate_query,
        w_in, inputs, grad_rows, slot, user,
        flops=4_000_000_000, moved=8_000_000,
    )
    arrived = lax.all_to_all(
        outgoing.reshape(owners, capacity, model_width), "dp", split_axis=0, concat_axis=0, tiled=True
    ).reshape(slots, model_width)
    weight_block = (X_CHIPS, chips, weight_rows, 5 * model_width // X_CHIPS)
    weight_kept, weight_sent = call(
        lambda *refs: weights_body(piece_in, piece_out, *refs),
        [(weight_block, bf16), (weight_block, bf16)],
        core, packed, gate_query, value_key, mixed, grad_rows,
        flops=4_000_000_000, moved=6_000_000,
    )
    z_send, wide = weights_to_z(sum_along_y(sum_along_x(pair_sum(weight_kept, weight_sent))), owners)
    arrived, z_send = lax.optimization_barrier((arrived, z_send))
    table_block = (chips, model_width // (2 * chips), table_dev)
    table_kept, table_sent = call(
        table_body, [(table_block, bf16), (table_block, bf16)], core, asked_row, arrived
    )
    table_sum = pair_sum(table_kept, table_sent)
    table_grad = total_of(spread(table_sum, "ctx", chips_along_y())).T
    summed = sum_along_z(z_send, owners)
    return (layer_out[None], table_grad, summed[:, :wide], summed[:, wide:])


def solution(mesh):
    return jax.shard_map(
        local,
        mesh=mesh,
        in_specs=(
            P(None, "dp", "ctx"),
            P("dp", "ctx"),
            P("dp", None),
            P(),
            P(),
            P("dp", "ctx", None),
        ),
        out_specs=(P("dp", "ctx", None), P("dp", "ctx"), P("ctx", "dp"), P("ctx", "dp")),
        check_vma=False,
    )
```

```python
import math

import jax
import jax.numpy as jnp
from jax import lax
from jax.experimental import pallas as pl
from jax.experimental.pallas import tpu as pltpu
from jax.sharding import PartitionSpec as P

H = 8
DH = 64
X_CHIPS = 4
REACH = 4
USER_ROWS = 16

epsilon = 1e-05
f32 = jnp.float32
bf16 = jnp.bfloat16


def passed_along(block, axis, distance):
    devices = range(lax.axis_size(axis))
    route = [(i - distance, i) for i in devices if i - distance in devices]
    return lax.ppermute(block, axis, route)


def swapped(block, senders=(0, 1)):
    devices = range(lax.axis_size("ctx"))
    return lax.ppermute(block, "ctx", [(i, i ^ 1) for i in devices if i % 2 in senders])


def halo(block, direction, own):
    two = passed_along(block, "ctx", 2 * direction)
    four = passed_along(block, "ctx", 4 * direction)
    far_sender = 1 if direction > 0 else 0
    return (four, swapped(four, (far_sender,)), two, swapped(two), own)


def nearest_last(core, four, mate_four, two, mate_two, mate_own):
    even = core == 0
    return (
        four,
        jnp.where(even, mate_four, mate_two),
        two,
        jnp.where(even, mate_two, mate_own),
    )


def nearest_first(core, four, mate_four, two, mate_two, mate_own):
    even = core == 0
    return (
        jnp.where(even, mate_own, mate_two),
        two,
        jnp.where(even, mate_two, mate_four),
        four,
    )


def layer_norm(values):
    centered = values - jnp.mean(values, axis=-1, keepdims=True)
    inverse = lax.rsqrt(jnp.mean(centered * centered, axis=-1, keepdims=True) + epsilon)
    return (centered * inverse, inverse)


def norm_backward(normed, inverse, upstream):
    first_mean = jnp.mean(upstream, axis=-1, keepdims=True)
    second_mean = jnp.mean(upstream * normed, axis=-1, keepdims=True)
    return inverse * (upstream - first_mean - normed * second_mean)


def sigmoid(values):
    return 0.5 * jnp.tanh(0.5 * values) + 0.5


def silu_slope(values):
    sig = sigmoid(values)
    return sig * (1.0 + values * (1.0 - sig))


def iota(shape, dim):
    return lax.broadcasted_iota(jnp.int32, shape, dim)


def dot(left, right):
    return jnp.dot(left, right, preferred_element_type=f32)


def dot_nt(left, right):
    return lax.dot_general(left, right, (((1,), (1,)), ((), ())), preferred_element_type=f32)


def dot_tn(left, right):
    return lax.dot_general(left, right, (((0,), (0,)), ((), ())), preferred_element_type=f32)


def hot(condition):
    return condition.astype(f32).astype(bf16)


def as_column(row):
    length = row.shape[1]
    eye = iota((length, length), 0) == iota((length, length), 1)
    return jnp.sum(jnp.where(eye, jnp.broadcast_to(row, (length, length)), 0.0), axis=1, keepdims=True)


def both_heads(pair):
    low = iota(pair.shape, 1) < DH
    zero = jnp.zeros_like(pair)
    return jnp.concatenate([jnp.where(low, pair, zero), jnp.where(low, zero, pair)], axis=0)


def one_pair(stacked):
    rows = stacked.shape[0] // 2
    low = iota((rows, stacked.shape[1]), 1) < DH
    return jnp.where(low, stacked[:rows], stacked[rows:])


def call(body, outs, *operands, core=None, flops=0, moved=0):
    in_specs = [pl.BlockSpec(memory_space=pltpu.VMEM)] * len(operands)
    if core is not None:
        in_specs = [pl.BlockSpec(memory_space=pltpu.SMEM)] + in_specs
        operands = (core,) + operands
    return pl.pallas_call(
        body,
        out_shape=[jax.ShapeDtypeStruct(shape, kind) for shape, kind in outs],
        in_specs=in_specs,
        compiler_params=pltpu.CompilerParams(vmem_limit_bytes=16 * 1024 * 1024),
        cost_estimate=pl.CostEstimate(flops=flops, bytes_accessed=moved, transcendentals=0),
    )(*operands)


def route_body(table_dev, ids_ref, request_ref, slot_ref):
    owners, capacity = request_ref.shape
    ids = jnp.concatenate([as_column(ids_ref[h : h + 1, :].astype(f32)) for h in range(2)], axis=0)
    ids = ids.astype(jnp.int32)
    count = ids.shape[0]
    shift = table_dev.bit_length() - 1
    owner = jnp.right_shift(ids, shift)
    row = jnp.bitwise_and(ids, table_dev - 1)
    member_f = (owner == iota((count, owners), 1)).astype(f32)
    member = member_f.astype(bf16)
    earlier = hot(iota((count, count), 0) > iota((count, count), 1))
    rank = jnp.sum(dot(earlier, member) * member_f, axis=1, keepdims=True).astype(jnp.int32)
    rank_hot = hot(rank == iota((count, capacity), 1))
    high = (member_f * jnp.right_shift(row, 4).astype(f32)).astype(bf16)
    low = (member_f * jnp.bitwise_and(row, 15).astype(f32)).astype(bf16)
    found = 16.0 * dot_tn(high, rank_hot) + dot_tn(low, rank_hot) + dot_tn(member, rank_hot)
    request_ref[...] = found.astype(jnp.int32) - 1
    slot_ref[...] = owner * capacity + rank


def gather_body(asked_ref, table_ref, found_ref, asked_row_ref):
    asked_rows = asked_ref[...]
    asked_row = jnp.concatenate(
        [asked_rows[g : g + 1, :] for g in range(asked_rows.shape[0])], axis=1
    )
    asked_row_ref[...] = asked_row
    slots = asked_row.shape[1]
    hits = hot(iota((table_ref.shape[0], slots), 0) == asked_row)
    found_ref[...] = dot_tn(hits, table_ref[...]).astype(bf16)


def slot_matrix(slot, slots):
    events = slot.shape[0] // 2
    places = iota((events, slots), 1)
    return hot((slot[:events] == places) | (slot[events:] == places))


def embed_body(slot_ref, fetched_ref, user_ref, inputs_ref, packed_ref):
    rows = inputs_ref.shape[0]
    places = slot_matrix(slot_ref[...], fetched_ref.shape[0])
    inputs = dot(places, fetched_ref[...]).astype(bf16)
    inputs_ref[...] = inputs
    packed_ref[:rows, :] = layer_norm(inputs.astype(f32))[0].astype(bf16)
    packed_ref[rows:, :] = user_rows(user_ref[...], packed_ref.shape[1])


def user_rows(user, width):
    wide = jnp.concatenate([user, jnp.zeros((1, width - user.shape[1]), f32)], axis=1)
    return jnp.broadcast_to(wide, (USER_ROWS, width)).astype(bf16)


def project_body(
    packed_ref, w_in_ref, w_out_ref, grad_ref,
    projected_ref, gates_ref, values_ref, queries_ref, keys_ref, mixed_grad_ref,
):
    rows = grad_ref.shape[0]
    width = grad_ref.shape[1]
    normed = packed_ref[:rows, :]
    for part, out_ref in enumerate((gates_ref, values_ref, queries_ref, keys_ref)):
        columns = slice(part * width, (part + 1) * width)
        projected = dot(normed, w_in_ref[:, columns])
        projected_ref[:, columns] = projected
        out_ref[...] = (projected * sigmoid(projected)).astype(bf16)
    mixed_grad_ref[...] = dot_nt(grad_ref[...], w_out_ref[...])


def window_mask(user_row, key_user_row, margin):
    rows = user_row.shape[1]
    columns = key_user_row.shape[1]
    user_column = as_column(user_row)
    allowed = (user_column == key_user_row) & (
        iota((rows, columns), 1) <= iota((rows, columns), 0) + margin
    )
    weight = allowed.astype(f32)
    return jnp.concatenate([weight, weight], axis=0) > 0.0


def forward_body(
    core_ref, four_ref, mate_four_ref, two_ref, mate_two_ref, mate_own_ref, values_ref, keys_ref, queries_ref, gates_ref,
    inputs_ref, mixed_grad_ref, w_in_ref, w_out_ref, user_ref,
    out_ref, mixed_ref, gate_grad_ref, att_grad_ref, all_keys_ref, all_values_ref, key_user_ref,
):
    rows, width = inputs_ref.shape
    score_scale = 1.0 / math.sqrt(DH)
    halos = nearest_last(
        core_ref[0], four_ref[...], mate_four_ref[...], two_ref[...], mate_two_ref[...], mate_own_ref[...]
    )
    far = jnp.concatenate([block[:rows, :] for block in halos], axis=0)
    margin = far.shape[0]
    for part, own_ref, all_ref in ((1, values_ref, all_values_ref), (3, keys_ref, all_keys_ref)):
        projected = dot(far, w_in_ref[:, part * width : (part + 1) * width])
        all_ref[:margin, :] = (projected * sigmoid(projected)).astype(bf16)
        all_ref[margin:, :] = own_ref[...]
    user_row = user_ref[...]
    key_user = jnp.concatenate(
        [block[rows : rows + 1, :rows].astype(f32) for block in halos] + [user_row], axis=1
    )
    key_user_ref[...] = key_user
    allowed = window_mask(user_row, key_user, margin)
    parts = []
    for pair in range(H // 2):
        columns = slice(2 * DH * pair, 2 * DH * (pair + 1))
        scores = dot_nt(both_heads(queries_ref[:, columns]), all_keys_ref[:, columns]) * score_scale
        weights = jnp.where(allowed, scores * sigmoid(scores), 0.0).astype(bf16)
        parts.append(one_pair(dot(weights, all_values_ref[:, columns])))
    att_hat, att_inv = layer_norm(jnp.concatenate(parts, axis=1))
    gates = gates_ref[...].astype(f32)
    mixed = (att_hat * gates).astype(bf16)
    mixed_ref[...] = mixed
    out_ref[...] = (inputs_ref[...].astype(f32) + dot(mixed, w_out_ref[...])).astype(bf16)
    mixed_grad = mixed_grad_ref[...]
    gate_grad_ref[...] = mixed_grad * att_hat
    att_grad_ref[...] = norm_backward(att_hat, att_inv, mixed_grad * gates).astype(bf16)


def core_first(block, rows):
    width = block.shape[1]
    old = iota((width, width), 0)
    new = iota((width, width), 1)
    inner = jnp.bitwise_and(old, rows - 1)
    device = jnp.right_shift(old, rows.bit_length() - 1)
    place = jnp.bitwise_and(device, 1) * (width // 2) + jnp.right_shift(device, 1) * rows + inner
    return dot(block, hot(new == place)).astype(bf16)


def split_by_core(core, terms, first_owner, piece, first_row, stride, kept_ref, sent_ref):
    half = terms.shape[1] // 2
    even = core == 0
    for local_owner in range(terms.shape[0] // piece):
        owner = first_owner + local_owner
        rows = terms[local_owner * piece : (local_owner + 1) * piece]
        place = first_row + (local_owner // X_CHIPS) * stride
        kept_ref[owner % X_CHIPS, place : place + piece, :] = jnp.where(
            even, rows[:, :half], rows[:, half:]
        ).astype(bf16)
        sent_ref[owner % X_CHIPS, place : place + piece, :] = jnp.where(
            even, rows[:, half:], rows[:, :half]
        ).astype(bf16)


def query_body(
    core_ref, queries_ref, all_keys_ref, all_values_ref, att_grad_ref, gate_grad_ref,
    projected_ref, user_ref, key_user_ref,
    four_ref, mate_four_ref, two_ref, mate_two_ref, mate_own_ref, w_in_ref,
    gate_query_ref, all_queries_ref, query_user_ref,
):
    rows, width = gate_grad_ref.shape
    score_scale = 1.0 / math.sqrt(DH)
    margin = all_keys_ref.shape[0] - rows
    allowed = window_mask(user_ref[...], key_user_ref[...], margin)
    parts = []
    for pair in range(H // 2):
        columns = slice(2 * DH * pair, 2 * DH * (pair + 1))
        keys = all_keys_ref[:, columns]
        scores = dot_nt(both_heads(queries_ref[:, columns]), keys) * score_scale
        prob_grad = dot_nt(both_heads(att_grad_ref[:, columns]), all_values_ref[:, columns])
        score_grad = jnp.where(allowed, prob_grad * silu_slope(scores), 0.0).astype(bf16)
        parts.append(one_pair(dot(score_grad, keys)) * score_scale)
    query_grad = jnp.concatenate(parts, axis=1)
    gate_part = gate_grad_ref[...] * silu_slope(projected_ref[:, :width])
    query_part = query_grad * silu_slope(projected_ref[:, 2 * width : 3 * width])
    gate_query_ref[:, :width] = gate_part.astype(bf16)
    gate_query_ref[:, width:] = query_part.astype(bf16)
    halos = nearest_first(
        core_ref[0], four_ref[...], mate_four_ref[...], two_ref[...], mate_two_ref[...], mate_own_ref[...]
    )
    far = jnp.concatenate([block[:rows, :] for block in halos], axis=0)
    projected = dot(far, w_in_ref[:, 2 * width : 3 * width])
    all_queries_ref[:rows, :] = queries_ref[...]
    all_queries_ref[rows:, :] = (projected * sigmoid(projected)).astype(bf16)
    query_user_ref[...] = jnp.concatenate(
        [as_column(user_ref[...])]
        + [as_column(block[rows : rows + 1, :rows].astype(f32)) for block in halos],
        axis=0,
    )


def key_body(
    core_ref, all_queries_ref, query_user_ref, att_grad_ref,
    four_ref, mate_four_ref, two_ref, mate_two_ref, mate_own_ref,
    keys_ref, values_ref, projected_ref, gate_query_ref, w_in_ref, inputs_ref, out_grad_ref, slot_ref, user_ref,
    value_key_ref, outgoing_ref,
):
    rows, width = inputs_ref.shape
    score_scale = 1.0 / math.sqrt(DH)
    user_row = user_ref[...]
    query_user = query_user_ref[...]
    halos = nearest_first(
        core_ref[0], four_ref[...], mate_four_ref[...], two_ref[...], mate_two_ref[...], mate_own_ref[...]
    )
    all_grads = jnp.concatenate((att_grad_ref[...],) + halos, axis=0)
    total = query_user.shape[0]
    allowed = (query_user == user_row) & (iota((total, rows), 1) <= iota((total, rows), 0))
    weight = allowed.astype(f32)
    allowed = jnp.concatenate([weight, weight], axis=0) > 0.0
    key_parts = []
    value_parts = []
    for pair in range(H // 2):
        columns = slice(2 * DH * pair, 2 * DH * (pair + 1))
        queries = both_heads(all_queries_ref[:, columns])
        grads = both_heads(all_grads[:, columns])
        scores = dot_nt(queries, keys_ref[:, columns]) * score_scale
        sig = sigmoid(scores)
        raw = scores * sig
        weights = jnp.where(allowed, raw, 0.0).astype(bf16)
        prob_grad = dot_nt(grads, values_ref[:, columns])
        score_grad = jnp.where(allowed, prob_grad * (sig + raw * (1.0 - sig)), 0.0).astype(bf16)
        key_parts.append(dot_tn(score_grad, queries) * score_scale)
        value_parts.append(dot_tn(weights, grads))
    key_grad = jnp.concatenate(key_parts, axis=1)
    value_grad = jnp.concatenate(value_parts, axis=1)
    value_part = (value_grad * silu_slope(projected_ref[:, width : 2 * width])).astype(bf16)
    key_part = (key_grad * silu_slope(projected_ref[:, 3 * width :])).astype(bf16)
    value_key_ref[:, :width] = value_part
    value_key_ref[:, width:] = key_part
    joined = jnp.concatenate(
        [gate_query_ref[:, :width], value_part, gate_query_ref[:, width:], key_part], axis=1
    )
    normed_grad = dot_nt(joined, w_in_ref[...])
    input_hat, input_inv = layer_norm(inputs_ref[...].astype(f32))
    inputs_grad = (
        out_grad_ref[...].astype(f32) + norm_backward(input_hat, input_inv, normed_grad)
    ).astype(bf16)
    places = slot_matrix(slot_ref[...], outgoing_ref.shape[0])
    outgoing_ref[...] = dot_tn(places, inputs_grad).astype(bf16)


def early_body(
    piece_in, piece_out, weight_rows,
    core_ref, packed_ref, gate_query_ref, mixed_ref, grad_ref, kept_ref, sent_ref,
):
    rows, width = grad_ref.shape
    core = core_ref[0]
    per_part = width // piece_in
    in_rows = piece_in * per_part // X_CHIPS
    normed = core_first(packed_ref[:rows, :], weight_rows)
    for section, first_owner in ((0, 0), (1, 2 * per_part)):
        terms = dot_tn(gate_query_ref[:, section * width : (section + 1) * width], normed)
        split_by_core(
            core, terms, first_owner, piece_in, section * in_rows, piece_in, kept_ref, sent_ref
        )
    terms = dot_tn(grad_ref[...], core_first(mixed_ref[...], weight_rows))
    split_by_core(core, terms, 0, piece_out, 2 * in_rows, piece_out, kept_ref, sent_ref)


def late_body(piece_in, weight_rows, core_ref, packed_ref, value_key_ref, kept_ref, sent_ref):
    rows = value_key_ref.shape[0]
    width = value_key_ref.shape[1] // 2
    core = core_ref[0]
    per_part = width // piece_in
    in_rows = piece_in * per_part // X_CHIPS
    normed = core_first(packed_ref[:rows, :], weight_rows)
    for section in range(2):
        terms = dot_tn(value_key_ref[:, section * width : (section + 1) * width], normed)
        split_by_core(
            core, terms, (2 * section + 1) * per_part, piece_in, section * in_rows, piece_in,
            kept_ref, sent_ref,
        )


def table_body(core_ref, asked_ref, arrived_ref, kept_ref, sent_ref):
    slots = asked_ref.shape[1]
    table_dev = kept_ref.shape[2]
    hits = hot(iota((table_dev, slots), 0) == asked_ref[...])
    sums = dot(hits, arrived_ref[...]).T
    rows = kept_ref.shape[1]
    even = core_ref[0] == 0
    for chip in range(kept_ref.shape[0]):
        first = sums[2 * chip * rows : (2 * chip + 1) * rows]
        second = sums[(2 * chip + 1) * rows : (2 * chip + 2) * rows]
        kept_ref[chip] = jnp.where(even, first, second).astype(bf16)
        sent_ref[chip] = jnp.where(even, second, first).astype(bf16)


def pair_sum(kept, sent):
    devices = lax.axis_size("ctx")
    got = lax.ppermute(sent, "ctx", [(i, i ^ 1) for i in range(devices)])
    return (kept.astype(f32) + got.astype(f32)).astype(bf16)


def chips_along_y():
    devices = lax.axis_size("ctx")
    return [list(range(first, devices, 2)) for first in range(2)]


def spread(block, axis, groups):
    return lax.all_to_all(
        block, axis, split_axis=0, concat_axis=0, tiled=True, axis_index_groups=groups
    )


def total_of(blocks):
    return jnp.sum(blocks.astype(f32), axis=0)


def sum_along(block, axis_at, stride, count):
    devices = lax.axis_size("dp")
    me = axis_at % count
    own = lax.dynamic_index_in_dim(block, me, 0, keepdims=False).astype(f32)
    for step in range(1, count):
        route = []
        for i in range(devices):
            at = i // stride % count
            route.append((i, i + ((at + step) % count - at) * stride))
        piece = lax.dynamic_index_in_dim(block, (me + step) % count, 0, keepdims=False)
        own = own + lax.ppermute(piece, "dp", route).astype(f32)
    return own.astype(bf16)


def sum_along_x(block):
    return sum_along(block, lax.axis_index("dp"), 1, X_CHIPS)


def sum_along_z(early, late, piece_in, piece_out, owners):
    z_chips = owners // X_CHIPS
    width = early.shape[1]
    half = early.shape[0] - z_chips * piece_out
    first = early[:half].reshape(2, -1, piece_in, width)
    second = late.reshape(2, -1, piece_in, width)
    wide = jnp.concatenate([first, second], axis=1).reshape(z_chips, piece_in, width)
    thin = early[half:].reshape(z_chips, piece_out, width)
    both = jnp.concatenate([wide, thin], axis=1)
    return sum_along(both, lax.axis_index("dp") // X_CHIPS, X_CHIPS, z_chips)


def local(item_ids, segments, touched_rows, w_in, w_out, out_grad):
    rows_dev = segments.shape[1]
    model_width = w_in.shape[0]
    table_dev = touched_rows.shape[0]
    owners = lax.axis_size("dp")
    capacity = max(rows_dev // 4, 6 * rows_dev // owners + 2)
    slots = owners * capacity
    core = (lax.axis_index("ctx") % 2).astype(jnp.int32).reshape(1)
    piece_in = w_in.shape[1] // owners
    piece_out = model_width // owners
    block = (rows_dev, model_width)
    packed_block = (rows_dev + USER_ROWS, model_width)
    reach_block = ((REACH + 1) * rows_dev, model_width)
    chips = lax.axis_size("ctx") // 2
    weight_rows = model_width // (2 * chips)

    user = (segments + 1).astype(f32)
    grad_rows = out_grad[0]
    requests, slot = call(
        lambda *refs: route_body(table_dev, *refs),
        [((owners, capacity), jnp.int32), ((2 * rows_dev, 1), jnp.int32)],
        item_ids.reshape(2, rows_dev),
    )
    asked = lax.all_to_all(requests, "dp", split_axis=0, concat_axis=0, tiled=True)
    found, asked_row = call(
        gather_body, [((slots, model_width), bf16), ((1, slots), jnp.int32)], asked, touched_rows
    )
    fetched = lax.all_to_all(
        found.reshape(owners, capacity, model_width), "dp", split_axis=0, concat_axis=0, tiled=True
    ).reshape(slots, model_width)
    inputs, packed = call(
        embed_body, [(block, bf16), (packed_block, bf16)], slot, fetched, user
    )
    own = swapped(packed)
    earlier = halo(packed, 1, own)
    later = halo(packed, -1, own)
    projected, gates, values, queries, keys, mixed_grad = call(
        project_body,
        [
            ((rows_dev, 4 * model_width), f32), (block, bf16), (block, bf16),
            (block, bf16), (block, bf16), (block, f32),
        ],
        packed, w_in, w_out, grad_rows,
        flops=1_500_000_000, moved=6_000_000,
    )
    layer_out, mixed, gate_grad, att_grad, all_keys, all_values, key_user = call(
        forward_body,
        [
            (block, bf16), (block, bf16), (block, f32), (block, bf16),
            (reach_block, bf16), (reach_block, bf16), ((1, (REACH + 1) * rows_dev), f32),
        ],
        *earlier, values, keys, queries, gates, inputs, mixed_grad, w_in, w_out, user,
        core=core, flops=4_000_000_000, moved=8_000_000,
    )
    later_grads = halo(att_grad, -1, swapped(att_grad, (1,)))
    four, mate_four, two, mate_two, mate_own = later_grads
    gate_grad, mate_own = lax.optimization_barrier((gate_grad, mate_own))
    mixed, four, mate_two = lax.optimization_barrier((mixed, four, mate_two))
    later_grads = (four, mate_four, two, mate_two, mate_own)
    gate_query, all_queries, query_user = call(
        query_body,
        [
            ((rows_dev, 2 * model_width), bf16), (reach_block, bf16),
            (((REACH + 1) * rows_dev, 1), f32),
        ],
        queries, all_keys, all_values, att_grad, gate_grad, projected, user, key_user, *later, w_in,
        core=core, flops=4_000_000_000, moved=8_000_000,
    )
    half_width = model_width // 2
    early_block = (X_CHIPS, 3 * model_width // X_CHIPS, half_width)
    early_kept, early_sent = call(
        lambda *refs: early_body(piece_in, piece_out, weight_rows, *refs),
        [(early_block, bf16), (early_block, bf16)],
        packed, gate_query, mixed, grad_rows,
        core=core, flops=2_000_000_000, moved=4_000_000,
    )
    early_pair = pair_sum(early_kept, early_sent)
    gate_query, early_pair = lax.optimization_barrier((gate_query, early_pair))
    early = sum_along_x(early_pair)
    value_key, outgoing = call(
        key_body,
        [((rows_dev, 2 * model_width), bf16), ((slots, model_width), bf16)],
        all_queries, query_user, att_grad, *later_grads, keys, values, projected, gate_query,
        w_in, inputs, grad_rows, slot, user,
        core=core, flops=4_000_000_000, moved=8_000_000,
    )
    arrived = lax.all_to_all(
        outgoing.reshape(owners, capacity, model_width), "dp", split_axis=0, concat_axis=0, tiled=True
    ).reshape(slots, model_width)
    late_block = (X_CHIPS, 2 * model_width // X_CHIPS, half_width)
    late_kept, late_sent = call(
        lambda *refs: late_body(piece_in, weight_rows, *refs),
        [(late_block, bf16), (late_block, bf16)],
        packed, value_key,
        core=core, flops=1_500_000_000, moved=3_000_000,
    )
    late = sum_along_x(pair_sum(late_kept, late_sent))
    along_dp = sum_along_z(early, late, piece_in, piece_out, owners)
    weight_terms = along_dp.T.reshape(chips, weight_rows, piece_in + piece_out)
    table_block = (chips, model_width // (2 * chips), table_dev)
    table_kept, table_sent = call(
        table_body, [(table_block, bf16), (table_block, bf16)], asked_row, arrived, core=core
    )
    table_sum = pair_sum(table_kept, table_sent)
    last = jnp.concatenate([table_sum, weight_terms], axis=2)
    summed = total_of(spread(last, "ctx", chips_along_y()))
    table_grad = summed[:, :table_dev].T
    w_in_grad = summed[:, table_dev : table_dev + piece_in]
    w_out_grad = summed[:, table_dev + piece_in :]
    return (layer_out[None], table_grad, w_in_grad, w_out_grad)


def solution(mesh):
    return jax.shard_map(
        local,
        mesh=mesh,
        in_specs=(
            P(None, "dp", "ctx"),
            P("dp", "ctx"),
            P("dp", None),
            P(),
            P(),
            P("dp", "ctx", None),
        ),
        out_specs=(P("dp", "ctx", None), P("dp", "ctx"), P("ctx", "dp"), P("ctx", "dp")),
        check_vma=False,
    )
```

```python
import math

import jax
import jax.numpy as jnp
from jax import lax
from jax.experimental import pallas as pl
from jax.experimental.pallas import tpu as pltpu
from jax.sharding import PartitionSpec as P

H = 8
DH = 64
X_CHIPS = 4
REACH = 4
USER_ROWS = 16

epsilon = 1e-05
f32 = jnp.float32
bf16 = jnp.bfloat16


def passed_along(block, axis, distance):
    devices = range(lax.axis_size(axis))
    route = [(i - distance, i) for i in devices if i - distance in devices]
    return lax.ppermute(block, axis, route)


def swapped(block, senders=(0, 1)):
    devices = range(lax.axis_size("ctx"))
    return lax.ppermute(block, "ctx", [(i, i ^ 1) for i in devices if i % 2 in senders])


def halo_across(block, direction):
    return (
        passed_along(block, "ctx", 4 * direction),
        passed_along(block, "ctx", 2 * direction),
    )


def halo_inside(four, two, direction):
    far_sender = 1 if direction > 0 else 0
    return (swapped(four, (far_sender,)), swapped(two))


def nearest_last(core, four, mate_four, two, mate_two, mate_own):
    even = core == 0
    return (
        four,
        jnp.where(even, mate_four, mate_two),
        two,
        jnp.where(even, mate_two, mate_own),
    )


def nearest_first(core, four, mate_four, two, mate_two, mate_own):
    even = core == 0
    return (
        jnp.where(even, mate_own, mate_two),
        two,
        jnp.where(even, mate_two, mate_four),
        four,
    )


def layer_norm(values):
    centered = values - jnp.mean(values, axis=-1, keepdims=True)
    inverse = lax.rsqrt(jnp.mean(centered * centered, axis=-1, keepdims=True) + epsilon)
    return (centered * inverse, inverse)


def norm_backward(normed, inverse, upstream):
    first_mean = jnp.mean(upstream, axis=-1, keepdims=True)
    second_mean = jnp.mean(upstream * normed, axis=-1, keepdims=True)
    return inverse * (upstream - first_mean - normed * second_mean)


def sigmoid(values):
    return 0.5 * jnp.tanh(0.5 * values) + 0.5


def silu_slope(values):
    sig = sigmoid(values)
    return sig * (1.0 + values * (1.0 - sig))


def iota(shape, dim):
    return lax.broadcasted_iota(jnp.int32, shape, dim)


def dot(left, right):
    return jnp.dot(left, right, preferred_element_type=f32)


def dot_nt(left, right):
    return lax.dot_general(left, right, (((1,), (1,)), ((), ())), preferred_element_type=f32)


def dot_tn(left, right):
    return lax.dot_general(left, right, (((0,), (0,)), ((), ())), preferred_element_type=f32)


def hot(condition):
    return condition.astype(f32).astype(bf16)


def as_column(row):
    length = row.shape[1]
    eye = iota((length, length), 0) == iota((length, length), 1)
    return jnp.sum(jnp.where(eye, jnp.broadcast_to(row, (length, length)), 0.0), axis=1, keepdims=True)


def both_heads(pair):
    low = iota(pair.shape, 1) < DH
    zero = jnp.zeros_like(pair)
    return jnp.concatenate([jnp.where(low, pair, zero), jnp.where(low, zero, pair)], axis=0)


def one_pair(stacked):
    rows = stacked.shape[0] // 2
    low = iota((rows, stacked.shape[1]), 1) < DH
    return jnp.where(low, stacked[:rows], stacked[rows:])


def call(body, outs, *operands, core=None, flops=0, moved=0):
    in_specs = [pl.BlockSpec(memory_space=pltpu.VMEM)] * len(operands)
    if core is not None:
        in_specs = [pl.BlockSpec(memory_space=pltpu.SMEM)] + in_specs
        operands = (core,) + operands
    return pl.pallas_call(
        body,
        out_shape=[jax.ShapeDtypeStruct(shape, kind) for shape, kind in outs],
        in_specs=in_specs,
        compiler_params=pltpu.CompilerParams(vmem_limit_bytes=16 * 1024 * 1024),
        cost_estimate=pl.CostEstimate(flops=flops, bytes_accessed=moved, transcendentals=0),
    )(*operands)


def route_body(table_dev, ids_ref, request_ref, slot_ref):
    owners, capacity = request_ref.shape
    ids = jnp.concatenate([as_column(ids_ref[h : h + 1, :].astype(f32)) for h in range(2)], axis=0)
    ids = ids.astype(jnp.int32)
    count = ids.shape[0]
    shift = table_dev.bit_length() - 1
    owner = jnp.right_shift(ids, shift)
    row = jnp.bitwise_and(ids, table_dev - 1)
    member_f = (owner == iota((count, owners), 1)).astype(f32)
    member = member_f.astype(bf16)
    earlier = hot(iota((count, count), 0) > iota((count, count), 1))
    rank = jnp.sum(dot(earlier, member) * member_f, axis=1, keepdims=True).astype(jnp.int32)
    rank_hot = hot(rank == iota((count, capacity), 1))
    high = (member_f * jnp.right_shift(row, 4).astype(f32)).astype(bf16)
    low = (member_f * jnp.bitwise_and(row, 15).astype(f32)).astype(bf16)
    found = 16.0 * dot_tn(high, rank_hot) + dot_tn(low, rank_hot) + dot_tn(member, rank_hot)
    request_ref[...] = found.astype(jnp.int32) - 1
    slot_ref[...] = owner * capacity + rank


def gather_body(asked_ref, table_ref, found_ref, asked_row_ref):
    asked_rows = asked_ref[...]
    asked_row = jnp.concatenate(
        [asked_rows[g : g + 1, :] for g in range(asked_rows.shape[0])], axis=1
    )
    asked_row_ref[...] = asked_row
    slots = asked_row.shape[1]
    hits = hot(iota((table_ref.shape[0], slots), 0) == asked_row)
    found_ref[...] = dot_tn(hits, table_ref[...]).astype(bf16)


def slot_matrix(slot, slots):
    events = slot.shape[0] // 2
    places = iota((events, slots), 1)
    return hot((slot[:events] == places) | (slot[events:] == places))


def embed_body(slot_ref, fetched_ref, user_ref, inputs_ref, packed_ref):
    rows = inputs_ref.shape[0]
    places = slot_matrix(slot_ref[...], fetched_ref.shape[0])
    inputs = dot(places, fetched_ref[...]).astype(bf16)
    inputs_ref[...] = inputs
    packed_ref[:rows, :] = layer_norm(inputs.astype(f32))[0].astype(bf16)
    packed_ref[rows:, :] = user_rows(user_ref[...], packed_ref.shape[1])


def user_rows(user, width):
    wide = jnp.concatenate([user, jnp.zeros((1, width - user.shape[1]), f32)], axis=1)
    return jnp.broadcast_to(wide, (USER_ROWS, width)).astype(bf16)


def project_body(
    packed_ref, w_in_ref, w_out_ref, grad_ref,
    gates_ref, values_ref, queries_ref, keys_ref, mixed_grad_ref,
):
    rows = grad_ref.shape[0]
    width = grad_ref.shape[1]
    normed = packed_ref[:rows, :]
    for part, out_ref in enumerate((gates_ref, values_ref, queries_ref, keys_ref)):
        columns = slice(part * width, (part + 1) * width)
        projected = dot(normed, w_in_ref[:, columns])
        out_ref[...] = (projected * sigmoid(projected)).astype(bf16)
    mixed_grad_ref[...] = dot_nt(grad_ref[...], w_out_ref[...])


def window_mask(user_row, key_user_row, margin):
    rows = user_row.shape[1]
    columns = key_user_row.shape[1]
    user_column = as_column(user_row)
    allowed = (user_column == key_user_row) & (
        iota((rows, columns), 1) <= iota((rows, columns), 0) + margin
    )
    weight = allowed.astype(f32)
    return jnp.concatenate([weight, weight], axis=0) > 0.0


def forward_body(
    core_ref, four_ref, mate_four_ref, two_ref, mate_two_ref, mate_own_ref, values_ref, keys_ref, queries_ref, gates_ref,
    inputs_ref, mixed_grad_ref, w_in_ref, w_out_ref, user_ref,
    out_ref, mixed_ref, gate_grad_ref, att_grad_ref, all_keys_ref, all_values_ref, key_user_ref,
):
    rows, width = inputs_ref.shape
    score_scale = 1.0 / math.sqrt(DH)
    halos = nearest_last(
        core_ref[0], four_ref[...], mate_four_ref[...], two_ref[...], mate_two_ref[...], mate_own_ref[...]
    )
    far = jnp.concatenate([block[:rows, :] for block in halos], axis=0)
    margin = far.shape[0]
    for part, own_ref, all_ref in ((1, values_ref, all_values_ref), (3, keys_ref, all_keys_ref)):
        projected = dot(far, w_in_ref[:, part * width : (part + 1) * width])
        all_ref[:margin, :] = (projected * sigmoid(projected)).astype(bf16)
        all_ref[margin:, :] = own_ref[...]
    user_row = user_ref[...]
    key_user = jnp.concatenate(
        [block[rows : rows + 1, :rows].astype(f32) for block in halos] + [user_row], axis=1
    )
    key_user_ref[...] = key_user
    allowed = window_mask(user_row, key_user, margin)
    parts = []
    for pair in range(H // 2):
        columns = slice(2 * DH * pair, 2 * DH * (pair + 1))
        scores = dot_nt(both_heads(queries_ref[:, columns]), all_keys_ref[:, columns]) * score_scale
        weights = jnp.where(allowed, scores * sigmoid(scores), 0.0).astype(bf16)
        parts.append(one_pair(dot(weights, all_values_ref[:, columns])))
    att_hat, att_inv = layer_norm(jnp.concatenate(parts, axis=1))
    gates = gates_ref[...].astype(f32)
    mixed = (att_hat * gates).astype(bf16)
    mixed_ref[...] = mixed
    out_ref[...] = (inputs_ref[...].astype(f32) + dot(mixed, w_out_ref[...])).astype(bf16)
    mixed_grad = mixed_grad_ref[...]
    gate_grad_ref[...] = mixed_grad * att_hat
    att_grad_ref[...] = norm_backward(att_hat, att_inv, mixed_grad * gates).astype(bf16)


def core_first(block, rows):
    width = block.shape[1]
    old = iota((width, width), 0)
    new = iota((width, width), 1)
    inner = jnp.bitwise_and(old, rows - 1)
    device = jnp.right_shift(old, rows.bit_length() - 1)
    place = jnp.bitwise_and(device, 1) * (width // 2) + jnp.right_shift(device, 1) * rows + inner
    return dot(block, hot(new == place)).astype(bf16)


def split_by_core(core, terms, first_owner, piece, first_row, stride, kept_ref, sent_ref):
    half = terms.shape[1] // 2
    even = core == 0
    for local_owner in range(terms.shape[0] // piece):
        owner = first_owner + local_owner
        rows = terms[local_owner * piece : (local_owner + 1) * piece]
        place = first_row + (local_owner // X_CHIPS) * stride
        kept_ref[owner % X_CHIPS, place : place + piece, :] = jnp.where(
            even, rows[:, :half], rows[:, half:]
        ).astype(bf16)
        sent_ref[owner % X_CHIPS, place : place + piece, :] = jnp.where(
            even, rows[:, half:], rows[:, :half]
        ).astype(bf16)


def query_body(
    core_ref, queries_ref, all_keys_ref, all_values_ref, att_grad_ref, gate_grad_ref,
    packed_ref, user_ref, key_user_ref,
    four_ref, mate_four_ref, two_ref, mate_two_ref, mate_own_ref, w_in_ref,
    gate_query_ref, value_key_slope_ref, all_queries_ref, query_user_ref,
):
    rows, width = gate_grad_ref.shape
    score_scale = 1.0 / math.sqrt(DH)
    margin = all_keys_ref.shape[0] - rows
    allowed = window_mask(user_ref[...], key_user_ref[...], margin)
    parts = []
    for pair in range(H // 2):
        columns = slice(2 * DH * pair, 2 * DH * (pair + 1))
        keys = all_keys_ref[:, columns]
        scores = dot_nt(both_heads(queries_ref[:, columns]), keys) * score_scale
        prob_grad = dot_nt(both_heads(att_grad_ref[:, columns]), all_values_ref[:, columns])
        score_grad = jnp.where(allowed, prob_grad * silu_slope(scores), 0.0).astype(bf16)
        parts.append(one_pair(dot(score_grad, keys)) * score_scale)
    query_grad = jnp.concatenate(parts, axis=1)
    normed = packed_ref[:rows, :]
    gate_slope, value_slope, query_slope, key_slope = [
        silu_slope(dot(normed, w_in_ref[:, part * width : (part + 1) * width])) for part in range(4)
    ]
    value_key_slope_ref[:, :width] = value_slope
    value_key_slope_ref[:, width:] = key_slope
    gate_part = gate_grad_ref[...] * gate_slope
    query_part = query_grad * query_slope
    gate_query_ref[:, :width] = gate_part.astype(bf16)
    gate_query_ref[:, width:] = query_part.astype(bf16)
    halos = nearest_first(
        core_ref[0], four_ref[...], mate_four_ref[...], two_ref[...], mate_two_ref[...], mate_own_ref[...]
    )
    far = jnp.concatenate([block[:rows, :] for block in halos], axis=0)
    projected = dot(far, w_in_ref[:, 2 * width : 3 * width])
    all_queries_ref[:rows, :] = queries_ref[...]
    all_queries_ref[rows:, :] = (projected * sigmoid(projected)).astype(bf16)
    query_user_ref[...] = jnp.concatenate(
        [as_column(user_ref[...])]
        + [as_column(block[rows : rows + 1, :rows].astype(f32)) for block in halos],
        axis=0,
    )


def key_body(
    core_ref, all_queries_ref, query_user_ref, att_grad_ref,
    four_ref, mate_four_ref, two_ref, mate_two_ref, mate_own_ref,
    keys_ref, values_ref, value_key_slope_ref, gate_query_ref, w_in_ref, inputs_ref, out_grad_ref, slot_ref, user_ref,
    value_key_ref, outgoing_ref,
):
    rows, width = inputs_ref.shape
    score_scale = 1.0 / math.sqrt(DH)
    user_row = user_ref[...]
    query_user = query_user_ref[...]
    halos = nearest_first(
        core_ref[0], four_ref[...], mate_four_ref[...], two_ref[...], mate_two_ref[...], mate_own_ref[...]
    )
    all_grads = jnp.concatenate((att_grad_ref[...],) + halos, axis=0)
    total = query_user.shape[0]
    allowed = (query_user == user_row) & (iota((total, rows), 1) <= iota((total, rows), 0))
    weight = allowed.astype(f32)
    allowed = jnp.concatenate([weight, weight], axis=0) > 0.0
    key_parts = []
    value_parts = []
    for pair in range(H // 2):
        columns = slice(2 * DH * pair, 2 * DH * (pair + 1))
        queries = both_heads(all_queries_ref[:, columns])
        grads = both_heads(all_grads[:, columns])
        scores = dot_nt(queries, keys_ref[:, columns]) * score_scale
        sig = sigmoid(scores)
        raw = scores * sig
        weights = jnp.where(allowed, raw, 0.0).astype(bf16)
        prob_grad = dot_nt(grads, values_ref[:, columns])
        score_grad = jnp.where(allowed, prob_grad * (sig + raw * (1.0 - sig)), 0.0).astype(bf16)
        key_parts.append(dot_tn(score_grad, queries) * score_scale)
        value_parts.append(dot_tn(weights, grads))
    key_grad = jnp.concatenate(key_parts, axis=1)
    value_grad = jnp.concatenate(value_parts, axis=1)
    value_part = (value_grad * value_key_slope_ref[:, :width]).astype(bf16)
    key_part = (key_grad * value_key_slope_ref[:, width:]).astype(bf16)
    value_key_ref[:, :width] = value_part
    value_key_ref[:, width:] = key_part
    joined = jnp.concatenate(
        [gate_query_ref[:, :width], value_part, gate_query_ref[:, width:], key_part], axis=1
    )
    normed_grad = dot_nt(joined, w_in_ref[...])
    input_hat, input_inv = layer_norm(inputs_ref[...].astype(f32))
    inputs_grad = (
        out_grad_ref[...].astype(f32) + norm_backward(input_hat, input_inv, normed_grad)
    ).astype(bf16)
    places = slot_matrix(slot_ref[...], outgoing_ref.shape[0])
    outgoing_ref[...] = dot_tn(places, inputs_grad).astype(bf16)


def early_body(
    piece_in, piece_out, weight_rows,
    core_ref, packed_ref, gate_query_ref, mixed_ref, grad_ref, kept_ref, sent_ref,
):
    rows, width = grad_ref.shape
    core = core_ref[0]
    per_part = width // piece_in
    in_rows = piece_in * per_part // X_CHIPS
    normed = core_first(packed_ref[:rows, :], weight_rows)
    for section, first_owner in ((0, 0), (1, 2 * per_part)):
        terms = dot_tn(gate_query_ref[:, section * width : (section + 1) * width], normed)
        split_by_core(
            core, terms, first_owner, piece_in, section * in_rows, piece_in, kept_ref, sent_ref
        )
    terms = dot_tn(grad_ref[...], core_first(mixed_ref[...], weight_rows))
    split_by_core(core, terms, 0, piece_out, 2 * in_rows, piece_out, kept_ref, sent_ref)


def late_body(
    piece_in, piece_out, weight_rows,
    core_ref, packed_ref, value_key_ref, early_kept_ref, early_sent_ref, kept_ref, sent_ref,
):
    rows = value_key_ref.shape[0]
    width = value_key_ref.shape[1] // 2
    core = core_ref[0]
    piece = piece_in + piece_out
    z_part = width // piece_in // X_CHIPS
    z_chips = kept_ref.shape[1] // piece
    for early_ref, ref in ((early_kept_ref, kept_ref), (early_sent_ref, sent_ref)):
        for z in range(z_chips):
            section, inner = divmod(z, z_part)
            if section % 2 == 0:
                old = (section // 2 * z_part + inner) * piece_in
                ref[:, z * piece : z * piece + piece_in, :] = early_ref[:, old : old + piece_in, :]
            old = 2 * z_part * piece_in + z * piece_out
            ref[:, z * piece + piece_in : (z + 1) * piece, :] = early_ref[:, old : old + piece_out, :]
    normed = core_first(packed_ref[:rows, :], weight_rows)
    for section in range(2):
        terms = dot_tn(value_key_ref[:, section * width : (section + 1) * width], normed)
        split_by_core(
            core, terms, 0, piece_in, (2 * section + 1) * z_part * piece, piece, kept_ref, sent_ref
        )


def table_body(core_ref, asked_ref, arrived_ref, kept_ref, sent_ref):
    slots = asked_ref.shape[1]
    table_dev = kept_ref.shape[2]
    hits = hot(iota((table_dev, slots), 0) == asked_ref[...])
    sums = dot(hits, arrived_ref[...]).T
    rows = kept_ref.shape[1]
    even = core_ref[0] == 0
    for chip in range(kept_ref.shape[0]):
        first = sums[2 * chip * rows : (2 * chip + 1) * rows]
        second = sums[(2 * chip + 1) * rows : (2 * chip + 2) * rows]
        kept_ref[chip] = jnp.where(even, first, second).astype(bf16)
        sent_ref[chip] = jnp.where(even, second, first).astype(bf16)


def pair_sum(kept, sent):
    devices = lax.axis_size("ctx")
    got = lax.ppermute(sent, "ctx", [(i, i ^ 1) for i in range(devices)])
    return (kept.astype(f32) + got.astype(f32)).astype(bf16)


def chips_along_y():
    devices = lax.axis_size("ctx")
    return [list(range(first, devices, 2)) for first in range(2)]


def spread(block, axis, groups):
    return lax.all_to_all(
        block, axis, split_axis=0, concat_axis=0, tiled=True, axis_index_groups=groups
    )


def total_of(blocks):
    return jnp.sum(blocks.astype(f32), axis=0)


def sum_along_x(block):
    devices = lax.axis_size("dp")
    me = lax.axis_index("dp") % X_CHIPS
    own = lax.dynamic_index_in_dim(block, me, 0, keepdims=False).astype(f32)
    for step in range(1, X_CHIPS):
        route = [(i, i - i % X_CHIPS + (i + step) % X_CHIPS) for i in range(devices)]
        piece = lax.dynamic_index_in_dim(block, (me + step) % X_CHIPS, 0, keepdims=False)
        own = own + lax.ppermute(piece, "dp", route).astype(f32)
    return own.astype(bf16)


def chips_along_z(owners):
    return [list(range(first, owners, X_CHIPS)) for first in range(X_CHIPS)]


def local(item_ids, segments, touched_rows, w_in, w_out, out_grad):
    rows_dev = segments.shape[1]
    model_width = w_in.shape[0]
    table_dev = touched_rows.shape[0]
    owners = lax.axis_size("dp")
    capacity = max(rows_dev // 4, 6 * rows_dev // owners + 2)
    slots = owners * capacity
    core = (lax.axis_index("ctx") % 2).astype(jnp.int32).reshape(1)
    piece_in = w_in.shape[1] // owners
    piece_out = model_width // owners
    block = (rows_dev, model_width)
    packed_block = (rows_dev + USER_ROWS, model_width)
    reach_block = ((REACH + 1) * rows_dev, model_width)
    chips = lax.axis_size("ctx") // 2
    weight_rows = model_width // (2 * chips)

    user = (segments + 1).astype(f32)
    grad_rows = out_grad[0]
    requests, slot = call(
        lambda *refs: route_body(table_dev, *refs),
        [((owners, capacity), jnp.int32), ((2 * rows_dev, 1), jnp.int32)],
        item_ids.reshape(2, rows_dev),
    )
    asked = lax.all_to_all(requests, "dp", split_axis=0, concat_axis=0, tiled=True)
    found, asked_row = call(
        gather_body, [((slots, model_width), bf16), ((1, slots), jnp.int32)], asked, touched_rows
    )
    fetched = lax.all_to_all(
        found.reshape(owners, capacity, model_width), "dp", split_axis=0, concat_axis=0, tiled=True
    ).reshape(slots, model_width)
    inputs, packed = call(
        embed_body, [(block, bf16), (packed_block, bf16)], slot, fetched, user
    )
    mate_own = swapped(packed)
    earlier_four, earlier_two = halo_across(packed, 1)
    later_four, later_two = halo_across(packed, -1)
    gates, values, queries, keys, mixed_grad = call(
        project_body,
        [
            (block, bf16), (block, bf16), (block, bf16), (block, bf16), (block, f32),
        ],
        packed, w_in, w_out, grad_rows,
        flops=1_500_000_000, moved=6_000_000,
    )
    earlier_four, later_four, later_two, mate_own, mixed_grad = lax.optimization_barrier(
        (earlier_four, later_four, later_two, mate_own, mixed_grad)
    )
    inside = halo_inside(earlier_four, earlier_two, 1) + halo_inside(later_four, later_two, -1)
    mate_four, mate_two, later_mate_four, later_mate_two = lax.optimization_barrier(inside)
    earlier = (earlier_four, mate_four, earlier_two, mate_two, mate_own)
    later = (later_four, later_mate_four, later_two, later_mate_two, mate_own)
    layer_out, mixed, gate_grad, att_grad, all_keys, all_values, key_user = call(
        forward_body,
        [
            (block, bf16), (block, bf16), (block, f32), (block, bf16),
            (reach_block, bf16), (reach_block, bf16), ((1, (REACH + 1) * rows_dev), f32),
        ],
        *earlier, values, keys, queries, gates, inputs, mixed_grad, w_in, w_out, user,
        core=core, flops=4_000_000_000, moved=8_000_000,
    )
    own_grad = swapped(att_grad, (1,))
    grad_four, grad_two = halo_across(att_grad, -1)
    grad_mate_four, grad_mate_two = halo_inside(grad_four, grad_two, -1)
    gate_grad, own_grad, grad_two = lax.optimization_barrier((gate_grad, own_grad, grad_two))
    mixed, grad_four, grad_mate_two = lax.optimization_barrier((mixed, grad_four, grad_mate_two))
    later_grads = (grad_four, grad_mate_four, grad_two, grad_mate_two, own_grad)
    gate_query, value_key_slope, all_queries, query_user = call(
        query_body,
        [
            ((rows_dev, 2 * model_width), bf16), ((rows_dev, 2 * model_width), f32), (reach_block, bf16),
            (((REACH + 1) * rows_dev, 1), f32),
        ],
        queries, all_keys, all_values, att_grad, gate_grad, packed, user, key_user, *later, w_in,
        core=core, flops=4_000_000_000, moved=8_000_000,
    )
    half_width = model_width // 2
    early_block = (X_CHIPS, 3 * model_width // X_CHIPS, half_width)
    early_kept, early_sent = call(
        lambda *refs: early_body(piece_in, piece_out, weight_rows, *refs),
        [(early_block, bf16), (early_block, bf16)],
        packed, gate_query, mixed, grad_rows,
        core=core, flops=2_000_000_000, moved=4_000_000,
    )
    gate_query, early_kept, early_sent = lax.optimization_barrier(
        (gate_query, early_kept, early_sent)
    )
    value_key, outgoing = call(
        key_body,
        [((rows_dev, 2 * model_width), bf16), ((slots, model_width), bf16)],
        all_queries, query_user, att_grad, *later_grads, keys, values, value_key_slope, gate_query,
        w_in, inputs, grad_rows, slot, user,
        core=core, flops=4_000_000_000, moved=8_000_000,
    )
    arrived = lax.all_to_all(
        outgoing.reshape(owners, capacity, model_width), "dp", split_axis=0, concat_axis=0, tiled=True
    ).reshape(slots, model_width)
    piece = piece_in + piece_out
    z_chips = owners // X_CHIPS
    weight_block = (X_CHIPS, z_chips * piece, half_width)
    weight_kept, weight_sent = call(
        lambda *refs: late_body(piece_in, piece_out, weight_rows, *refs),
        [(weight_block, bf16), (weight_block, bf16)],
        packed, value_key, early_kept, early_sent,
        core=core, flops=1_500_000_000, moved=3_000_000,
    )
    along_x = sum_along_x(pair_sum(weight_kept, weight_sent)).reshape(z_chips, piece, half_width)
    arrived, along_x = lax.optimization_barrier((arrived, along_x))
    along_dp = total_of(spread(along_x, "dp", chips_along_z(owners))).astype(bf16)
    weight_terms = along_dp.T.reshape(chips, weight_rows, piece)
    table_block = (chips, model_width // (2 * chips), table_dev)
    table_kept, table_sent = call(
        table_body, [(table_block, bf16), (table_block, bf16)], asked_row, arrived, core=core
    )
    table_sum = pair_sum(table_kept, table_sent)
    last = jnp.concatenate([table_sum, weight_terms], axis=2)
    summed = total_of(spread(last, "ctx", chips_along_y()))
    table_grad = summed[:, :table_dev].T
    w_in_grad = summed[:, table_dev : table_dev + piece_in]
    w_out_grad = summed[:, table_dev + piece_in :]
    return (layer_out[None], table_grad, w_in_grad, w_out_grad)


def solution(mesh):
    return jax.shard_map(
        local,
        mesh=mesh,
        in_specs=(
            P(None, "dp", "ctx"),
            P("dp", "ctx"),
            P("dp", None),
            P(),
            P(),
            P("dp", "ctx", None),
        ),
        out_specs=(P("dp", "ctx", None), P("dp", "ctx"), P("ctx", "dp"), P("ctx", "dp")),
        check_vma=False,
    )
```

```python
import math

import jax
import jax.numpy as jnp
from jax import lax
from jax.experimental import pallas as pl
from jax.experimental.pallas import tpu as pltpu
from jax.sharding import PartitionSpec as P

H = 8
DH = 64
X_CHIPS = 4
REACH = 4
USER_ROWS = 16

epsilon = 1e-05
f32 = jnp.float32
bf16 = jnp.bfloat16


def passed_along(block, axis, distance):
    devices = range(lax.axis_size(axis))
    route = [(i - distance, i) for i in devices if i - distance in devices]
    return lax.ppermute(block, axis, route)


def swapped(block, senders=(0, 1)):
    devices = range(lax.axis_size("ctx"))
    return lax.ppermute(block, "ctx", [(i, i ^ 1) for i in devices if i % 2 in senders])


def mate_of_four(four, direction):
    return swapped(four, (1,) if direction > 0 else (0,))


def nearest_last(core, four, mate_four, two, mate_two, mate_own):
    even = core == 0
    return (
        four,
        jnp.where(even, mate_four, mate_two),
        two,
        jnp.where(even, mate_two, mate_own),
    )


def nearest_first(core, four, mate_four, two, mate_two, mate_own):
    even = core == 0
    return (
        jnp.where(even, mate_own, mate_two),
        two,
        jnp.where(even, mate_two, mate_four),
        four,
    )


def layer_norm(values):
    centered = values - jnp.mean(values, axis=-1, keepdims=True)
    inverse = lax.rsqrt(jnp.mean(centered * centered, axis=-1, keepdims=True) + epsilon)
    return (centered * inverse, inverse)


def norm_backward(normed, inverse, upstream):
    first_mean = jnp.mean(upstream, axis=-1, keepdims=True)
    second_mean = jnp.mean(upstream * normed, axis=-1, keepdims=True)
    return inverse * (upstream - first_mean - normed * second_mean)


def sigmoid(values):
    return 0.5 * jnp.tanh(0.5 * values) + 0.5


def silu_slope(values):
    sig = sigmoid(values)
    return sig * (1.0 + values * (1.0 - sig))


def iota(shape, dim):
    return lax.broadcasted_iota(jnp.int32, shape, dim)


def dot(left, right):
    return jnp.dot(left, right, preferred_element_type=f32)


def dot_nt(left, right):
    return lax.dot_general(left, right, (((1,), (1,)), ((), ())), preferred_element_type=f32)


def dot_tn(left, right):
    return lax.dot_general(left, right, (((0,), (0,)), ((), ())), preferred_element_type=f32)


def hot(condition):
    return condition.astype(f32).astype(bf16)


def as_column(row):
    length = row.shape[1]
    eye = iota((length, length), 0) == iota((length, length), 1)
    return jnp.sum(jnp.where(eye, jnp.broadcast_to(row, (length, length)), 0.0), axis=1, keepdims=True)


def both_heads(pair):
    low = iota(pair.shape, 1) < DH
    zero = jnp.zeros_like(pair)
    return jnp.concatenate([jnp.where(low, pair, zero), jnp.where(low, zero, pair)], axis=0)


def one_pair(stacked):
    rows = stacked.shape[0] // 2
    low = iota((rows, stacked.shape[1]), 1) < DH
    return jnp.where(low, stacked[:rows], stacked[rows:])


def call(body, outs, *operands, core=None, flops=0, moved=0):
    in_specs = [pl.BlockSpec(memory_space=pltpu.VMEM)] * len(operands)
    if core is not None:
        in_specs = [pl.BlockSpec(memory_space=pltpu.SMEM)] + in_specs
        operands = (core,) + operands
    return pl.pallas_call(
        body,
        out_shape=[jax.ShapeDtypeStruct(shape, kind) for shape, kind in outs],
        in_specs=in_specs,
        compiler_params=pltpu.CompilerParams(vmem_limit_bytes=16 * 1024 * 1024),
        cost_estimate=pl.CostEstimate(flops=flops, bytes_accessed=moved, transcendentals=0),
    )(*operands)


def route_body(table_dev, ids_ref, request_ref, slot_ref):
    owners, capacity = request_ref.shape
    ids = jnp.concatenate([as_column(ids_ref[h : h + 1, :].astype(f32)) for h in range(2)], axis=0)
    ids = ids.astype(jnp.int32)
    count = ids.shape[0]
    shift = table_dev.bit_length() - 1
    owner = jnp.right_shift(ids, shift)
    row = jnp.bitwise_and(ids, table_dev - 1)
    member_f = (owner == iota((count, owners), 1)).astype(f32)
    member = member_f.astype(bf16)
    earlier = hot(iota((count, count), 0) > iota((count, count), 1))
    rank = jnp.sum(dot(earlier, member) * member_f, axis=1, keepdims=True).astype(jnp.int32)
    rank_hot = hot(rank == iota((count, capacity), 1))
    high = (member_f * jnp.right_shift(row, 4).astype(f32)).astype(bf16)
    low = (member_f * jnp.bitwise_and(row, 15).astype(f32)).astype(bf16)
    found = 16.0 * dot_tn(high, rank_hot) + dot_tn(low, rank_hot) + dot_tn(member, rank_hot)
    request_ref[...] = found.astype(jnp.int32) - 1
    slot_ref[...] = owner * capacity + rank


def gather_body(asked_ref, table_ref, found_ref, asked_row_ref):
    asked_rows = asked_ref[...]
    asked_row = jnp.concatenate(
        [asked_rows[g : g + 1, :] for g in range(asked_rows.shape[0])], axis=1
    )
    asked_row_ref[...] = asked_row
    slots = asked_row.shape[1]
    hits = hot(iota((table_ref.shape[0], slots), 0) == asked_row)
    found_ref[...] = dot_tn(hits, table_ref[...]).astype(bf16)


def slot_matrix(slot, slots):
    events = slot.shape[0] // 2
    places = iota((events, slots), 1)
    return hot((slot[:events] == places) | (slot[events:] == places))


def embed_body(slot_ref, fetched_ref, user_ref, inputs_ref, packed_ref):
    rows = inputs_ref.shape[0]
    places = slot_matrix(slot_ref[...], fetched_ref.shape[0])
    inputs = dot(places, fetched_ref[...]).astype(bf16)
    inputs_ref[...] = inputs
    packed_ref[:rows, :] = layer_norm(inputs.astype(f32))[0].astype(bf16)
    packed_ref[rows:, :] = user_rows(user_ref[...], packed_ref.shape[1])


def user_rows(user, width):
    wide = jnp.concatenate([user, jnp.zeros((1, width - user.shape[1]), f32)], axis=1)
    return jnp.broadcast_to(wide, (USER_ROWS, width)).astype(bf16)


def project_body(
    packed_ref, w_in_ref, w_out_ref, grad_ref,
    gates_ref, values_ref, queries_ref, keys_ref, mixed_grad_ref,
):
    rows = grad_ref.shape[0]
    width = grad_ref.shape[1]
    normed = packed_ref[:rows, :]
    for part, out_ref in enumerate((gates_ref, values_ref, queries_ref, keys_ref)):
        columns = slice(part * width, (part + 1) * width)
        projected = dot(normed, w_in_ref[:, columns])
        out_ref[...] = (projected * sigmoid(projected)).astype(bf16)
    mixed_grad_ref[...] = dot_nt(grad_ref[...], w_out_ref[...])


def window_mask(user_row, key_user_row, margin):
    rows = user_row.shape[1]
    columns = key_user_row.shape[1]
    user_column = as_column(user_row)
    allowed = (user_column == key_user_row) & (
        iota((rows, columns), 1) <= iota((rows, columns), 0) + margin
    )
    weight = allowed.astype(f32)
    return jnp.concatenate([weight, weight], axis=0) > 0.0


def forward_body(
    core_ref, four_ref, mate_four_ref, two_ref, mate_two_ref, mate_own_ref, values_ref, keys_ref, queries_ref, gates_ref,
    inputs_ref, mixed_grad_ref, w_in_ref, w_out_ref, user_ref,
    out_ref, mixed_ref, gate_grad_ref, att_grad_ref, all_keys_ref, all_values_ref, key_user_ref,
):
    rows, width = inputs_ref.shape
    score_scale = 1.0 / math.sqrt(DH)
    halos = nearest_last(
        core_ref[0], four_ref[...], mate_four_ref[...], two_ref[...], mate_two_ref[...], mate_own_ref[...]
    )
    far = jnp.concatenate([block[:rows, :] for block in halos], axis=0)
    margin = far.shape[0]
    for part, own_ref, all_ref in ((1, values_ref, all_values_ref), (3, keys_ref, all_keys_ref)):
        projected = dot(far, w_in_ref[:, part * width : (part + 1) * width])
        all_ref[:margin, :] = (projected * sigmoid(projected)).astype(bf16)
        all_ref[margin:, :] = own_ref[...]
    user_row = user_ref[...]
    key_user = jnp.concatenate(
        [block[rows : rows + 1, :rows].astype(f32) for block in halos] + [user_row], axis=1
    )
    key_user_ref[...] = key_user
    allowed = window_mask(user_row, key_user, margin)
    parts = []
    for pair in range(H // 2):
        columns = slice(2 * DH * pair, 2 * DH * (pair + 1))
        scores = dot_nt(both_heads(queries_ref[:, columns]), all_keys_ref[:, columns]) * score_scale
        weights = jnp.where(allowed, scores * sigmoid(scores), 0.0).astype(bf16)
        parts.append(one_pair(dot(weights, all_values_ref[:, columns])))
    att_hat, att_inv = layer_norm(jnp.concatenate(parts, axis=1))
    gates = gates_ref[...].astype(f32)
    mixed = (att_hat * gates).astype(bf16)
    mixed_ref[...] = mixed
    out_ref[...] = (inputs_ref[...].astype(f32) + dot(mixed, w_out_ref[...])).astype(bf16)
    mixed_grad = mixed_grad_ref[...]
    gate_grad_ref[...] = mixed_grad * att_hat
    att_grad_ref[...] = norm_backward(att_hat, att_inv, mixed_grad * gates).astype(bf16)


def core_first(block, rows):
    width = block.shape[1]
    old = iota((width, width), 0)
    new = iota((width, width), 1)
    inner = jnp.bitwise_and(old, rows - 1)
    device = jnp.right_shift(old, rows.bit_length() - 1)
    place = jnp.bitwise_and(device, 1) * (width // 2) + jnp.right_shift(device, 1) * rows + inner
    return dot(block, hot(new == place)).astype(bf16)


def split_by_core(core, terms, first_owner, piece, first_row, stride, kept_ref, sent_ref):
    half = terms.shape[1] // 2
    even = core == 0
    for local_owner in range(terms.shape[0] // piece):
        owner = first_owner + local_owner
        rows = terms[local_owner * piece : (local_owner + 1) * piece]
        place = first_row + (local_owner // X_CHIPS) * stride
        kept_ref[owner % X_CHIPS, place : place + piece, :] = jnp.where(
            even, rows[:, :half], rows[:, half:]
        ).astype(bf16)
        sent_ref[owner % X_CHIPS, place : place + piece, :] = jnp.where(
            even, rows[:, half:], rows[:, :half]
        ).astype(bf16)


def query_body(
    core_ref, queries_ref, all_keys_ref, all_values_ref, att_grad_ref, gate_grad_ref,
    packed_ref, user_ref, key_user_ref,
    four_ref, mate_four_ref, two_ref, mate_two_ref, mate_own_ref, w_in_ref,
    gate_query_ref, value_key_slope_ref, all_queries_ref, query_user_ref,
):
    rows, width = gate_grad_ref.shape
    score_scale = 1.0 / math.sqrt(DH)
    margin = all_keys_ref.shape[0] - rows
    allowed = window_mask(user_ref[...], key_user_ref[...], margin)
    parts = []
    for pair in range(H // 2):
        columns = slice(2 * DH * pair, 2 * DH * (pair + 1))
        keys = all_keys_ref[:, columns]
        scores = dot_nt(both_heads(queries_ref[:, columns]), keys) * score_scale
        prob_grad = dot_nt(both_heads(att_grad_ref[:, columns]), all_values_ref[:, columns])
        score_grad = jnp.where(allowed, prob_grad * silu_slope(scores), 0.0).astype(bf16)
        parts.append(one_pair(dot(score_grad, keys)) * score_scale)
    query_grad = jnp.concatenate(parts, axis=1)
    normed = packed_ref[:rows, :]
    gate_slope, value_slope, query_slope, key_slope = [
        silu_slope(dot(normed, w_in_ref[:, part * width : (part + 1) * width])) for part in range(4)
    ]
    value_key_slope_ref[:, :width] = value_slope
    value_key_slope_ref[:, width:] = key_slope
    gate_part = gate_grad_ref[...] * gate_slope
    query_part = query_grad * query_slope
    gate_query_ref[:, :width] = gate_part.astype(bf16)
    gate_query_ref[:, width:] = query_part.astype(bf16)
    halos = nearest_first(
        core_ref[0], four_ref[...], mate_four_ref[...], two_ref[...], mate_two_ref[...], mate_own_ref[...]
    )
    far = jnp.concatenate([block[:rows, :] for block in halos], axis=0)
    projected = dot(far, w_in_ref[:, 2 * width : 3 * width])
    all_queries_ref[:rows, :] = queries_ref[...]
    all_queries_ref[rows:, :] = (projected * sigmoid(projected)).astype(bf16)
    query_user_ref[...] = jnp.concatenate(
        [as_column(user_ref[...])]
        + [as_column(block[rows : rows + 1, :rows].astype(f32)) for block in halos],
        axis=0,
    )


def key_body(
    core_ref, all_queries_ref, query_user_ref, att_grad_ref,
    four_ref, mate_four_ref, two_ref, mate_two_ref, mate_own_ref,
    keys_ref, values_ref, value_key_slope_ref, gate_query_ref, w_in_ref, inputs_ref, out_grad_ref, slot_ref, user_ref,
    value_key_ref, outgoing_ref,
):
    rows, width = inputs_ref.shape
    score_scale = 1.0 / math.sqrt(DH)
    user_row = user_ref[...]
    query_user = query_user_ref[...]
    halos = nearest_first(
        core_ref[0], four_ref[...], mate_four_ref[...], two_ref[...], mate_two_ref[...], mate_own_ref[...]
    )
    all_grads = jnp.concatenate((att_grad_ref[...],) + halos, axis=0)
    total = query_user.shape[0]
    allowed = (query_user == user_row) & (iota((total, rows), 1) <= iota((total, rows), 0))
    weight = allowed.astype(f32)
    allowed = jnp.concatenate([weight, weight], axis=0) > 0.0
    key_parts = []
    value_parts = []
    for pair in range(H // 2):
        columns = slice(2 * DH * pair, 2 * DH * (pair + 1))
        queries = both_heads(all_queries_ref[:, columns])
        grads = both_heads(all_grads[:, columns])
        scores = dot_nt(queries, keys_ref[:, columns]) * score_scale
        sig = sigmoid(scores)
        raw = scores * sig
        weights = jnp.where(allowed, raw, 0.0).astype(bf16)
        prob_grad = dot_nt(grads, values_ref[:, columns])
        score_grad = jnp.where(allowed, prob_grad * (sig + raw * (1.0 - sig)), 0.0).astype(bf16)
        key_parts.append(dot_tn(score_grad, queries) * score_scale)
        value_parts.append(dot_tn(weights, grads))
    key_grad = jnp.concatenate(key_parts, axis=1)
    value_grad = jnp.concatenate(value_parts, axis=1)
    value_part = (value_grad * value_key_slope_ref[:, :width]).astype(bf16)
    key_part = (key_grad * value_key_slope_ref[:, width:]).astype(bf16)
    value_key_ref[:, :width] = value_part
    value_key_ref[:, width:] = key_part
    joined = jnp.concatenate(
        [gate_query_ref[:, :width], value_part, gate_query_ref[:, width:], key_part], axis=1
    )
    normed_grad = dot_nt(joined, w_in_ref[...])
    input_hat, input_inv = layer_norm(inputs_ref[...].astype(f32))
    inputs_grad = (
        out_grad_ref[...].astype(f32) + norm_backward(input_hat, input_inv, normed_grad)
    ).astype(bf16)
    places = slot_matrix(slot_ref[...], outgoing_ref.shape[0])
    outgoing_ref[...] = dot_tn(places, inputs_grad).astype(bf16)


def early_body(
    piece_in, piece_out, weight_rows,
    core_ref, packed_ref, gate_query_ref, mixed_ref, grad_ref, kept_ref, sent_ref,
):
    rows, width = grad_ref.shape
    core = core_ref[0]
    per_part = width // piece_in
    in_rows = piece_in * per_part // X_CHIPS
    normed = core_first(packed_ref[:rows, :], weight_rows)
    for section, first_owner in ((0, 0), (1, 2 * per_part)):
        terms = dot_tn(gate_query_ref[:, section * width : (section + 1) * width], normed)
        split_by_core(
            core, terms, first_owner, piece_in, section * in_rows, piece_in, kept_ref, sent_ref
        )
    terms = dot_tn(grad_ref[...], core_first(mixed_ref[...], weight_rows))
    split_by_core(core, terms, 0, piece_out, 2 * in_rows, piece_out, kept_ref, sent_ref)


def late_body(
    piece_in, piece_out, weight_rows,
    core_ref, packed_ref, value_key_ref, early_kept_ref, early_sent_ref, kept_ref, sent_ref,
):
    rows = value_key_ref.shape[0]
    width = value_key_ref.shape[1] // 2
    core = core_ref[0]
    piece = piece_in + piece_out
    z_part = width // piece_in // X_CHIPS
    z_chips = kept_ref.shape[1] // piece
    for early_ref, ref in ((early_kept_ref, kept_ref), (early_sent_ref, sent_ref)):
        for z in range(z_chips):
            section, inner = divmod(z, z_part)
            if section % 2 == 0:
                old = (section // 2 * z_part + inner) * piece_in
                ref[:, z * piece : z * piece + piece_in, :] = early_ref[:, old : old + piece_in, :]
            old = 2 * z_part * piece_in + z * piece_out
            ref[:, z * piece + piece_in : (z + 1) * piece, :] = early_ref[:, old : old + piece_out, :]
    normed = core_first(packed_ref[:rows, :], weight_rows)
    for section in range(2):
        terms = dot_tn(value_key_ref[:, section * width : (section + 1) * width], normed)
        split_by_core(
            core, terms, 0, piece_in, (2 * section + 1) * z_part * piece, piece, kept_ref, sent_ref
        )


def table_body(core_ref, asked_ref, arrived_ref, kept_ref, sent_ref):
    slots = asked_ref.shape[1]
    table_dev = kept_ref.shape[2]
    hits = hot(iota((table_dev, slots), 0) == asked_ref[...])
    sums = dot(hits, arrived_ref[...]).T
    rows = kept_ref.shape[1]
    even = core_ref[0] == 0
    for chip in range(kept_ref.shape[0]):
        first = sums[2 * chip * rows : (2 * chip + 1) * rows]
        second = sums[(2 * chip + 1) * rows : (2 * chip + 2) * rows]
        kept_ref[chip] = jnp.where(even, first, second).astype(bf16)
        sent_ref[chip] = jnp.where(even, second, first).astype(bf16)


def pair_sum(kept, sent):
    devices = lax.axis_size("ctx")
    got = lax.ppermute(sent, "ctx", [(i, i ^ 1) for i in range(devices)])
    return (kept.astype(f32) + got.astype(f32)).astype(bf16)


def chips_along_y():
    devices = lax.axis_size("ctx")
    return [list(range(first, devices, 2)) for first in range(2)]


def spread(block, axis, groups):
    return lax.all_to_all(
        block, axis, split_axis=0, concat_axis=0, tiled=True, axis_index_groups=groups
    )


def total_of(blocks):
    return jnp.sum(blocks.astype(f32), axis=0)


def sum_along_x(block):
    devices = lax.axis_size("dp")
    me = lax.axis_index("dp") % X_CHIPS
    own = lax.dynamic_index_in_dim(block, me, 0, keepdims=False).astype(f32)
    for step in range(1, X_CHIPS):
        route = [(i, i - i % X_CHIPS + (i + step) % X_CHIPS) for i in range(devices)]
        piece = lax.dynamic_index_in_dim(block, (me + step) % X_CHIPS, 0, keepdims=False)
        own = own + lax.ppermute(piece, "dp", route).astype(f32)
    return own.astype(bf16)


def chips_along_z(owners):
    return [list(range(first, owners, X_CHIPS)) for first in range(X_CHIPS)]


def local(item_ids, segments, touched_rows, w_in, w_out, out_grad):
    rows_dev = segments.shape[1]
    model_width = w_in.shape[0]
    table_dev = touched_rows.shape[0]
    owners = lax.axis_size("dp")
    capacity = max(rows_dev // 4, 6 * rows_dev // owners + 2)
    slots = owners * capacity
    core = (lax.axis_index("ctx") % 2).astype(jnp.int32).reshape(1)
    piece_in = w_in.shape[1] // owners
    piece_out = model_width // owners
    block = (rows_dev, model_width)
    packed_block = (rows_dev + USER_ROWS, model_width)
    reach_block = ((REACH + 1) * rows_dev, model_width)
    chips = lax.axis_size("ctx") // 2
    weight_rows = model_width // (2 * chips)

    user = (segments + 1).astype(f32)
    grad_rows = out_grad[0]
    requests, slot = call(
        lambda *refs: route_body(table_dev, *refs),
        [((owners, capacity), jnp.int32), ((2 * rows_dev, 1), jnp.int32)],
        item_ids.reshape(2, rows_dev),
    )
    asked = lax.all_to_all(requests, "dp", split_axis=0, concat_axis=0, tiled=True)
    found, asked_row = call(
        gather_body, [((slots, model_width), bf16), ((1, slots), jnp.int32)], asked, touched_rows
    )
    fetched = lax.all_to_all(
        found.reshape(owners, capacity, model_width), "dp", split_axis=0, concat_axis=0, tiled=True
    ).reshape(slots, model_width)
    inputs, packed = call(
        embed_body, [(block, bf16), (packed_block, bf16)], slot, fetched, user
    )
    earlier_two = passed_along(packed, "ctx", 2)
    gates, values, queries, keys, mixed_grad = call(
        project_body,
        [
            (block, bf16), (block, bf16), (block, bf16), (block, bf16), (block, f32),
        ],
        packed, w_in, w_out, grad_rows,
        flops=1_500_000_000, moved=6_000_000,
    )
    packed_later, mixed_grad = lax.optimization_barrier((packed, mixed_grad))
    mate_own = swapped(packed_later)
    later_two = passed_along(packed_later, "ctx", -2)
    earlier_two, mixed_grad = lax.optimization_barrier((earlier_two, mixed_grad))
    earlier_four = passed_along(earlier_two, "ctx", 2)
    earlier_four, mate_two, mate_own = lax.optimization_barrier(
        (earlier_four, swapped(earlier_two), mate_own)
    )
    mate_four, later_mate_two = lax.optimization_barrier(
        (mate_of_four(earlier_four, 1), swapped(later_two))
    )
    earlier = (earlier_four, mate_four, earlier_two, mate_two, mate_own)
    later_four = passed_along(later_two, "ctx", -2)
    layer_out, mixed, gate_grad, att_grad, all_keys, all_values, key_user = call(
        forward_body,
        [
            (block, bf16), (block, bf16), (block, f32), (block, bf16),
            (reach_block, bf16), (reach_block, bf16), ((1, (REACH + 1) * rows_dev), f32),
        ],
        *earlier, values, keys, queries, gates, inputs, mixed_grad, w_in, w_out, user,
        core=core, flops=4_000_000_000, moved=8_000_000,
    )
    own_grad = swapped(att_grad, (1,))
    grad_two = passed_along(att_grad, "ctx", -2)
    grad_four = passed_along(grad_two, "ctx", -2)
    later_four, own_grad = lax.optimization_barrier((later_four, own_grad))
    later = (later_four, mate_of_four(later_four, -1), later_two, later_mate_two, mate_own)
    grad_mate_two = swapped(grad_two)
    gate_grad, own_grad, grad_mate_two = lax.optimization_barrier((gate_grad, own_grad, grad_mate_two))
    gate_query, value_key_slope, all_queries, query_user = call(
        query_body,
        [
            ((rows_dev, 2 * model_width), bf16), ((rows_dev, 2 * model_width), f32), (reach_block, bf16),
            (((REACH + 1) * rows_dev, 1), f32),
        ],
        queries, all_keys, all_values, att_grad, gate_grad, packed, user, key_user, *later, w_in,
        core=core, flops=4_000_000_000, moved=8_000_000,
    )
    gate_query, mixed, grad_four = lax.optimization_barrier((gate_query, mixed, grad_four))
    later_grads = (
        grad_four, mate_of_four(grad_four, -1), grad_two, grad_mate_two, own_grad,
    )
    half_width = model_width // 2
    early_block = (X_CHIPS, 3 * model_width // X_CHIPS, half_width)
    early_kept, early_sent = call(
        lambda *refs: early_body(piece_in, piece_out, weight_rows, *refs),
        [(early_block, bf16), (early_block, bf16)],
        packed, gate_query, mixed, grad_rows,
        core=core, flops=2_000_000_000, moved=4_000_000,
    )
    gate_query, early_kept, early_sent = lax.optimization_barrier(
        (gate_query, early_kept, early_sent)
    )
    value_key, outgoing = call(
        key_body,
        [((rows_dev, 2 * model_width), bf16), ((slots, model_width), bf16)],
        all_queries, query_user, att_grad, *later_grads, keys, values, value_key_slope, gate_query,
        w_in, inputs, grad_rows, slot, user,
        core=core, flops=4_000_000_000, moved=8_000_000,
    )
    arrived = lax.all_to_all(
        outgoing.reshape(owners, capacity, model_width), "dp", split_axis=0, concat_axis=0, tiled=True
    ).reshape(slots, model_width)
    piece = piece_in + piece_out
    z_chips = owners // X_CHIPS
    weight_block = (X_CHIPS, z_chips * piece, half_width)
    weight_kept, weight_sent = call(
        lambda *refs: late_body(piece_in, piece_out, weight_rows, *refs),
        [(weight_block, bf16), (weight_block, bf16)],
        packed, value_key, early_kept, early_sent,
        core=core, flops=1_500_000_000, moved=3_000_000,
    )
    along_x = sum_along_x(pair_sum(weight_kept, weight_sent)).reshape(z_chips, piece, half_width)
    arrived, along_x = lax.optimization_barrier((arrived, along_x))
    along_dp = total_of(spread(along_x, "dp", chips_along_z(owners))).astype(bf16)
    weight_terms = along_dp.T.reshape(chips, weight_rows, piece)
    table_block = (chips, model_width // (2 * chips), table_dev)
    table_kept, table_sent = call(
        table_body, [(table_block, bf16), (table_block, bf16)], asked_row, arrived, core=core
    )
    table_sum = pair_sum(table_kept, table_sent)
    last = jnp.concatenate([table_sum, weight_terms], axis=2)
    summed = total_of(spread(last, "ctx", chips_along_y()))
    table_grad = summed[:, :table_dev].T
    w_in_grad = summed[:, table_dev : table_dev + piece_in]
    w_out_grad = summed[:, table_dev + piece_in :]
    return (layer_out[None], table_grad, w_in_grad, w_out_grad)


def solution(mesh):
    return jax.shard_map(
        local,
        mesh=mesh,
        in_specs=(
            P(None, "dp", "ctx"),
            P("dp", "ctx"),
            P("dp", None),
            P(),
            P(),
            P("dp", "ctx", None),
        ),
        out_specs=(P("dp", "ctx", None), P("dp", "ctx"), P("ctx", "dp"), P("ctx", "dp")),
        check_vma=False,
    )
```

```python
import math

import jax
import jax.numpy as jnp
from jax import lax
from jax.experimental import pallas as pl
from jax.experimental.pallas import tpu as pltpu
from jax.sharding import PartitionSpec as P

H = 8
DH = 64
X_CHIPS = 4
REACH = 4
USER_ROWS = 16

epsilon = 1e-05
f32 = jnp.float32
bf16 = jnp.bfloat16


def passed_along(block, axis, distance):
    devices = range(lax.axis_size(axis))
    route = [(i - distance, i) for i in devices if i - distance in devices]
    return lax.ppermute(block, axis, route)


def swapped(block, senders=(0, 1)):
    devices = range(lax.axis_size("ctx"))
    return lax.ppermute(block, "ctx", [(i, i ^ 1) for i in devices if i % 2 in senders])


def mate_of_four(four, direction):
    return swapped(four, (1,) if direction > 0 else (0,))


def nearest_last(core, four, mate_four, two, mate_two, mate_own):
    even = core == 0
    return (
        four,
        jnp.where(even, mate_four, mate_two),
        two,
        jnp.where(even, mate_two, mate_own),
    )


def nearest_first(core, four, mate_four, two, mate_two, mate_own):
    even = core == 0
    return (
        jnp.where(even, mate_own, mate_two),
        two,
        jnp.where(even, mate_two, mate_four),
        four,
    )


def layer_norm(values):
    centered = values - jnp.mean(values, axis=-1, keepdims=True)
    inverse = lax.rsqrt(jnp.mean(centered * centered, axis=-1, keepdims=True) + epsilon)
    return (centered * inverse, inverse)


def norm_backward(normed, inverse, upstream):
    first_mean = jnp.mean(upstream, axis=-1, keepdims=True)
    second_mean = jnp.mean(upstream * normed, axis=-1, keepdims=True)
    return inverse * (upstream - first_mean - normed * second_mean)


def sigmoid(values):
    return 0.5 * jnp.tanh(0.5 * values) + 0.5


def silu_slope(values):
    sig = sigmoid(values)
    return sig * (1.0 + values * (1.0 - sig))


def iota(shape, dim):
    return lax.broadcasted_iota(jnp.int32, shape, dim)


def dot(left, right):
    return jnp.dot(left, right, preferred_element_type=f32)


def dot_nt(left, right):
    return lax.dot_general(left, right, (((1,), (1,)), ((), ())), preferred_element_type=f32)


def dot_tn(left, right):
    return lax.dot_general(left, right, (((0,), (0,)), ((), ())), preferred_element_type=f32)


def hot(condition):
    return condition.astype(f32).astype(bf16)


def as_column(row):
    length = row.shape[1]
    eye = iota((length, length), 0) == iota((length, length), 1)
    return jnp.sum(jnp.where(eye, jnp.broadcast_to(row, (length, length)), 0.0), axis=1, keepdims=True)


def both_heads(pair):
    low = iota(pair.shape, 1) < DH
    zero = jnp.zeros_like(pair)
    return jnp.concatenate([jnp.where(low, pair, zero), jnp.where(low, zero, pair)], axis=0)


def one_pair(stacked):
    rows = stacked.shape[0] // 2
    low = iota((rows, stacked.shape[1]), 1) < DH
    return jnp.where(low, stacked[:rows], stacked[rows:])


def call(body, outs, *operands, core=None, flops=0, moved=0):
    in_specs = [pl.BlockSpec(memory_space=pltpu.VMEM)] * len(operands)
    if core is not None:
        in_specs = [pl.BlockSpec(memory_space=pltpu.SMEM)] + in_specs
        operands = (core,) + operands
    return pl.pallas_call(
        body,
        out_shape=[jax.ShapeDtypeStruct(shape, kind) for shape, kind in outs],
        in_specs=in_specs,
        compiler_params=pltpu.CompilerParams(vmem_limit_bytes=16 * 1024 * 1024),
        cost_estimate=pl.CostEstimate(flops=flops, bytes_accessed=moved, transcendentals=0),
    )(*operands)


def route_body(table_dev, ids_ref, request_ref, slot_ref):
    owners, capacity = request_ref.shape
    ids = jnp.concatenate([as_column(ids_ref[h : h + 1, :].astype(f32)) for h in range(2)], axis=0)
    ids = ids.astype(jnp.int32)
    count = ids.shape[0]
    shift = table_dev.bit_length() - 1
    owner = jnp.right_shift(ids, shift)
    row = jnp.bitwise_and(ids, table_dev - 1)
    member_f = (owner == iota((count, owners), 1)).astype(f32)
    member = member_f.astype(bf16)
    earlier = hot(iota((count, count), 0) > iota((count, count), 1))
    rank = jnp.sum(dot(earlier, member) * member_f, axis=1, keepdims=True).astype(jnp.int32)
    rank_hot = hot(rank == iota((count, capacity), 1))
    high = (member_f * jnp.right_shift(row, 4).astype(f32)).astype(bf16)
    low = (member_f * jnp.bitwise_and(row, 15).astype(f32)).astype(bf16)
    found = 16.0 * dot_tn(high, rank_hot) + dot_tn(low, rank_hot) + dot_tn(member, rank_hot)
    request_ref[...] = found.astype(jnp.int32) - 1
    slot_ref[...] = owner * capacity + rank


def gather_body(asked_ref, table_ref, found_ref, asked_row_ref):
    asked_rows = asked_ref[...]
    asked_row = jnp.concatenate(
        [asked_rows[g : g + 1, :] for g in range(asked_rows.shape[0])], axis=1
    )
    asked_row_ref[...] = asked_row
    slots = asked_row.shape[1]
    hits = hot(iota((table_ref.shape[0], slots), 0) == asked_row)
    found_ref[...] = dot_tn(hits, table_ref[...]).astype(bf16)


def slot_matrix(slot, slots):
    events = slot.shape[0] // 2
    places = iota((events, slots), 1)
    return hot((slot[:events] == places) | (slot[events:] == places))


def embed_body(slot_ref, fetched_ref, user_ref, inputs_ref, packed_ref):
    rows = inputs_ref.shape[0]
    places = slot_matrix(slot_ref[...], fetched_ref.shape[0])
    inputs = dot(places, fetched_ref[...]).astype(bf16)
    inputs_ref[...] = inputs
    packed_ref[:rows, :] = layer_norm(inputs.astype(f32))[0].astype(bf16)
    packed_ref[rows:, :] = user_rows(user_ref[...], packed_ref.shape[1])


def user_rows(user, width):
    wide = jnp.concatenate([user, jnp.zeros((1, width - user.shape[1]), f32)], axis=1)
    return jnp.broadcast_to(wide, (USER_ROWS, width)).astype(bf16)


def project_body(
    packed_ref, w_in_ref, w_out_ref, grad_ref,
    gates_ref, values_ref, queries_ref, keys_ref, mixed_grad_ref,
):
    rows = grad_ref.shape[0]
    width = grad_ref.shape[1]
    normed = packed_ref[:rows, :]
    for part, out_ref in enumerate((gates_ref, values_ref, queries_ref, keys_ref)):
        columns = slice(part * width, (part + 1) * width)
        projected = dot(normed, w_in_ref[:, columns])
        out_ref[...] = (projected * sigmoid(projected)).astype(bf16)
    mixed_grad_ref[...] = dot_nt(grad_ref[...], w_out_ref[...])


def window_mask(user_row, key_user_row, margin):
    rows = user_row.shape[1]
    columns = key_user_row.shape[1]
    user_column = as_column(user_row)
    allowed = (user_column == key_user_row) & (
        iota((rows, columns), 1) <= iota((rows, columns), 0) + margin
    )
    weight = allowed.astype(f32)
    return jnp.concatenate([weight, weight], axis=0) > 0.0


def forward_body(
    core_ref, four_ref, mate_four_ref, two_ref, mate_two_ref, mate_own_ref, values_ref, keys_ref, queries_ref, gates_ref,
    inputs_ref, mixed_grad_ref, w_in_ref, w_out_ref, user_ref,
    out_ref, mixed_ref, gate_grad_ref, att_grad_ref, all_keys_ref, all_values_ref, key_user_ref,
):
    rows, width = inputs_ref.shape
    score_scale = 1.0 / math.sqrt(DH)
    halos = nearest_last(
        core_ref[0], four_ref[...], mate_four_ref[...], two_ref[...], mate_two_ref[...], mate_own_ref[...]
    )
    far = jnp.concatenate([block[:rows, :] for block in halos], axis=0)
    margin = far.shape[0]
    for part, own_ref, all_ref in ((1, values_ref, all_values_ref), (3, keys_ref, all_keys_ref)):
        projected = dot(far, w_in_ref[:, part * width : (part + 1) * width])
        all_ref[:margin, :] = (projected * sigmoid(projected)).astype(bf16)
        all_ref[margin:, :] = own_ref[...]
    user_row = user_ref[...]
    key_user = jnp.concatenate(
        [block[rows : rows + 1, :rows].astype(f32) for block in halos] + [user_row], axis=1
    )
    key_user_ref[...] = key_user
    allowed = window_mask(user_row, key_user, margin)
    parts = []
    for pair in range(H // 2):
        columns = slice(2 * DH * pair, 2 * DH * (pair + 1))
        scores = dot_nt(both_heads(queries_ref[:, columns]), all_keys_ref[:, columns]) * score_scale
        weights = jnp.where(allowed, scores * sigmoid(scores), 0.0).astype(bf16)
        parts.append(one_pair(dot(weights, all_values_ref[:, columns])))
    att_hat, att_inv = layer_norm(jnp.concatenate(parts, axis=1))
    gates = gates_ref[...].astype(f32)
    mixed = (att_hat * gates).astype(bf16)
    mixed_ref[...] = mixed
    out_ref[...] = (inputs_ref[...].astype(f32) + dot(mixed, w_out_ref[...])).astype(bf16)
    mixed_grad = mixed_grad_ref[...]
    gate_grad_ref[...] = mixed_grad * att_hat
    att_grad_ref[...] = norm_backward(att_hat, att_inv, mixed_grad * gates).astype(bf16)


def core_first(block, rows):
    width = block.shape[1]
    old = iota((width, width), 0)
    new = iota((width, width), 1)
    inner = jnp.bitwise_and(old, rows - 1)
    device = jnp.right_shift(old, rows.bit_length() - 1)
    place = jnp.bitwise_and(device, 1) * (width // 2) + jnp.right_shift(device, 1) * rows + inner
    return dot(block, hot(new == place)).astype(bf16)


def split_by_core(core, terms, first_owner, piece, first_row, stride, kept_ref, sent_ref):
    half = terms.shape[1] // 2
    even = core == 0
    for local_owner in range(terms.shape[0] // piece):
        owner = first_owner + local_owner
        rows = terms[local_owner * piece : (local_owner + 1) * piece]
        place = first_row + (local_owner // X_CHIPS) * stride
        kept_ref[owner % X_CHIPS, place : place + piece, :] = jnp.where(
            even, rows[:, :half], rows[:, half:]
        ).astype(bf16)
        sent_ref[owner % X_CHIPS, place : place + piece, :] = jnp.where(
            even, rows[:, half:], rows[:, :half]
        ).astype(bf16)


def query_body(
    core_ref, queries_ref, all_keys_ref, all_values_ref, att_grad_ref, gate_grad_ref,
    packed_ref, user_ref, key_user_ref,
    four_ref, mate_four_ref, two_ref, mate_two_ref, mate_own_ref, w_in_ref,
    gate_query_ref, value_key_slope_ref, all_queries_ref, query_user_ref,
):
    rows, width = gate_grad_ref.shape
    score_scale = 1.0 / math.sqrt(DH)
    margin = all_keys_ref.shape[0] - rows
    allowed = window_mask(user_ref[...], key_user_ref[...], margin)
    parts = []
    for pair in range(H // 2):
        columns = slice(2 * DH * pair, 2 * DH * (pair + 1))
        keys = all_keys_ref[:, columns]
        scores = dot_nt(both_heads(queries_ref[:, columns]), keys) * score_scale
        prob_grad = dot_nt(both_heads(att_grad_ref[:, columns]), all_values_ref[:, columns])
        score_grad = jnp.where(allowed, prob_grad * silu_slope(scores), 0.0).astype(bf16)
        parts.append(one_pair(dot(score_grad, keys)) * score_scale)
    query_grad = jnp.concatenate(parts, axis=1)
    normed = packed_ref[:rows, :]
    gate_slope, value_slope, query_slope, key_slope = [
        silu_slope(dot(normed, w_in_ref[:, part * width : (part + 1) * width])) for part in range(4)
    ]
    value_key_slope_ref[:, :width] = value_slope
    value_key_slope_ref[:, width:] = key_slope
    gate_part = gate_grad_ref[...] * gate_slope
    query_part = query_grad * query_slope
    gate_query_ref[:, :width] = gate_part.astype(bf16)
    gate_query_ref[:, width:] = query_part.astype(bf16)
    halos = nearest_first(
        core_ref[0], four_ref[...], mate_four_ref[...], two_ref[...], mate_two_ref[...], mate_own_ref[...]
    )
    far = jnp.concatenate([block[:rows, :] for block in halos], axis=0)
    projected = dot(far, w_in_ref[:, 2 * width : 3 * width])
    all_queries_ref[:rows, :] = queries_ref[...]
    all_queries_ref[rows:, :] = (projected * sigmoid(projected)).astype(bf16)
    query_user_ref[...] = jnp.concatenate(
        [as_column(user_ref[...])]
        + [as_column(block[rows : rows + 1, :rows].astype(f32)) for block in halos],
        axis=0,
    )


def key_body(
    core_ref, all_queries_ref, query_user_ref, att_grad_ref,
    four_ref, mate_four_ref, two_ref, mate_two_ref, mate_own_ref,
    keys_ref, values_ref, value_key_slope_ref, gate_query_ref, w_in_ref, inputs_ref, out_grad_ref, slot_ref, user_ref,
    value_key_ref, outgoing_ref,
):
    rows, width = inputs_ref.shape
    score_scale = 1.0 / math.sqrt(DH)
    user_row = user_ref[...]
    query_user = query_user_ref[...]
    halos = nearest_first(
        core_ref[0], four_ref[...], mate_four_ref[...], two_ref[...], mate_two_ref[...], mate_own_ref[...]
    )
    all_grads = jnp.concatenate((att_grad_ref[...],) + halos, axis=0)
    total = query_user.shape[0]
    allowed = (query_user == user_row) & (iota((total, rows), 1) <= iota((total, rows), 0))
    weight = allowed.astype(f32)
    allowed = jnp.concatenate([weight, weight], axis=0) > 0.0
    key_parts = []
    value_parts = []
    for pair in range(H // 2):
        columns = slice(2 * DH * pair, 2 * DH * (pair + 1))
        queries = both_heads(all_queries_ref[:, columns])
        grads = both_heads(all_grads[:, columns])
        scores = dot_nt(queries, keys_ref[:, columns]) * score_scale
        sig = sigmoid(scores)
        raw = scores * sig
        weights = jnp.where(allowed, raw, 0.0).astype(bf16)
        prob_grad = dot_nt(grads, values_ref[:, columns])
        score_grad = jnp.where(allowed, prob_grad * (sig + raw * (1.0 - sig)), 0.0).astype(bf16)
        key_parts.append(dot_tn(score_grad, queries) * score_scale)
        value_parts.append(dot_tn(weights, grads))
    key_grad = jnp.concatenate(key_parts, axis=1)
    value_grad = jnp.concatenate(value_parts, axis=1)
    value_part = (value_grad * value_key_slope_ref[:, :width]).astype(bf16)
    key_part = (key_grad * value_key_slope_ref[:, width:]).astype(bf16)
    value_key_ref[:, :width] = value_part
    value_key_ref[:, width:] = key_part
    joined = jnp.concatenate(
        [gate_query_ref[:, :width], value_part, gate_query_ref[:, width:], key_part], axis=1
    )
    normed_grad = dot_nt(joined, w_in_ref[...])
    input_hat, input_inv = layer_norm(inputs_ref[...].astype(f32))
    inputs_grad = (
        out_grad_ref[...].astype(f32) + norm_backward(input_hat, input_inv, normed_grad)
    ).astype(bf16)
    places = slot_matrix(slot_ref[...], outgoing_ref.shape[0])
    outgoing_ref[...] = dot_tn(places, inputs_grad).astype(bf16)


def early_body(
    piece_in, piece_out, weight_rows,
    core_ref, packed_ref, gate_query_ref, mixed_ref, grad_ref, kept_ref, sent_ref,
):
    rows, width = grad_ref.shape
    core = core_ref[0]
    per_part = width // piece_in
    in_rows = piece_in * per_part // X_CHIPS
    normed = core_first(packed_ref[:rows, :], weight_rows)
    for section, first_owner in ((0, 0), (1, 2 * per_part)):
        terms = dot_tn(gate_query_ref[:, section * width : (section + 1) * width], normed)
        split_by_core(
            core, terms, first_owner, piece_in, section * in_rows, piece_in, kept_ref, sent_ref
        )
    terms = dot_tn(grad_ref[...], core_first(mixed_ref[...], weight_rows))
    split_by_core(core, terms, 0, piece_out, 2 * in_rows, piece_out, kept_ref, sent_ref)


def late_body(
    piece_in, piece_out, weight_rows,
    core_ref, packed_ref, value_key_ref, early_kept_ref, early_sent_ref, kept_ref, sent_ref,
):
    rows = value_key_ref.shape[0]
    width = value_key_ref.shape[1] // 2
    core = core_ref[0]
    piece = piece_in + piece_out
    z_part = width // piece_in // X_CHIPS
    z_chips = kept_ref.shape[1] // piece
    for early_ref, ref in ((early_kept_ref, kept_ref), (early_sent_ref, sent_ref)):
        for z in range(z_chips):
            section, inner = divmod(z, z_part)
            if section % 2 == 0:
                old = (section // 2 * z_part + inner) * piece_in
                ref[:, z * piece : z * piece + piece_in, :] = early_ref[:, old : old + piece_in, :]
            old = 2 * z_part * piece_in + z * piece_out
            ref[:, z * piece + piece_in : (z + 1) * piece, :] = early_ref[:, old : old + piece_out, :]
    normed = core_first(packed_ref[:rows, :], weight_rows)
    for section in range(2):
        terms = dot_tn(value_key_ref[:, section * width : (section + 1) * width], normed)
        split_by_core(
            core, terms, 0, piece_in, (2 * section + 1) * z_part * piece, piece, kept_ref, sent_ref
        )


def table_body(core_ref, asked_ref, arrived_ref, kept_ref, sent_ref):
    slots = asked_ref.shape[1]
    table_dev = kept_ref.shape[2]
    hits = hot(iota((table_dev, slots), 0) == asked_ref[...])
    sums = dot(hits, arrived_ref[...]).T
    rows = kept_ref.shape[1]
    even = core_ref[0] == 0
    for chip in range(kept_ref.shape[0]):
        first = sums[2 * chip * rows : (2 * chip + 1) * rows]
        second = sums[(2 * chip + 1) * rows : (2 * chip + 2) * rows]
        kept_ref[chip] = jnp.where(even, first, second).astype(bf16)
        sent_ref[chip] = jnp.where(even, second, first).astype(bf16)


def sum_pieces(kept, sent, axis, stride):
    devices = range(lax.axis_size(axis))
    count = kept.shape[0]
    me = lax.axis_index(axis) // stride % count
    got = lax.ppermute(sent, "ctx", [(i, i ^ 1) for i in range(lax.axis_size("ctx"))])

    def piece(step):
        at = (me + step) % count
        return lax.dynamic_index_in_dim(kept, at, 0, keepdims=False).astype(
            f32
        ) + lax.dynamic_index_in_dim(got, at, 0, keepdims=False).astype(f32)

    total = piece(0)
    for step in range(1, count):
        route = []
        for i in devices:
            at = i // stride % count
            route.append((i, i + ((at + step) % count - at) * stride))
        total = total + lax.ppermute(piece(step).astype(bf16), axis, route).astype(f32)
    return total


def chips_along_y():
    devices = lax.axis_size("ctx")
    return [list(range(first, devices, 2)) for first in range(2)]


def spread(block, axis, groups):
    return lax.all_to_all(
        block, axis, split_axis=0, concat_axis=0, tiled=True, axis_index_groups=groups
    )


def total_of(blocks):
    return jnp.sum(blocks.astype(f32), axis=0)


def chips_along_z(owners):
    return [list(range(first, owners, X_CHIPS)) for first in range(X_CHIPS)]


def local(item_ids, segments, touched_rows, w_in, w_out, out_grad):
    rows_dev = segments.shape[1]
    model_width = w_in.shape[0]
    table_dev = touched_rows.shape[0]
    owners = lax.axis_size("dp")
    capacity = max(rows_dev // 4, 6 * rows_dev // owners + 2)
    slots = owners * capacity
    core = (lax.axis_index("ctx") % 2).astype(jnp.int32).reshape(1)
    piece_in = w_in.shape[1] // owners
    piece_out = model_width // owners
    block = (rows_dev, model_width)
    packed_block = (rows_dev + USER_ROWS, model_width)
    reach_block = ((REACH + 1) * rows_dev, model_width)
    chips = lax.axis_size("ctx") // 2
    weight_rows = model_width // (2 * chips)

    user = (segments + 1).astype(f32)
    grad_rows = out_grad[0]
    requests, slot = call(
        lambda *refs: route_body(table_dev, *refs),
        [((owners, capacity), jnp.int32), ((2 * rows_dev, 1), jnp.int32)],
        item_ids.reshape(2, rows_dev),
    )
    asked = lax.all_to_all(requests, "dp", split_axis=0, concat_axis=0, tiled=True)
    found, asked_row = call(
        gather_body, [((slots, model_width), bf16), ((1, slots), jnp.int32)], asked, touched_rows
    )
    fetched = lax.all_to_all(
        found.reshape(owners, capacity, model_width), "dp", split_axis=0, concat_axis=0, tiled=True
    ).reshape(slots, model_width)
    inputs, packed = call(
        embed_body, [(block, bf16), (packed_block, bf16)], slot, fetched, user
    )
    earlier_two = passed_along(packed, "ctx", 2)
    gates, values, queries, keys, mixed_grad = call(
        project_body,
        [
            (block, bf16), (block, bf16), (block, bf16), (block, bf16), (block, f32),
        ],
        packed, w_in, w_out, grad_rows,
        flops=1_500_000_000, moved=6_000_000,
    )
    packed_later, mixed_grad = lax.optimization_barrier((packed, mixed_grad))
    mate_own = swapped(packed_later)
    later_two = passed_along(packed_later, "ctx", -2)
    earlier_two, mixed_grad = lax.optimization_barrier((earlier_two, mixed_grad))
    earlier_four = passed_along(earlier_two, "ctx", 2)
    earlier_four, mate_two, mate_own = lax.optimization_barrier(
        (earlier_four, swapped(earlier_two), mate_own)
    )
    mate_four, later_mate_two = lax.optimization_barrier(
        (mate_of_four(earlier_four, 1), swapped(later_two))
    )
    earlier = (earlier_four, mate_four, earlier_two, mate_two, mate_own)
    later_four = passed_along(later_two, "ctx", -2)
    layer_out, mixed, gate_grad, att_grad, all_keys, all_values, key_user = call(
        forward_body,
        [
            (block, bf16), (block, bf16), (block, f32), (block, bf16),
            (reach_block, bf16), (reach_block, bf16), ((1, (REACH + 1) * rows_dev), f32),
        ],
        *earlier, values, keys, queries, gates, inputs, mixed_grad, w_in, w_out, user,
        core=core, flops=4_000_000_000, moved=8_000_000,
    )
    own_grad = swapped(att_grad, (1,))
    grad_two = passed_along(att_grad, "ctx", -2)
    grad_four = passed_along(grad_two, "ctx", -2)
    later_four, own_grad = lax.optimization_barrier((later_four, own_grad))
    later = (later_four, mate_of_four(later_four, -1), later_two, later_mate_two, mate_own)
    grad_mate_two = swapped(grad_two)
    gate_grad, own_grad, grad_mate_two = lax.optimization_barrier((gate_grad, own_grad, grad_mate_two))
    gate_query, value_key_slope, all_queries, query_user = call(
        query_body,
        [
            ((rows_dev, 2 * model_width), bf16), ((rows_dev, 2 * model_width), f32), (reach_block, bf16),
            (((REACH + 1) * rows_dev, 1), f32),
        ],
        queries, all_keys, all_values, att_grad, gate_grad, packed, user, key_user, *later, w_in,
        core=core, flops=4_000_000_000, moved=8_000_000,
    )
    gate_query, mixed, grad_four = lax.optimization_barrier((gate_query, mixed, grad_four))
    later_grads = (
        grad_four, mate_of_four(grad_four, -1), grad_two, grad_mate_two, own_grad,
    )
    half_width = model_width // 2
    early_block = (X_CHIPS, 3 * model_width // X_CHIPS, half_width)
    early_kept, early_sent = call(
        lambda *refs: early_body(piece_in, piece_out, weight_rows, *refs),
        [(early_block, bf16), (early_block, bf16)],
        packed, gate_query, mixed, grad_rows,
        core=core, flops=2_000_000_000, moved=4_000_000,
    )
    gate_query, early_kept, early_sent = lax.optimization_barrier(
        (gate_query, early_kept, early_sent)
    )
    value_key, outgoing = call(
        key_body,
        [((rows_dev, 2 * model_width), bf16), ((slots, model_width), bf16)],
        all_queries, query_user, att_grad, *later_grads, keys, values, value_key_slope, gate_query,
        w_in, inputs, grad_rows, slot, user,
        core=core, flops=4_000_000_000, moved=8_000_000,
    )
    arrived = lax.all_to_all(
        outgoing.reshape(owners, capacity, model_width), "dp", split_axis=0, concat_axis=0, tiled=True
    ).reshape(slots, model_width)
    piece = piece_in + piece_out
    z_chips = owners // X_CHIPS
    weight_block = (X_CHIPS, z_chips * piece, half_width)
    weight_kept, weight_sent = call(
        lambda *refs: late_body(piece_in, piece_out, weight_rows, *refs),
        [(weight_block, bf16), (weight_block, bf16)],
        packed, value_key, early_kept, early_sent,
        core=core, flops=1_500_000_000, moved=3_000_000,
    )
    along_x = sum_pieces(weight_kept, weight_sent, "dp", 1).astype(bf16)
    along_x = along_x.reshape(z_chips, piece, half_width)
    arrived, along_x = lax.optimization_barrier((arrived, along_x))
    along_dp = total_of(spread(along_x, "dp", chips_along_z(owners))).astype(bf16)
    weight_terms = along_dp.T.reshape(chips, weight_rows, piece)
    table_block = (chips, model_width // (2 * chips), table_dev)
    table_kept, table_sent = call(
        table_body, [(table_block, bf16), (table_block, bf16)], asked_row, arrived, core=core
    )
    table_grad = sum_pieces(table_kept, table_sent, "ctx", 2).T
    weight_grad = total_of(spread(weight_terms, "ctx", chips_along_y()))
    w_in_grad = weight_grad[:, :piece_in]
    w_out_grad = weight_grad[:, piece_in:]
    return (layer_out[None], table_grad, w_in_grad, w_out_grad)


def solution(mesh):
    return jax.shard_map(
        local,
        mesh=mesh,
        in_specs=(
            P(None, "dp", "ctx"),
            P("dp", "ctx"),
            P("dp", None),
            P(),
            P(),
            P("dp", "ctx", None),
        ),
        out_specs=(P("dp", "ctx", None), P("dp", "ctx"), P("ctx", "dp"), P("ctx", "dp")),
        check_vma=False,
    )
```

```python
import math

import jax
import jax.numpy as jnp
from jax import lax
from jax.experimental import pallas as pl
from jax.experimental.pallas import tpu as pltpu
from jax.sharding import PartitionSpec as P

H = 8
DH = 64
REACH = 4
USER_ROWS = 16

epsilon = 1e-05
f32 = jnp.float32
bf16 = jnp.bfloat16


def passed_along(block, axis, distance):
    devices = range(lax.axis_size(axis))
    route = [(i - distance, i) for i in devices if i - distance in devices]
    return lax.ppermute(block, axis, route)


def swapped(block, senders=(0, 1)):
    devices = range(lax.axis_size("ctx"))
    return lax.ppermute(block, "ctx", [(i, i ^ 1) for i in devices if i % 2 in senders])


def mate_of_four(four, direction):
    return swapped(four, (1,) if direction > 0 else (0,))


def nearest_last(core, four, mate_four, two, mate_two, mate_own):
    even = core == 0
    return (
        four,
        jnp.where(even, mate_four, mate_two),
        two,
        jnp.where(even, mate_two, mate_own),
    )


def nearest_first(core, four, mate_four, two, mate_two, mate_own):
    even = core == 0
    return (
        jnp.where(even, mate_own, mate_two),
        two,
        jnp.where(even, mate_two, mate_four),
        four,
    )


def layer_norm(values):
    centered = values - jnp.mean(values, axis=-1, keepdims=True)
    inverse = lax.rsqrt(jnp.mean(centered * centered, axis=-1, keepdims=True) + epsilon)
    return (centered * inverse, inverse)


def norm_backward(normed, inverse, upstream):
    first_mean = jnp.mean(upstream, axis=-1, keepdims=True)
    second_mean = jnp.mean(upstream * normed, axis=-1, keepdims=True)
    return inverse * (upstream - first_mean - normed * second_mean)


def sigmoid(values):
    return 0.5 * jnp.tanh(0.5 * values) + 0.5


def silu_slope(values):
    sig = sigmoid(values)
    return sig * (1.0 + values * (1.0 - sig))


def iota(shape, dim):
    return lax.broadcasted_iota(jnp.int32, shape, dim)


def dot(left, right):
    return jnp.dot(left, right, preferred_element_type=f32)


def dot_nt(left, right):
    return lax.dot_general(left, right, (((1,), (1,)), ((), ())), preferred_element_type=f32)


def dot_tn(left, right):
    return lax.dot_general(left, right, (((0,), (0,)), ((), ())), preferred_element_type=f32)


def hot(condition):
    return condition.astype(f32).astype(bf16)


def as_column(row):
    length = row.shape[1]
    eye = iota((length, length), 0) == iota((length, length), 1)
    return jnp.sum(jnp.where(eye, jnp.broadcast_to(row, (length, length)), 0.0), axis=1, keepdims=True)


def both_heads(pair):
    low = iota(pair.shape, 1) < DH
    zero = jnp.zeros_like(pair)
    return jnp.concatenate([jnp.where(low, pair, zero), jnp.where(low, zero, pair)], axis=0)


def one_pair(stacked):
    rows = stacked.shape[0] // 2
    low = iota((rows, stacked.shape[1]), 1) < DH
    return jnp.where(low, stacked[:rows], stacked[rows:])


def call(body, outs, *operands, core=None, flops=0, moved=0):
    in_specs = [pl.BlockSpec(memory_space=pltpu.VMEM)] * len(operands)
    if core is not None:
        in_specs = [pl.BlockSpec(memory_space=pltpu.SMEM)] + in_specs
        operands = (core,) + operands
    return pl.pallas_call(
        body,
        out_shape=[jax.ShapeDtypeStruct(shape, kind) for shape, kind in outs],
        in_specs=in_specs,
        compiler_params=pltpu.CompilerParams(vmem_limit_bytes=16 * 1024 * 1024),
        cost_estimate=pl.CostEstimate(flops=flops, bytes_accessed=moved, transcendentals=0),
    )(*operands)


def route_body(table_dev, ids_ref, request_ref, slot_ref):
    owners, capacity = request_ref.shape
    ids = jnp.concatenate([as_column(ids_ref[h : h + 1, :].astype(f32)) for h in range(2)], axis=0)
    ids = ids.astype(jnp.int32)
    count = ids.shape[0]
    shift = table_dev.bit_length() - 1
    owner = jnp.right_shift(ids, shift)
    row = jnp.bitwise_and(ids, table_dev - 1)
    member_f = (owner == iota((count, owners), 1)).astype(f32)
    member = member_f.astype(bf16)
    earlier = hot(iota((count, count), 0) > iota((count, count), 1))
    rank = jnp.sum(dot(earlier, member) * member_f, axis=1, keepdims=True).astype(jnp.int32)
    rank_hot = hot(rank == iota((count, capacity), 1))
    high = (member_f * jnp.right_shift(row, 4).astype(f32)).astype(bf16)
    low = (member_f * jnp.bitwise_and(row, 15).astype(f32)).astype(bf16)
    found = 16.0 * dot_tn(high, rank_hot) + dot_tn(low, rank_hot) + dot_tn(member, rank_hot)
    request_ref[...] = found.astype(jnp.int32) - 1
    slot_ref[...] = owner * capacity + rank


def gather_body(asked_ref, table_ref, found_ref, asked_row_ref):
    asked_rows = asked_ref[...]
    asked_row = jnp.concatenate(
        [asked_rows[g : g + 1, :] for g in range(asked_rows.shape[0])], axis=1
    )
    asked_row_ref[...] = asked_row
    slots = asked_row.shape[1]
    hits = hot(iota((table_ref.shape[0], slots), 0) == asked_row)
    found_ref[...] = dot_tn(hits, table_ref[...]).astype(bf16)


def slot_matrix(slot, slots):
    events = slot.shape[0] // 2
    places = iota((events, slots), 1)
    return hot((slot[:events] == places) | (slot[events:] == places))


def embed_body(slot_ref, fetched_ref, user_ref, inputs_ref, packed_ref):
    rows = inputs_ref.shape[0]
    places = slot_matrix(slot_ref[...], fetched_ref.shape[0])
    inputs = dot(places, fetched_ref[...]).astype(bf16)
    inputs_ref[...] = inputs
    packed_ref[:rows, :] = layer_norm(inputs.astype(f32))[0].astype(bf16)
    packed_ref[rows:, :] = user_rows(user_ref[...], packed_ref.shape[1])


def user_rows(user, width):
    wide = jnp.concatenate([user, jnp.zeros((1, width - user.shape[1]), f32)], axis=1)
    return jnp.broadcast_to(wide, (USER_ROWS, width)).astype(bf16)


def project_body(
    packed_ref, w_in_ref, w_out_ref, grad_ref,
    gates_ref, values_ref, queries_ref, keys_ref, mixed_grad_ref,
):
    rows = grad_ref.shape[0]
    width = grad_ref.shape[1]
    normed = packed_ref[:rows, :]
    for part, out_ref in enumerate((gates_ref, values_ref, queries_ref, keys_ref)):
        columns = slice(part * width, (part + 1) * width)
        projected = dot(normed, w_in_ref[:, columns])
        out_ref[...] = (projected * sigmoid(projected)).astype(bf16)
    mixed_grad_ref[...] = dot_nt(grad_ref[...], w_out_ref[...])


def window_mask(user_row, key_user_row, margin):
    rows = user_row.shape[1]
    columns = key_user_row.shape[1]
    user_column = as_column(user_row)
    allowed = (user_column == key_user_row) & (
        iota((rows, columns), 1) <= iota((rows, columns), 0) + margin
    )
    weight = allowed.astype(f32)
    return jnp.concatenate([weight, weight], axis=0) > 0.0


def forward_body(
    core_ref, four_ref, mate_four_ref, two_ref, mate_two_ref, mate_own_ref, values_ref, keys_ref, queries_ref, gates_ref,
    inputs_ref, mixed_grad_ref, w_in_ref, w_out_ref, user_ref,
    out_ref, mixed_ref, gate_grad_ref, att_grad_ref, all_keys_ref, all_values_ref, key_user_ref,
):
    rows, width = inputs_ref.shape
    score_scale = 1.0 / math.sqrt(DH)
    halos = nearest_last(
        core_ref[0], four_ref[...], mate_four_ref[...], two_ref[...], mate_two_ref[...], mate_own_ref[...]
    )
    far = jnp.concatenate([block[:rows, :] for block in halos], axis=0)
    margin = far.shape[0]
    for part, own_ref, all_ref in ((1, values_ref, all_values_ref), (3, keys_ref, all_keys_ref)):
        projected = dot(far, w_in_ref[:, part * width : (part + 1) * width])
        all_ref[:margin, :] = (projected * sigmoid(projected)).astype(bf16)
        all_ref[margin:, :] = own_ref[...]
    user_row = user_ref[...]
    key_user = jnp.concatenate(
        [block[rows : rows + 1, :rows].astype(f32) for block in halos] + [user_row], axis=1
    )
    key_user_ref[...] = key_user
    allowed = window_mask(user_row, key_user, margin)
    parts = []
    for pair in range(H // 2):
        columns = slice(2 * DH * pair, 2 * DH * (pair + 1))
        scores = dot_nt(both_heads(queries_ref[:, columns]), all_keys_ref[:, columns]) * score_scale
        weights = jnp.where(allowed, scores * sigmoid(scores), 0.0).astype(bf16)
        parts.append(one_pair(dot(weights, all_values_ref[:, columns])))
    att_hat, att_inv = layer_norm(jnp.concatenate(parts, axis=1))
    gates = gates_ref[...].astype(f32)
    mixed = (att_hat * gates).astype(bf16)
    mixed_ref[...] = mixed
    out_ref[...] = (inputs_ref[...].astype(f32) + dot(mixed, w_out_ref[...])).astype(bf16)
    mixed_grad = mixed_grad_ref[...]
    gate_grad_ref[...] = mixed_grad * att_hat
    att_grad_ref[...] = norm_backward(att_hat, att_inv, mixed_grad * gates).astype(bf16)


def split_by_core(core, terms, first_column, kept_ref, sent_ref):
    chips = 8
    rows = terms.shape[0] // (2 * chips)
    columns = slice(first_column, first_column + terms.shape[1])
    even = core == 0
    for chip in range(chips):
        first = terms[2 * chip * rows : (2 * chip + 1) * rows]
        second = terms[(2 * chip + 1) * rows : (2 * chip + 2) * rows]
        kept_ref[chip * rows : (chip + 1) * rows, columns] = jnp.where(even, first, second).astype(bf16)
        sent_ref[chip * rows : (chip + 1) * rows, columns] = jnp.where(even, second, first).astype(bf16)


def query_body(
    core_ref, queries_ref, all_keys_ref, all_values_ref, att_grad_ref, gate_grad_ref,
    packed_ref, user_ref, key_user_ref,
    four_ref, mate_four_ref, two_ref, mate_two_ref, mate_own_ref, w_in_ref,
    gate_query_ref, value_key_slope_ref, all_queries_ref, query_user_ref,
):
    rows, width = gate_grad_ref.shape
    score_scale = 1.0 / math.sqrt(DH)
    margin = all_keys_ref.shape[0] - rows
    allowed = window_mask(user_ref[...], key_user_ref[...], margin)
    parts = []
    for pair in range(H // 2):
        columns = slice(2 * DH * pair, 2 * DH * (pair + 1))
        keys = all_keys_ref[:, columns]
        scores = dot_nt(both_heads(queries_ref[:, columns]), keys) * score_scale
        prob_grad = dot_nt(both_heads(att_grad_ref[:, columns]), all_values_ref[:, columns])
        score_grad = jnp.where(allowed, prob_grad * silu_slope(scores), 0.0).astype(bf16)
        parts.append(one_pair(dot(score_grad, keys)) * score_scale)
    query_grad = jnp.concatenate(parts, axis=1)
    normed = packed_ref[:rows, :]
    gate_slope, value_slope, query_slope, key_slope = [
        silu_slope(dot(normed, w_in_ref[:, part * width : (part + 1) * width])) for part in range(4)
    ]
    value_key_slope_ref[:, :width] = value_slope
    value_key_slope_ref[:, width:] = key_slope
    gate_part = gate_grad_ref[...] * gate_slope
    query_part = query_grad * query_slope
    gate_query_ref[:, :width] = gate_part.astype(bf16)
    gate_query_ref[:, width:] = query_part.astype(bf16)
    halos = nearest_first(
        core_ref[0], four_ref[...], mate_four_ref[...], two_ref[...], mate_two_ref[...], mate_own_ref[...]
    )
    far = jnp.concatenate([block[:rows, :] for block in halos], axis=0)
    projected = dot(far, w_in_ref[:, 2 * width : 3 * width])
    all_queries_ref[:rows, :] = queries_ref[...]
    all_queries_ref[rows:, :] = (projected * sigmoid(projected)).astype(bf16)
    query_user_ref[...] = jnp.concatenate(
        [as_column(user_ref[...])]
        + [as_column(block[rows : rows + 1, :rows].astype(f32)) for block in halos],
        axis=0,
    )


def key_body(
    core_ref, all_queries_ref, query_user_ref, att_grad_ref,
    four_ref, mate_four_ref, two_ref, mate_two_ref, mate_own_ref,
    keys_ref, values_ref, value_key_slope_ref, gate_query_ref, w_in_ref, inputs_ref, out_grad_ref, slot_ref, user_ref,
    value_key_ref, outgoing_ref,
):
    rows, width = inputs_ref.shape
    score_scale = 1.0 / math.sqrt(DH)
    user_row = user_ref[...]
    query_user = query_user_ref[...]
    halos = nearest_first(
        core_ref[0], four_ref[...], mate_four_ref[...], two_ref[...], mate_two_ref[...], mate_own_ref[...]
    )
    all_grads = jnp.concatenate((att_grad_ref[...],) + halos, axis=0)
    total = query_user.shape[0]
    allowed = (query_user == user_row) & (iota((total, rows), 1) <= iota((total, rows), 0))
    weight = allowed.astype(f32)
    allowed = jnp.concatenate([weight, weight], axis=0) > 0.0
    key_parts = []
    value_parts = []
    for pair in range(H // 2):
        columns = slice(2 * DH * pair, 2 * DH * (pair + 1))
        queries = both_heads(all_queries_ref[:, columns])
        grads = both_heads(all_grads[:, columns])
        scores = dot_nt(queries, keys_ref[:, columns]) * score_scale
        sig = sigmoid(scores)
        raw = scores * sig
        weights = jnp.where(allowed, raw, 0.0).astype(bf16)
        prob_grad = dot_nt(grads, values_ref[:, columns])
        score_grad = jnp.where(allowed, prob_grad * (sig + raw * (1.0 - sig)), 0.0).astype(bf16)
        key_parts.append(dot_tn(score_grad, queries) * score_scale)
        value_parts.append(dot_tn(weights, grads))
    key_grad = jnp.concatenate(key_parts, axis=1)
    value_grad = jnp.concatenate(value_parts, axis=1)
    value_part = (value_grad * value_key_slope_ref[:, :width]).astype(bf16)
    key_part = (key_grad * value_key_slope_ref[:, width:]).astype(bf16)
    value_key_ref[:, :width] = value_part
    value_key_ref[:, width:] = key_part
    joined = jnp.concatenate(
        [gate_query_ref[:, :width], value_part, gate_query_ref[:, width:], key_part], axis=1
    )
    normed_grad = dot_nt(joined, w_in_ref[...])
    input_hat, input_inv = layer_norm(inputs_ref[...].astype(f32))
    inputs_grad = (
        out_grad_ref[...].astype(f32) + norm_backward(input_hat, input_inv, normed_grad)
    ).astype(bf16)
    places = slot_matrix(slot_ref[...], outgoing_ref.shape[0])
    outgoing_ref[...] = dot_tn(places, inputs_grad).astype(bf16)


def early_body(core_ref, packed_ref, gate_query_ref, mixed_ref, grad_ref, kept_ref, sent_ref):
    rows, width = grad_ref.shape
    core = core_ref[0]
    normed = packed_ref[:rows, :]
    for section in range(2):
        part = gate_query_ref[:, section * width : (section + 1) * width]
        split_by_core(core, dot_tn(normed, part), section * width, kept_ref, sent_ref)
    split_by_core(core, dot_tn(mixed_ref[...], grad_ref[...]), 2 * width, kept_ref, sent_ref)


def late_body(core_ref, packed_ref, value_key_ref, early_kept_ref, early_sent_ref, kept_ref, sent_ref):
    rows = value_key_ref.shape[0]
    width = value_key_ref.shape[1] // 2
    core = core_ref[0]
    for early_ref, ref in ((early_kept_ref, kept_ref), (early_sent_ref, sent_ref)):
        for section in range(3):
            ref[:, 2 * section * width : (2 * section + 1) * width] = early_ref[
                :, section * width : (section + 1) * width
            ]
    normed = packed_ref[:rows, :]
    for section in range(2):
        part = value_key_ref[:, section * width : (section + 1) * width]
        split_by_core(core, dot_tn(normed, part), (2 * section + 1) * width, kept_ref, sent_ref)


def owners_body(piece_in, piece_out, share_ref, send_ref):
    owners, rows, lanes = send_ref.shape
    share = share_ref[...].astype(f32)
    blank = jnp.zeros((rows, lanes - piece_in - piece_out), f32)
    start = owners * piece_in
    for owner in range(owners):
        wide = share[:, owner * piece_in : (owner + 1) * piece_in]
        thin = share[:, start + owner * piece_out : start + (owner + 1) * piece_out]
        send_ref[owner] = jnp.concatenate([wide, thin, blank], axis=1).astype(bf16)


def table_body(core_ref, asked_ref, arrived_ref, kept_ref, sent_ref):
    slots = asked_ref.shape[1]
    table_dev = kept_ref.shape[2]
    hits = hot(iota((table_dev, slots), 0) == asked_ref[...])
    sums = dot(hits, arrived_ref[...]).T
    rows = kept_ref.shape[1]
    even = core_ref[0] == 0
    for chip in range(kept_ref.shape[0]):
        first = sums[2 * chip * rows : (2 * chip + 1) * rows]
        second = sums[(2 * chip + 1) * rows : (2 * chip + 2) * rows]
        kept_ref[chip] = jnp.where(even, first, second).astype(bf16)
        sent_ref[chip] = jnp.where(even, second, first).astype(bf16)


def pair_sum(kept, sent):
    devices = lax.axis_size("ctx")
    got = lax.ppermute(sent, "ctx", [(i, i ^ 1) for i in range(devices)])
    return (kept.astype(f32) + got.astype(f32)).astype(bf16)


def chips_along_y():
    devices = lax.axis_size("ctx")
    return [list(range(first, devices, 2)) for first in range(2)]


def spread(block, axis, groups):
    return lax.all_to_all(
        block, axis, split_axis=0, concat_axis=0, tiled=True, axis_index_groups=groups
    )


def total_of(blocks):
    return jnp.sum(blocks.astype(f32), axis=0)


def local(item_ids, segments, touched_rows, w_in, w_out, out_grad):
    rows_dev = segments.shape[1]
    model_width = w_in.shape[0]
    table_dev = touched_rows.shape[0]
    owners = lax.axis_size("dp")
    capacity = max(rows_dev // 4, 6 * rows_dev // owners + 2)
    slots = owners * capacity
    core = (lax.axis_index("ctx") % 2).astype(jnp.int32).reshape(1)
    piece_in = w_in.shape[1] // owners
    piece_out = model_width // owners
    block = (rows_dev, model_width)
    packed_block = (rows_dev + USER_ROWS, model_width)
    reach_block = ((REACH + 1) * rows_dev, model_width)
    chips = lax.axis_size("ctx") // 2
    weight_rows = model_width // (2 * chips)

    user = (segments + 1).astype(f32)
    grad_rows = out_grad[0]
    requests, slot = call(
        lambda *refs: route_body(table_dev, *refs),
        [((owners, capacity), jnp.int32), ((2 * rows_dev, 1), jnp.int32)],
        item_ids.reshape(2, rows_dev),
    )
    asked = lax.all_to_all(requests, "dp", split_axis=0, concat_axis=0, tiled=True)
    found, asked_row = call(
        gather_body, [((slots, model_width), bf16), ((1, slots), jnp.int32)], asked, touched_rows
    )
    fetched = lax.all_to_all(
        found.reshape(owners, capacity, model_width), "dp", split_axis=0, concat_axis=0, tiled=True
    ).reshape(slots, model_width)
    inputs, packed = call(
        embed_body, [(block, bf16), (packed_block, bf16)], slot, fetched, user
    )
    earlier_two = passed_along(packed, "ctx", 2)
    gates, values, queries, keys, mixed_grad = call(
        project_body,
        [
            (block, bf16), (block, bf16), (block, bf16), (block, bf16), (block, f32),
        ],
        packed, w_in, w_out, grad_rows,
        flops=1_500_000_000, moved=6_000_000,
    )
    packed_later, mixed_grad = lax.optimization_barrier((packed, mixed_grad))
    mate_own = swapped(packed_later)
    later_two = passed_along(packed_later, "ctx", -2)
    earlier_two, mixed_grad = lax.optimization_barrier((earlier_two, mixed_grad))
    earlier_four = passed_along(earlier_two, "ctx", 2)
    earlier_four, mate_two, mate_own = lax.optimization_barrier(
        (earlier_four, swapped(earlier_two), mate_own)
    )
    mate_four, later_mate_two = lax.optimization_barrier(
        (mate_of_four(earlier_four, 1), swapped(later_two))
    )
    earlier = (earlier_four, mate_four, earlier_two, mate_two, mate_own)
    later_four = passed_along(later_two, "ctx", -2)
    layer_out, mixed, gate_grad, att_grad, all_keys, all_values, key_user = call(
        forward_body,
        [
            (block, bf16), (block, bf16), (block, f32), (block, bf16),
            (reach_block, bf16), (reach_block, bf16), ((1, (REACH + 1) * rows_dev), f32),
        ],
        *earlier, values, keys, queries, gates, inputs, mixed_grad, w_in, w_out, user,
        core=core, flops=4_000_000_000, moved=8_000_000,
    )
    own_grad = swapped(att_grad, (1,))
    grad_two = passed_along(att_grad, "ctx", -2)
    grad_four = passed_along(grad_two, "ctx", -2)
    later_four, own_grad = lax.optimization_barrier((later_four, own_grad))
    later = (later_four, mate_of_four(later_four, -1), later_two, later_mate_two, mate_own)
    grad_mate_two = swapped(grad_two)
    gate_grad, own_grad, grad_mate_two = lax.optimization_barrier((gate_grad, own_grad, grad_mate_two))
    gate_query, value_key_slope, all_queries, query_user = call(
        query_body,
        [
            ((rows_dev, 2 * model_width), bf16), ((rows_dev, 2 * model_width), f32), (reach_block, bf16),
            (((REACH + 1) * rows_dev, 1), f32),
        ],
        queries, all_keys, all_values, att_grad, gate_grad, packed, user, key_user, *later, w_in,
        core=core, flops=4_000_000_000, moved=8_000_000,
    )
    gate_query, mixed, grad_four = lax.optimization_barrier((gate_query, mixed, grad_four))
    later_grads = (
        grad_four, mate_of_four(grad_four, -1), grad_two, grad_mate_two, own_grad,
    )
    half_width = model_width // 2
    early_block = (half_width, 3 * model_width)
    early_kept, early_sent = call(
        early_body,
        [(early_block, bf16), (early_block, bf16)],
        packed, gate_query, mixed, grad_rows,
        core=core, flops=2_000_000_000, moved=4_000_000,
    )
    gate_query, early_kept, early_sent = lax.optimization_barrier(
        (gate_query, early_kept, early_sent)
    )
    value_key, outgoing = call(
        key_body,
        [((rows_dev, 2 * model_width), bf16), ((slots, model_width), bf16)],
        all_queries, query_user, att_grad, *later_grads, keys, values, value_key_slope, gate_query,
        w_in, inputs, grad_rows, slot, user,
        core=core, flops=4_000_000_000, moved=8_000_000,
    )
    arrived = lax.all_to_all(
        outgoing.reshape(owners, capacity, model_width), "dp", split_axis=0, concat_axis=0, tiled=True
    ).reshape(slots, model_width)
    weight_block = (half_width, 5 * model_width)
    weight_kept, weight_sent = call(
        late_body,
        [(weight_block, bf16), (weight_block, bf16)],
        packed, value_key, early_kept, early_sent,
        core=core, flops=1_500_000_000, moved=3_000_000,
    )
    share = lax.psum_scatter(
        pair_sum(weight_kept, weight_sent), "ctx", scatter_dimension=0, tiled=True,
        axis_index_groups=chips_along_y(),
    )
    (weight_send,) = call(
        lambda *refs: owners_body(piece_in, piece_out, *refs),
        [((owners, weight_rows, 128), bf16)], share,
    )
    table_block = (chips, model_width // (2 * chips), table_dev)
    table_kept, table_sent = call(
        table_body, [(table_block, bf16), (table_block, bf16)], asked_row, arrived, core=core
    )
    table_sum = pair_sum(table_kept, table_sent)
    table_spread = spread(table_sum, "ctx", chips_along_y())
    table_spread, weight_send = lax.optimization_barrier((table_spread, weight_send))
    table_grad = total_of(table_spread).T
    weight_grad = total_of(spread(weight_send, "dp", None))
    w_in_grad = weight_grad[:, :piece_in]
    w_out_grad = weight_grad[:, piece_in : piece_in + piece_out]
    return (layer_out[None], table_grad, w_in_grad, w_out_grad)


def solution(mesh):
    return jax.shard_map(
        local,
        mesh=mesh,
        in_specs=(
            P(None, "dp", "ctx"),
            P("dp", "ctx"),
            P("dp", None),
            P(),
            P(),
            P("dp", "ctx", None),
        ),
        out_specs=(P("dp", "ctx", None), P("dp", "ctx"), P("ctx", "dp"), P("ctx", "dp")),
        check_vma=False,
    )
```

```python
import math

import jax
import jax.numpy as jnp
from jax import lax
from jax.experimental import pallas as pl
from jax.experimental.pallas import tpu as pltpu
from jax.sharding import PartitionSpec as P

H = 8
DH = 64
X_CHIPS = 4
REACH = 4
USER_ROWS = 16

epsilon = 1e-05
f32 = jnp.float32
bf16 = jnp.bfloat16


def passed_along(block, axis, distance):
    devices = range(lax.axis_size(axis))
    route = [(i - distance, i) for i in devices if i - distance in devices]
    return lax.ppermute(block, axis, route)


def swapped(block, senders=(0, 1)):
    devices = range(lax.axis_size("ctx"))
    return lax.ppermute(block, "ctx", [(i, i ^ 1) for i in devices if i % 2 in senders])


def mate_of_four(four, direction):
    return swapped(four, (1,) if direction > 0 else (0,))


def nearest_last(core, four, mate_four, two, mate_two, mate_own):
    even = core == 0
    return (
        four,
        jnp.where(even, mate_four, mate_two),
        two,
        jnp.where(even, mate_two, mate_own),
    )


def nearest_first(core, four, mate_four, two, mate_two, mate_own):
    even = core == 0
    return (
        jnp.where(even, mate_own, mate_two),
        two,
        jnp.where(even, mate_two, mate_four),
        four,
    )


def layer_norm(values):
    centered = values - jnp.mean(values, axis=-1, keepdims=True)
    inverse = lax.rsqrt(jnp.mean(centered * centered, axis=-1, keepdims=True) + epsilon)
    return (centered * inverse, inverse)


def norm_backward(normed, inverse, upstream):
    first_mean = jnp.mean(upstream, axis=-1, keepdims=True)
    second_mean = jnp.mean(upstream * normed, axis=-1, keepdims=True)
    return inverse * (upstream - first_mean - normed * second_mean)


def sigmoid(values):
    return 0.5 * jnp.tanh(0.5 * values) + 0.5


def silu_slope(values):
    sig = sigmoid(values)
    return sig * (1.0 + values * (1.0 - sig))


def iota(shape, dim):
    return lax.broadcasted_iota(jnp.int32, shape, dim)


def dot(left, right):
    return jnp.dot(left, right, preferred_element_type=f32)


def dot_nt(left, right):
    return lax.dot_general(left, right, (((1,), (1,)), ((), ())), preferred_element_type=f32)


def dot_tn(left, right):
    return lax.dot_general(left, right, (((0,), (0,)), ((), ())), preferred_element_type=f32)


def hot(condition):
    return condition.astype(f32).astype(bf16)


def as_column(row):
    length = row.shape[1]
    eye = iota((length, length), 0) == iota((length, length), 1)
    return jnp.sum(jnp.where(eye, jnp.broadcast_to(row, (length, length)), 0.0), axis=1, keepdims=True)


def both_heads(pair):
    low = iota(pair.shape, 1) < DH
    zero = jnp.zeros_like(pair)
    return jnp.concatenate([jnp.where(low, pair, zero), jnp.where(low, zero, pair)], axis=0)


def one_pair(stacked):
    rows = stacked.shape[0] // 2
    low = iota((rows, stacked.shape[1]), 1) < DH
    return jnp.where(low, stacked[:rows], stacked[rows:])


def call(body, outs, *operands, core=None, flops=0, moved=0):
    in_specs = [pl.BlockSpec(memory_space=pltpu.VMEM)] * len(operands)
    if core is not None:
        in_specs = [pl.BlockSpec(memory_space=pltpu.SMEM)] + in_specs
        operands = (core,) + operands
    return pl.pallas_call(
        body,
        out_shape=[jax.ShapeDtypeStruct(shape, kind) for shape, kind in outs],
        in_specs=in_specs,
        compiler_params=pltpu.CompilerParams(vmem_limit_bytes=16 * 1024 * 1024),
        cost_estimate=pl.CostEstimate(flops=flops, bytes_accessed=moved, transcendentals=0),
    )(*operands)


def route_body(table_dev, ids_ref, request_ref, slot_ref):
    owners, capacity = request_ref.shape
    ids = jnp.concatenate([as_column(ids_ref[h : h + 1, :].astype(f32)) for h in range(2)], axis=0)
    ids = ids.astype(jnp.int32)
    count = ids.shape[0]
    shift = table_dev.bit_length() - 1
    owner = jnp.right_shift(ids, shift)
    row = jnp.bitwise_and(ids, table_dev - 1)
    member_f = (owner == iota((count, owners), 1)).astype(f32)
    member = member_f.astype(bf16)
    earlier = hot(iota((count, count), 0) > iota((count, count), 1))
    rank = jnp.sum(dot(earlier, member) * member_f, axis=1, keepdims=True).astype(jnp.int32)
    rank_hot = hot(rank == iota((count, capacity), 1))
    high = (member_f * jnp.right_shift(row, 4).astype(f32)).astype(bf16)
    low = (member_f * jnp.bitwise_and(row, 15).astype(f32)).astype(bf16)
    found = 16.0 * dot_tn(high, rank_hot) + dot_tn(low, rank_hot) + dot_tn(member, rank_hot)
    request_ref[...] = found.astype(jnp.int32) - 1
    slot_ref[...] = owner * capacity + rank


def gather_body(asked_ref, table_ref, found_ref, asked_row_ref):
    asked_rows = asked_ref[...]
    asked_row = jnp.concatenate(
        [asked_rows[g : g + 1, :] for g in range(asked_rows.shape[0])], axis=1
    )
    asked_row_ref[...] = asked_row
    slots = asked_row.shape[1]
    hits = hot(iota((table_ref.shape[0], slots), 0) == asked_row)
    found_ref[...] = dot_tn(hits, table_ref[...]).astype(bf16)


def slot_matrix(slot, slots):
    events = slot.shape[0] // 2
    places = iota((events, slots), 1)
    return hot((slot[:events] == places) | (slot[events:] == places))


def embed_body(slot_ref, fetched_ref, user_ref, inputs_ref, packed_ref):
    rows = inputs_ref.shape[0]
    places = slot_matrix(slot_ref[...], fetched_ref.shape[0])
    inputs = dot(places, fetched_ref[...]).astype(bf16)
    inputs_ref[...] = inputs
    packed_ref[:rows, :] = layer_norm(inputs.astype(f32))[0].astype(bf16)
    packed_ref[rows:, :] = user_rows(user_ref[...], packed_ref.shape[1])


def user_rows(user, width):
    wide = jnp.concatenate([user, jnp.zeros((1, width - user.shape[1]), f32)], axis=1)
    return jnp.broadcast_to(wide, (USER_ROWS, width)).astype(bf16)


def project_body(
    packed_ref, w_in_ref, w_out_ref, grad_ref,
    gates_ref, values_ref, queries_ref, keys_ref, mixed_grad_ref,
):
    rows = grad_ref.shape[0]
    width = grad_ref.shape[1]
    normed = packed_ref[:rows, :]
    for part, out_ref in enumerate((gates_ref, values_ref, queries_ref, keys_ref)):
        columns = slice(part * width, (part + 1) * width)
        projected = dot(normed, w_in_ref[:, columns])
        out_ref[...] = (projected * sigmoid(projected)).astype(bf16)
    mixed_grad_ref[...] = dot_nt(grad_ref[...], w_out_ref[...])


def window_mask(user_row, key_user_row, margin):
    rows = user_row.shape[1]
    columns = key_user_row.shape[1]
    user_column = as_column(user_row)
    allowed = (user_column == key_user_row) & (
        iota((rows, columns), 1) <= iota((rows, columns), 0) + margin
    )
    weight = allowed.astype(f32)
    return jnp.concatenate([weight, weight], axis=0) > 0.0


def forward_body(
    core_ref, four_ref, mate_four_ref, two_ref, mate_two_ref, mate_own_ref, values_ref, keys_ref, queries_ref, gates_ref,
    inputs_ref, mixed_grad_ref, w_in_ref, w_out_ref, user_ref,
    out_ref, mixed_ref, gate_grad_ref, att_grad_ref, all_keys_ref, all_values_ref, key_user_ref,
):
    rows, width = inputs_ref.shape
    score_scale = 1.0 / math.sqrt(DH)
    halos = nearest_last(
        core_ref[0], four_ref[...], mate_four_ref[...], two_ref[...], mate_two_ref[...], mate_own_ref[...]
    )
    far = jnp.concatenate([block[:rows, :] for block in halos], axis=0)
    margin = far.shape[0]
    for part, own_ref, all_ref in ((1, values_ref, all_values_ref), (3, keys_ref, all_keys_ref)):
        projected = dot(far, w_in_ref[:, part * width : (part + 1) * width])
        all_ref[:margin, :] = (projected * sigmoid(projected)).astype(bf16)
        all_ref[margin:, :] = own_ref[...]
    user_row = user_ref[...]
    key_user = jnp.concatenate(
        [block[rows : rows + 1, :rows].astype(f32) for block in halos] + [user_row], axis=1
    )
    key_user_ref[...] = key_user
    allowed = window_mask(user_row, key_user, margin)
    parts = []
    for pair in range(H // 2):
        columns = slice(2 * DH * pair, 2 * DH * (pair + 1))
        scores = dot_nt(both_heads(queries_ref[:, columns]), all_keys_ref[:, columns]) * score_scale
        weights = jnp.where(allowed, scores * sigmoid(scores), 0.0).astype(bf16)
        parts.append(one_pair(dot(weights, all_values_ref[:, columns])))
    att_hat, att_inv = layer_norm(jnp.concatenate(parts, axis=1))
    gates = gates_ref[...].astype(f32)
    mixed = (att_hat * gates).astype(bf16)
    mixed_ref[...] = mixed
    out_ref[...] = (inputs_ref[...].astype(f32) + dot(mixed, w_out_ref[...])).astype(bf16)
    mixed_grad = mixed_grad_ref[...]
    gate_grad_ref[...] = mixed_grad * att_hat
    att_grad_ref[...] = norm_backward(att_hat, att_inv, mixed_grad * gates).astype(bf16)


def core_first(block, rows):
    width = block.shape[1]
    old = iota((width, width), 0)
    new = iota((width, width), 1)
    inner = jnp.bitwise_and(old, rows - 1)
    device = jnp.right_shift(old, rows.bit_length() - 1)
    place = jnp.bitwise_and(device, 1) * (width // 2) + jnp.right_shift(device, 1) * rows + inner
    return dot(block, hot(new == place)).astype(bf16)


def split_by_core(core, terms, first_owner, piece, first_row, stride, kept_ref, sent_ref):
    half = terms.shape[1] // 2
    even = core == 0
    for local_owner in range(terms.shape[0] // piece):
        owner = first_owner + local_owner
        rows = terms[local_owner * piece : (local_owner + 1) * piece]
        place = first_row + (local_owner // X_CHIPS) * stride
        kept_ref[owner % X_CHIPS, place : place + piece, :] = jnp.where(
            even, rows[:, :half], rows[:, half:]
        ).astype(bf16)
        sent_ref[owner % X_CHIPS, place : place + piece, :] = jnp.where(
            even, rows[:, half:], rows[:, :half]
        ).astype(bf16)


def query_body(
    core_ref, queries_ref, all_keys_ref, all_values_ref, att_grad_ref, gate_grad_ref,
    packed_ref, user_ref, key_user_ref,
    four_ref, mate_four_ref, two_ref, mate_two_ref, mate_own_ref, w_in_ref,
    gate_query_ref, value_key_slope_ref, all_queries_ref, query_user_ref,
):
    rows, width = gate_grad_ref.shape
    score_scale = 1.0 / math.sqrt(DH)
    margin = all_keys_ref.shape[0] - rows
    allowed = window_mask(user_ref[...], key_user_ref[...], margin)
    parts = []
    for pair in range(H // 2):
        columns = slice(2 * DH * pair, 2 * DH * (pair + 1))
        keys = all_keys_ref[:, columns]
        scores = dot_nt(both_heads(queries_ref[:, columns]), keys) * score_scale
        prob_grad = dot_nt(both_heads(att_grad_ref[:, columns]), all_values_ref[:, columns])
        score_grad = jnp.where(allowed, prob_grad * silu_slope(scores), 0.0).astype(bf16)
        parts.append(one_pair(dot(score_grad, keys)) * score_scale)
    query_grad = jnp.concatenate(parts, axis=1)
    normed = packed_ref[:rows, :]
    gate_slope, value_slope, query_slope, key_slope = [
        silu_slope(dot(normed, w_in_ref[:, part * width : (part + 1) * width])) for part in range(4)
    ]
    value_key_slope_ref[:, :width] = value_slope
    value_key_slope_ref[:, width:] = key_slope
    gate_part = gate_grad_ref[...] * gate_slope
    query_part = query_grad * query_slope
    gate_query_ref[:, :width] = gate_part.astype(bf16)
    gate_query_ref[:, width:] = query_part.astype(bf16)
    halos = nearest_first(
        core_ref[0], four_ref[...], mate_four_ref[...], two_ref[...], mate_two_ref[...], mate_own_ref[...]
    )
    far = jnp.concatenate([block[:rows, :] for block in halos], axis=0)
    projected = dot(far, w_in_ref[:, 2 * width : 3 * width])
    all_queries_ref[:rows, :] = queries_ref[...]
    all_queries_ref[rows:, :] = (projected * sigmoid(projected)).astype(bf16)
    query_user_ref[...] = jnp.concatenate(
        [as_column(user_ref[...])]
        + [as_column(block[rows : rows + 1, :rows].astype(f32)) for block in halos],
        axis=0,
    )


def key_terms(queries, query_user, grads, first_row, keys_ref, values_ref, user_row):
    score_scale = 1.0 / math.sqrt(DH)
    total = queries.shape[0]
    rows = user_row.shape[1]
    allowed = (query_user == user_row) & (
        iota((total, rows), 1) <= iota((total, rows), 0) + first_row
    )
    weight = allowed.astype(f32)
    allowed = jnp.concatenate([weight, weight], axis=0) > 0.0
    key_parts = []
    value_parts = []
    for pair in range(H // 2):
        columns = slice(2 * DH * pair, 2 * DH * (pair + 1))
        pair_queries = both_heads(queries[:, columns])
        pair_grads = both_heads(grads[:, columns])
        scores = dot_nt(pair_queries, keys_ref[:, columns]) * score_scale
        sig = sigmoid(scores)
        raw = scores * sig
        weights = jnp.where(allowed, raw, 0.0).astype(bf16)
        prob_grad = dot_nt(pair_grads, values_ref[:, columns])
        score_grad = jnp.where(allowed, prob_grad * (sig + raw * (1.0 - sig)), 0.0).astype(bf16)
        key_parts.append(dot_tn(score_grad, pair_queries) * score_scale)
        value_parts.append(dot_tn(weights, pair_grads))
    return jnp.concatenate(key_parts, axis=1), jnp.concatenate(value_parts, axis=1)


def near_body(
    core_ref, all_queries_ref, query_user_ref, att_grad_ref, two_ref, mate_two_ref, mate_own_ref,
    keys_ref, values_ref, user_ref, key_grad_ref, value_grad_ref,
):
    rows = att_grad_ref.shape[0]
    near = jnp.where(core_ref[0] == 0, mate_own_ref[...], mate_two_ref[...])
    grads = jnp.concatenate([att_grad_ref[...], near, two_ref[...]], axis=0)
    key_grad_ref[...], value_grad_ref[...] = key_terms(
        all_queries_ref[: 3 * rows, :], query_user_ref[: 3 * rows, :], grads, 0,
        keys_ref, values_ref, user_ref[...],
    )


def key_body(
    core_ref, all_queries_ref, query_user_ref, four_ref, mate_four_ref, mate_two_ref,
    keys_ref, values_ref, near_key_ref, near_value_ref, value_key_slope_ref, gate_query_ref,
    w_in_ref, inputs_ref, out_grad_ref, slot_ref, user_ref,
    value_key_ref, outgoing_ref,
):
    rows, width = inputs_ref.shape
    third = jnp.where(core_ref[0] == 0, mate_two_ref[...], mate_four_ref[...])
    far_key, far_value = key_terms(
        all_queries_ref[3 * rows :, :], query_user_ref[3 * rows :, :],
        jnp.concatenate([third, four_ref[...]], axis=0), 3 * rows,
        keys_ref, values_ref, user_ref[...],
    )
    key_grad = near_key_ref[...] + far_key
    value_grad = near_value_ref[...] + far_value
    value_part = (value_grad * value_key_slope_ref[:, :width]).astype(bf16)
    key_part = (key_grad * value_key_slope_ref[:, width:]).astype(bf16)
    value_key_ref[:, :width] = value_part
    value_key_ref[:, width:] = key_part
    joined = jnp.concatenate(
        [gate_query_ref[:, :width], value_part, gate_query_ref[:, width:], key_part], axis=1
    )
    normed_grad = dot_nt(joined, w_in_ref[...])
    input_hat, input_inv = layer_norm(inputs_ref[...].astype(f32))
    inputs_grad = (
        out_grad_ref[...].astype(f32) + norm_backward(input_hat, input_inv, normed_grad)
    ).astype(bf16)
    places = slot_matrix(slot_ref[...], outgoing_ref.shape[0])
    outgoing_ref[...] = dot_tn(places, inputs_grad).astype(bf16)


def early_body(
    piece_in, piece_out, weight_rows,
    core_ref, packed_ref, gate_query_ref, mixed_ref, grad_ref, kept_ref, sent_ref,
):
    rows, width = grad_ref.shape
    core = core_ref[0]
    per_part = width // piece_in
    in_rows = piece_in * per_part // X_CHIPS
    normed = core_first(packed_ref[:rows, :], weight_rows)
    for section, first_owner in ((0, 0), (1, 2 * per_part)):
        terms = dot_tn(gate_query_ref[:, section * width : (section + 1) * width], normed)
        split_by_core(
            core, terms, first_owner, piece_in, section * in_rows, piece_in, kept_ref, sent_ref
        )
    terms = dot_tn(grad_ref[...], core_first(mixed_ref[...], weight_rows))
    split_by_core(core, terms, 0, piece_out, 2 * in_rows, piece_out, kept_ref, sent_ref)


def late_body(
    piece_in, piece_out, weight_rows,
    core_ref, packed_ref, value_key_ref, early_kept_ref, early_sent_ref, kept_ref, sent_ref,
):
    rows = value_key_ref.shape[0]
    width = value_key_ref.shape[1] // 2
    core = core_ref[0]
    piece = piece_in + piece_out
    z_part = width // piece_in // X_CHIPS
    z_chips = kept_ref.shape[1] // piece
    for early_ref, ref in ((early_kept_ref, kept_ref), (early_sent_ref, sent_ref)):
        for z in range(z_chips):
            section, inner = divmod(z, z_part)
            if section % 2 == 0:
                old = (section // 2 * z_part + inner) * piece_in
                ref[:, z * piece : z * piece + piece_in, :] = early_ref[:, old : old + piece_in, :]
            old = 2 * z_part * piece_in + z * piece_out
            ref[:, z * piece + piece_in : (z + 1) * piece, :] = early_ref[:, old : old + piece_out, :]
    normed = core_first(packed_ref[:rows, :], weight_rows)
    for section in range(2):
        terms = dot_tn(value_key_ref[:, section * width : (section + 1) * width], normed)
        split_by_core(
            core, terms, 0, piece_in, (2 * section + 1) * z_part * piece, piece, kept_ref, sent_ref
        )


def table_body(core_ref, asked_ref, arrived_ref, kept_ref, sent_ref):
    slots = asked_ref.shape[1]
    table_dev = kept_ref.shape[2]
    hits = hot(iota((table_dev, slots), 0) == asked_ref[...])
    sums = dot(hits, arrived_ref[...]).T
    rows = kept_ref.shape[1]
    even = core_ref[0] == 0
    for chip in range(kept_ref.shape[0]):
        first = sums[2 * chip * rows : (2 * chip + 1) * rows]
        second = sums[(2 * chip + 1) * rows : (2 * chip + 2) * rows]
        kept_ref[chip] = jnp.where(even, first, second).astype(bf16)
        sent_ref[chip] = jnp.where(even, second, first).astype(bf16)


def pair_sum(kept, sent):
    devices = lax.axis_size("ctx")
    got = lax.ppermute(sent, "ctx", [(i, i ^ 1) for i in range(devices)])
    return (kept.astype(f32) + got.astype(f32)).astype(bf16)


def chips_along_y():
    devices = lax.axis_size("ctx")
    return [list(range(first, devices, 2)) for first in range(2)]


def spread(block, axis, groups):
    return lax.all_to_all(
        block, axis, split_axis=0, concat_axis=0, tiled=True, axis_index_groups=groups
    )


def total_of(blocks):
    return jnp.sum(blocks.astype(f32), axis=0)


def sum_along_x(kept, sent):
    devices = lax.axis_size("dp")
    me = lax.axis_index("dp") % X_CHIPS
    got = swapped(sent)

    def piece(step):
        at = (me + step) % X_CHIPS
        return lax.dynamic_index_in_dim(kept, at, 0, keepdims=False).astype(
            f32
        ) + lax.dynamic_index_in_dim(got, at, 0, keepdims=False).astype(f32)

    total = piece(0)
    for step in range(1, X_CHIPS):
        route = [(i, i - i % X_CHIPS + (i + step) % X_CHIPS) for i in range(devices)]
        total = total + lax.ppermute(piece(step).astype(bf16), "dp", route).astype(f32)
    return total.astype(bf16)


def chips_along_z(owners):
    return [list(range(first, owners, X_CHIPS)) for first in range(X_CHIPS)]


def local(item_ids, segments, touched_rows, w_in, w_out, out_grad):
    rows_dev = segments.shape[1]
    model_width = w_in.shape[0]
    table_dev = touched_rows.shape[0]
    owners = lax.axis_size("dp")
    capacity = max(rows_dev // 4, 6 * rows_dev // owners + 2)
    slots = owners * capacity
    core = (lax.axis_index("ctx") % 2).astype(jnp.int32).reshape(1)
    piece_in = w_in.shape[1] // owners
    piece_out = model_width // owners
    block = (rows_dev, model_width)
    packed_block = (rows_dev + USER_ROWS, model_width)
    reach_block = ((REACH + 1) * rows_dev, model_width)
    chips = lax.axis_size("ctx") // 2
    weight_rows = model_width // (2 * chips)

    user = (segments + 1).astype(f32)
    grad_rows = out_grad[0]
    requests, slot = call(
        lambda *refs: route_body(table_dev, *refs),
        [((owners, capacity), jnp.int32), ((2 * rows_dev, 1), jnp.int32)],
        item_ids.reshape(2, rows_dev),
    )
    asked = lax.all_to_all(requests, "dp", split_axis=0, concat_axis=0, tiled=True)
    found, asked_row = call(
        gather_body, [((slots, model_width), bf16), ((1, slots), jnp.int32)], asked, touched_rows
    )
    fetched = lax.all_to_all(
        found.reshape(owners, capacity, model_width), "dp", split_axis=0, concat_axis=0, tiled=True
    ).reshape(slots, model_width)
    inputs, packed = call(
        embed_body, [(block, bf16), (packed_block, bf16)], slot, fetched, user
    )
    earlier_two = passed_along(packed, "ctx", 2)
    gates, values, queries, keys, mixed_grad = call(
        project_body,
        [
            (block, bf16), (block, bf16), (block, bf16), (block, bf16), (block, f32),
        ],
        packed, w_in, w_out, grad_rows,
        flops=1_500_000_000, moved=6_000_000,
    )
    packed_later, mixed_grad = lax.optimization_barrier((packed, mixed_grad))
    mate_own = swapped(packed_later)
    later_two = passed_along(packed_later, "ctx", -2)
    earlier_two, mixed_grad = lax.optimization_barrier((earlier_two, mixed_grad))
    earlier_four = passed_along(earlier_two, "ctx", 2)
    earlier_four, mate_two, mate_own = lax.optimization_barrier(
        (earlier_four, swapped(earlier_two), mate_own)
    )
    mate_four, later_mate_two = lax.optimization_barrier(
        (mate_of_four(earlier_four, 1), swapped(later_two))
    )
    earlier = (earlier_four, mate_four, earlier_two, mate_two, mate_own)
    later_four = passed_along(later_two, "ctx", -2)
    layer_out, mixed, gate_grad, att_grad, all_keys, all_values, key_user = call(
        forward_body,
        [
            (block, bf16), (block, bf16), (block, f32), (block, bf16),
            (reach_block, bf16), (reach_block, bf16), ((1, (REACH + 1) * rows_dev), f32),
        ],
        *earlier, values, keys, queries, gates, inputs, mixed_grad, w_in, w_out, user,
        core=core, flops=4_000_000_000, moved=8_000_000,
    )
    own_grad = swapped(att_grad, (1,))
    grad_two = passed_along(att_grad, "ctx", -2)
    grad_four = passed_along(grad_two, "ctx", -2)
    later_four, own_grad = lax.optimization_barrier((later_four, own_grad))
    later = (later_four, mate_of_four(later_four, -1), later_two, later_mate_two, mate_own)
    grad_mate_two = swapped(grad_two)
    gate_grad, own_grad, grad_mate_two = lax.optimization_barrier((gate_grad, own_grad, grad_mate_two))
    gate_query, value_key_slope, all_queries, query_user = call(
        query_body,
        [
            ((rows_dev, 2 * model_width), bf16), ((rows_dev, 2 * model_width), f32), (reach_block, bf16),
            (((REACH + 1) * rows_dev, 1), f32),
        ],
        queries, all_keys, all_values, att_grad, gate_grad, packed, user, key_user, *later, w_in,
        core=core, flops=4_000_000_000, moved=8_000_000,
    )
    near_key, near_value = call(
        near_body, [(block, f32), (block, f32)],
        all_queries, query_user, att_grad, grad_two, grad_mate_two, own_grad, keys, values, user,
        core=core, flops=3_000_000_000, moved=3_000_000,
    )
    gate_query, near_key, mixed, grad_four = lax.optimization_barrier(
        (gate_query, near_key, mixed, grad_four)
    )
    grad_mate_four = mate_of_four(grad_four, -1)
    half_width = model_width // 2
    early_block = (X_CHIPS, 3 * model_width // X_CHIPS, half_width)
    early_kept, early_sent = call(
        lambda *refs: early_body(piece_in, piece_out, weight_rows, *refs),
        [(early_block, bf16), (early_block, bf16)],
        packed, gate_query, mixed, grad_rows,
        core=core, flops=2_000_000_000, moved=4_000_000,
    )
    gate_query, early_kept, early_sent = lax.optimization_barrier(
        (gate_query, early_kept, early_sent)
    )
    value_key, outgoing = call(
        key_body,
        [((rows_dev, 2 * model_width), bf16), ((slots, model_width), bf16)],
        all_queries, query_user, grad_four, grad_mate_four, grad_mate_two, keys, values,
        near_key, near_value, value_key_slope, gate_query,
        w_in, inputs, grad_rows, slot, user,
        core=core, flops=4_000_000_000, moved=8_000_000,
    )
    arrived = lax.all_to_all(
        outgoing.reshape(owners, capacity, model_width), "dp", split_axis=0, concat_axis=0, tiled=True
    ).reshape(slots, model_width)
    piece = piece_in + piece_out
    z_chips = owners // X_CHIPS
    weight_block = (X_CHIPS, z_chips * piece, half_width)
    weight_kept, weight_sent = call(
        lambda *refs: late_body(piece_in, piece_out, weight_rows, *refs),
        [(weight_block, bf16), (weight_block, bf16)],
        packed, value_key, early_kept, early_sent,
        core=core, flops=1_500_000_000, moved=3_000_000,
    )
    along_x = sum_along_x(weight_kept, weight_sent).reshape(z_chips, piece, half_width)
    arrived, along_x = lax.optimization_barrier((arrived, along_x))
    along_dp = total_of(spread(along_x, "dp", chips_along_z(owners))).astype(bf16)
    weight_terms = along_dp.T.reshape(chips, weight_rows, piece)
    table_block = (chips, model_width // (2 * chips), table_dev)
    table_kept, table_sent = call(
        table_body, [(table_block, bf16), (table_block, bf16)], asked_row, arrived, core=core
    )
    table_sum = pair_sum(table_kept, table_sent)
    last = jnp.concatenate([table_sum, weight_terms], axis=2)
    summed = total_of(spread(last, "ctx", chips_along_y()))
    table_grad = summed[:, :table_dev].T
    w_in_grad = summed[:, table_dev : table_dev + piece_in]
    w_out_grad = summed[:, table_dev + piece_in :]
    return (layer_out[None], table_grad, w_in_grad, w_out_grad)


def solution(mesh):
    return jax.shard_map(
        local,
        mesh=mesh,
        in_specs=(
            P(None, "dp", "ctx"),
            P("dp", "ctx"),
            P("dp", None),
            P(),
            P(),
            P("dp", "ctx", None),
        ),
        out_specs=(P("dp", "ctx", None), P("dp", "ctx"), P("ctx", "dp"), P("ctx", "dp")),
        check_vma=False,
    )
```

```python
import math

import jax
import jax.numpy as jnp
from jax import lax
from jax.experimental import pallas as pl
from jax.experimental.pallas import tpu as pltpu
from jax.sharding import PartitionSpec as P

H = 8
DH = 64
X_CHIPS = 4
REACH = 4
USER_ROWS = 16

epsilon = 1e-05
f32 = jnp.float32
bf16 = jnp.bfloat16


def passed_along(block, axis, distance):
    devices = range(lax.axis_size(axis))
    route = [(i - distance, i) for i in devices if i - distance in devices]
    return lax.ppermute(block, axis, route)


def swapped(block, senders=(0, 1)):
    devices = range(lax.axis_size("ctx"))
    return lax.ppermute(block, "ctx", [(i, i ^ 1) for i in devices if i % 2 in senders])


def mate_of_four(four, direction):
    return swapped(four, (1,) if direction > 0 else (0,))


def nearest_last(core, four, mate_four, two, mate_two, mate_own):
    even = core == 0
    return (
        four,
        jnp.where(even, mate_four, mate_two),
        two,
        jnp.where(even, mate_two, mate_own),
    )


def nearest_first(core, four, mate_four, two, mate_two, mate_own):
    even = core == 0
    return (
        jnp.where(even, mate_own, mate_two),
        two,
        jnp.where(even, mate_two, mate_four),
        four,
    )


def layer_norm(values):
    centered = values - jnp.mean(values, axis=-1, keepdims=True)
    inverse = lax.rsqrt(jnp.mean(centered * centered, axis=-1, keepdims=True) + epsilon)
    return (centered * inverse, inverse)


def norm_backward(normed, inverse, upstream):
    first_mean = jnp.mean(upstream, axis=-1, keepdims=True)
    second_mean = jnp.mean(upstream * normed, axis=-1, keepdims=True)
    return inverse * (upstream - first_mean - normed * second_mean)


def sigmoid(values):
    return 0.5 * jnp.tanh(0.5 * values) + 0.5


def silu_slope(values):
    sig = sigmoid(values)
    return sig * (1.0 + values * (1.0 - sig))


def iota(shape, dim):
    return lax.broadcasted_iota(jnp.int32, shape, dim)


def dot(left, right):
    return jnp.dot(left, right, preferred_element_type=f32)


def dot_nt(left, right):
    return lax.dot_general(left, right, (((1,), (1,)), ((), ())), preferred_element_type=f32)


def dot_tn(left, right):
    return lax.dot_general(left, right, (((0,), (0,)), ((), ())), preferred_element_type=f32)


def hot(condition):
    return condition.astype(f32).astype(bf16)


def as_column(row):
    length = row.shape[1]
    eye = iota((length, length), 0) == iota((length, length), 1)
    return jnp.sum(jnp.where(eye, jnp.broadcast_to(row, (length, length)), 0.0), axis=1, keepdims=True)


def both_heads(pair):
    low = iota(pair.shape, 1) < DH
    zero = jnp.zeros_like(pair)
    return jnp.concatenate([jnp.where(low, pair, zero), jnp.where(low, zero, pair)], axis=0)


def one_pair(stacked):
    rows = stacked.shape[0] // 2
    low = iota((rows, stacked.shape[1]), 1) < DH
    return jnp.where(low, stacked[:rows], stacked[rows:])


def call(body, outs, *operands, core=None, flops=0, moved=0):
    in_specs = [pl.BlockSpec(memory_space=pltpu.VMEM)] * len(operands)
    if core is not None:
        in_specs = [pl.BlockSpec(memory_space=pltpu.SMEM)] + in_specs
        operands = (core,) + operands
    return pl.pallas_call(
        body,
        out_shape=[jax.ShapeDtypeStruct(shape, kind) for shape, kind in outs],
        in_specs=in_specs,
        compiler_params=pltpu.CompilerParams(vmem_limit_bytes=16 * 1024 * 1024),
        cost_estimate=pl.CostEstimate(flops=flops, bytes_accessed=moved, transcendentals=0),
    )(*operands)


def route_body(table_dev, ids_ref, request_ref, slot_ref):
    owners, capacity = request_ref.shape
    ids = jnp.concatenate([as_column(ids_ref[h : h + 1, :].astype(f32)) for h in range(2)], axis=0)
    ids = ids.astype(jnp.int32)
    count = ids.shape[0]
    shift = table_dev.bit_length() - 1
    owner = jnp.right_shift(ids, shift)
    row = jnp.bitwise_and(ids, table_dev - 1)
    member_f = (owner == iota((count, owners), 1)).astype(f32)
    member = member_f.astype(bf16)
    earlier = hot(iota((count, count), 0) > iota((count, count), 1))
    rank = jnp.sum(dot(earlier, member) * member_f, axis=1, keepdims=True).astype(jnp.int32)
    rank_hot = hot(rank == iota((count, capacity), 1))
    high = (member_f * jnp.right_shift(row, 4).astype(f32)).astype(bf16)
    low = (member_f * jnp.bitwise_and(row, 15).astype(f32)).astype(bf16)
    found = 16.0 * dot_tn(high, rank_hot) + dot_tn(low, rank_hot) + dot_tn(member, rank_hot)
    request_ref[...] = found.astype(jnp.int32) - 1
    slot_ref[...] = owner * capacity + rank


def gather_body(asked_ref, table_ref, found_ref, asked_row_ref):
    asked_rows = asked_ref[...]
    asked_row = jnp.concatenate(
        [asked_rows[g : g + 1, :] for g in range(asked_rows.shape[0])], axis=1
    )
    asked_row_ref[...] = asked_row
    slots = asked_row.shape[1]
    hits = hot(iota((table_ref.shape[0], slots), 0) == asked_row)
    found_ref[...] = dot_tn(hits, table_ref[...]).astype(bf16)


def slot_matrix(slot, slots):
    events = slot.shape[0] // 2
    places = iota((events, slots), 1)
    return hot((slot[:events] == places) | (slot[events:] == places))


def embed_body(slot_ref, fetched_ref, user_ref, inputs_ref, packed_ref):
    rows = inputs_ref.shape[0]
    places = slot_matrix(slot_ref[...], fetched_ref.shape[0])
    inputs = dot(places, fetched_ref[...]).astype(bf16)
    inputs_ref[...] = inputs
    packed_ref[:rows, :] = layer_norm(inputs.astype(f32))[0].astype(bf16)
    packed_ref[rows:, :] = user_rows(user_ref[...], packed_ref.shape[1])


def user_rows(user, width):
    wide = jnp.concatenate([user, jnp.zeros((1, width - user.shape[1]), f32)], axis=1)
    return jnp.broadcast_to(wide, (USER_ROWS, width)).astype(bf16)


def project_body(
    packed_ref, w_in_ref, w_out_ref, grad_ref,
    gates_ref, values_ref, queries_ref, keys_ref, mixed_grad_ref,
):
    rows = grad_ref.shape[0]
    width = grad_ref.shape[1]
    normed = packed_ref[:rows, :]
    for part, out_ref in enumerate((gates_ref, values_ref, queries_ref, keys_ref)):
        columns = slice(part * width, (part + 1) * width)
        projected = dot(normed, w_in_ref[:, columns])
        out_ref[...] = (projected * sigmoid(projected)).astype(bf16)
    mixed_grad_ref[...] = dot_nt(grad_ref[...], w_out_ref[...])


def window_mask(user_row, key_user_row, margin):
    rows = user_row.shape[1]
    columns = key_user_row.shape[1]
    user_column = as_column(user_row)
    allowed = (user_column == key_user_row) & (
        iota((rows, columns), 1) <= iota((rows, columns), 0) + margin
    )
    weight = allowed.astype(f32)
    return jnp.concatenate([weight, weight], axis=0) > 0.0


def forward_body(
    core_ref, four_ref, mate_four_ref, two_ref, mate_two_ref, mate_own_ref, values_ref, keys_ref, queries_ref, gates_ref,
    inputs_ref, mixed_grad_ref, w_in_ref, w_out_ref, user_ref,
    out_ref, mixed_ref, gate_grad_ref, att_grad_ref, all_keys_ref, all_values_ref, key_user_ref,
):
    rows, width = inputs_ref.shape
    score_scale = 1.0 / math.sqrt(DH)
    halos = nearest_last(
        core_ref[0], four_ref[...], mate_four_ref[...], two_ref[...], mate_two_ref[...], mate_own_ref[...]
    )
    far = jnp.concatenate([block[:rows, :] for block in halos], axis=0)
    margin = far.shape[0]
    for part, own_ref, all_ref in ((1, values_ref, all_values_ref), (3, keys_ref, all_keys_ref)):
        projected = dot(far, w_in_ref[:, part * width : (part + 1) * width])
        all_ref[:margin, :] = (projected * sigmoid(projected)).astype(bf16)
        all_ref[margin:, :] = own_ref[...]
    user_row = user_ref[...]
    key_user = jnp.concatenate(
        [block[rows : rows + 1, :rows].astype(f32) for block in halos] + [user_row], axis=1
    )
    key_user_ref[...] = key_user
    allowed = window_mask(user_row, key_user, margin)
    parts = []
    for pair in range(H // 2):
        columns = slice(2 * DH * pair, 2 * DH * (pair + 1))
        scores = dot_nt(both_heads(queries_ref[:, columns]), all_keys_ref[:, columns]) * score_scale
        weights = jnp.where(allowed, scores * sigmoid(scores), 0.0).astype(bf16)
        parts.append(one_pair(dot(weights, all_values_ref[:, columns])))
    att_hat, att_inv = layer_norm(jnp.concatenate(parts, axis=1))
    gates = gates_ref[...].astype(f32)
    mixed = (att_hat * gates).astype(bf16)
    mixed_ref[...] = mixed
    out_ref[...] = (inputs_ref[...].astype(f32) + dot(mixed, w_out_ref[...])).astype(bf16)
    mixed_grad = mixed_grad_ref[...]
    gate_grad_ref[...] = mixed_grad * att_hat
    att_grad_ref[...] = norm_backward(att_hat, att_inv, mixed_grad * gates).astype(bf16)


def core_first(block, rows):
    width = block.shape[1]
    old = iota((width, width), 0)
    new = iota((width, width), 1)
    inner = jnp.bitwise_and(old, rows - 1)
    device = jnp.right_shift(old, rows.bit_length() - 1)
    place = jnp.bitwise_and(device, 1) * (width // 2) + jnp.right_shift(device, 1) * rows + inner
    return dot(block, hot(new == place)).astype(bf16)


def split_by_core(core, terms, first_owner, piece, first_row, stride, kept_ref, sent_ref):
    half = terms.shape[1] // 2
    even = core == 0
    for local_owner in range(terms.shape[0] // piece):
        owner = first_owner + local_owner
        rows = terms[local_owner * piece : (local_owner + 1) * piece]
        place = first_row + (local_owner // X_CHIPS) * stride
        kept_ref[owner % X_CHIPS, place : place + piece, :] = jnp.where(
            even, rows[:, :half], rows[:, half:]
        ).astype(bf16)
        sent_ref[owner % X_CHIPS, place : place + piece, :] = jnp.where(
            even, rows[:, half:], rows[:, :half]
        ).astype(bf16)


def query_body(
    core_ref, queries_ref, all_keys_ref, all_values_ref, att_grad_ref, gate_grad_ref,
    packed_ref, user_ref, key_user_ref,
    four_ref, mate_four_ref, two_ref, mate_two_ref, mate_own_ref, w_in_ref,
    gate_query_ref, value_key_slope_ref, all_queries_ref, query_user_ref,
):
    rows, width = gate_grad_ref.shape
    score_scale = 1.0 / math.sqrt(DH)
    margin = all_keys_ref.shape[0] - rows
    allowed = window_mask(user_ref[...], key_user_ref[...], margin)
    parts = []
    for pair in range(H // 2):
        columns = slice(2 * DH * pair, 2 * DH * (pair + 1))
        keys = all_keys_ref[:, columns]
        scores = dot_nt(both_heads(queries_ref[:, columns]), keys) * score_scale
        prob_grad = dot_nt(both_heads(att_grad_ref[:, columns]), all_values_ref[:, columns])
        score_grad = jnp.where(allowed, prob_grad * silu_slope(scores), 0.0).astype(bf16)
        parts.append(one_pair(dot(score_grad, keys)) * score_scale)
    query_grad = jnp.concatenate(parts, axis=1)
    normed = packed_ref[:rows, :]
    gate_slope, value_slope, query_slope, key_slope = [
        silu_slope(dot(normed, w_in_ref[:, part * width : (part + 1) * width])) for part in range(4)
    ]
    value_key_slope_ref[:, :width] = value_slope
    value_key_slope_ref[:, width:] = key_slope
    gate_part = gate_grad_ref[...] * gate_slope
    query_part = query_grad * query_slope
    gate_query_ref[:, :width] = gate_part.astype(bf16)
    gate_query_ref[:, width:] = query_part.astype(bf16)
    halos = nearest_first(
        core_ref[0], four_ref[...], mate_four_ref[...], two_ref[...], mate_two_ref[...], mate_own_ref[...]
    )
    far = jnp.concatenate([block[:rows, :] for block in halos], axis=0)
    projected = dot(far, w_in_ref[:, 2 * width : 3 * width])
    all_queries_ref[:rows, :] = queries_ref[...]
    all_queries_ref[rows:, :] = (projected * sigmoid(projected)).astype(bf16)
    query_user_ref[...] = jnp.concatenate(
        [as_column(user_ref[...])]
        + [as_column(block[rows : rows + 1, :rows].astype(f32)) for block in halos],
        axis=0,
    )


def key_terms(queries, query_user, grads, first_row, keys_ref, values_ref, user_row):
    score_scale = 1.0 / math.sqrt(DH)
    total = queries.shape[0]
    rows = user_row.shape[1]
    allowed = (query_user == user_row) & (
        iota((total, rows), 1) <= iota((total, rows), 0) + first_row
    )
    weight = allowed.astype(f32)
    allowed = jnp.concatenate([weight, weight], axis=0) > 0.0
    key_parts = []
    value_parts = []
    for pair in range(H // 2):
        columns = slice(2 * DH * pair, 2 * DH * (pair + 1))
        pair_queries = both_heads(queries[:, columns])
        pair_grads = both_heads(grads[:, columns])
        scores = dot_nt(pair_queries, keys_ref[:, columns]) * score_scale
        sig = sigmoid(scores)
        raw = scores * sig
        weights = jnp.where(allowed, raw, 0.0).astype(bf16)
        prob_grad = dot_nt(pair_grads, values_ref[:, columns])
        score_grad = jnp.where(allowed, prob_grad * (sig + raw * (1.0 - sig)), 0.0).astype(bf16)
        key_parts.append(dot_tn(score_grad, pair_queries) * score_scale)
        value_parts.append(dot_tn(weights, pair_grads))
    return jnp.concatenate(key_parts, axis=1), jnp.concatenate(value_parts, axis=1)


def near_body(
    core_ref, all_queries_ref, query_user_ref, att_grad_ref, two_ref, mate_two_ref, mate_own_ref,
    keys_ref, values_ref, user_ref, key_grad_ref, value_grad_ref,
):
    rows = att_grad_ref.shape[0]
    near = jnp.where(core_ref[0] == 0, mate_own_ref[...], mate_two_ref[...])
    grads = jnp.concatenate([att_grad_ref[...], near, two_ref[...]], axis=0)
    key_grad_ref[...], value_grad_ref[...] = key_terms(
        all_queries_ref[: 3 * rows, :], query_user_ref[: 3 * rows, :], grads, 0,
        keys_ref, values_ref, user_ref[...],
    )


def key_body(
    core_ref, all_queries_ref, query_user_ref, four_ref, mate_four_ref, mate_two_ref,
    keys_ref, values_ref, near_key_ref, near_value_ref, value_key_slope_ref, gate_query_ref,
    w_in_ref, inputs_ref, out_grad_ref, slot_ref, user_ref,
    value_key_ref, outgoing_ref,
):
    rows, width = inputs_ref.shape
    third = jnp.where(core_ref[0] == 0, mate_two_ref[...], mate_four_ref[...])
    far_key, far_value = key_terms(
        all_queries_ref[3 * rows :, :], query_user_ref[3 * rows :, :],
        jnp.concatenate([third, four_ref[...]], axis=0), 3 * rows,
        keys_ref, values_ref, user_ref[...],
    )
    key_grad = near_key_ref[...] + far_key
    value_grad = near_value_ref[...] + far_value
    value_part = (value_grad * value_key_slope_ref[:, :width]).astype(bf16)
    key_part = (key_grad * value_key_slope_ref[:, width:]).astype(bf16)
    value_key_ref[:, :width] = value_part
    value_key_ref[:, width:] = key_part
    joined = jnp.concatenate(
        [gate_query_ref[:, :width], value_part, gate_query_ref[:, width:], key_part], axis=1
    )
    normed_grad = dot_nt(joined, w_in_ref[...])
    input_hat, input_inv = layer_norm(inputs_ref[...].astype(f32))
    inputs_grad = (
        out_grad_ref[...].astype(f32) + norm_backward(input_hat, input_inv, normed_grad)
    ).astype(bf16)
    places = slot_matrix(slot_ref[...], outgoing_ref.shape[0])
    outgoing_ref[...] = dot_tn(places, inputs_grad).astype(bf16)


def early_body(
    piece_in, piece_out, weight_rows,
    core_ref, packed_ref, gate_query_ref, mixed_ref, grad_ref, kept_ref, sent_ref,
):
    rows, width = grad_ref.shape
    core = core_ref[0]
    per_part = width // piece_in
    in_rows = piece_in * per_part // X_CHIPS
    normed = core_first(packed_ref[:rows, :], weight_rows)
    for section, first_owner in ((0, 0), (1, 2 * per_part)):
        terms = dot_tn(gate_query_ref[:, section * width : (section + 1) * width], normed)
        split_by_core(
            core, terms, first_owner, piece_in, section * in_rows, piece_in, kept_ref, sent_ref
        )
    terms = dot_tn(grad_ref[...], core_first(mixed_ref[...], weight_rows))
    split_by_core(core, terms, 0, piece_out, 2 * in_rows, piece_out, kept_ref, sent_ref)


def late_body(
    piece_in, piece_out, weight_rows,
    core_ref, packed_ref, value_key_ref, early_kept_ref, early_sent_ref, kept_ref, sent_ref,
):
    rows = value_key_ref.shape[0]
    width = value_key_ref.shape[1] // 2
    core = core_ref[0]
    piece = piece_in + piece_out
    z_part = width // piece_in // X_CHIPS
    z_chips = kept_ref.shape[1] // piece
    for early_ref, ref in ((early_kept_ref, kept_ref), (early_sent_ref, sent_ref)):
        for z in range(z_chips):
            section, inner = divmod(z, z_part)
            if section % 2 == 0:
                old = (section // 2 * z_part + inner) * piece_in
                ref[:, z * piece : z * piece + piece_in, :] = early_ref[:, old : old + piece_in, :]
            old = 2 * z_part * piece_in + z * piece_out
            ref[:, z * piece + piece_in : (z + 1) * piece, :] = early_ref[:, old : old + piece_out, :]
    normed = core_first(packed_ref[:rows, :], weight_rows)
    for section in range(2):
        terms = dot_tn(value_key_ref[:, section * width : (section + 1) * width], normed)
        split_by_core(
            core, terms, 0, piece_in, (2 * section + 1) * z_part * piece, piece, kept_ref, sent_ref
        )


def table_body(core_ref, asked_ref, arrived_ref, kept_ref, sent_ref):
    slots = asked_ref.shape[1]
    table_dev = kept_ref.shape[2]
    hits = hot(iota((table_dev, slots), 0) == asked_ref[...])
    sums = dot(hits, arrived_ref[...]).T
    rows = kept_ref.shape[1]
    even = core_ref[0] == 0
    for chip in range(kept_ref.shape[0]):
        first = sums[2 * chip * rows : (2 * chip + 1) * rows]
        second = sums[(2 * chip + 1) * rows : (2 * chip + 2) * rows]
        kept_ref[chip] = jnp.where(even, first, second).astype(bf16)
        sent_ref[chip] = jnp.where(even, second, first).astype(bf16)


def pair_sum(kept, sent):
    devices = lax.axis_size("ctx")
    got = lax.ppermute(sent, "ctx", [(i, i ^ 1) for i in range(devices)])
    return (kept.astype(f32) + got.astype(f32)).astype(bf16)


def chips_along_y():
    devices = lax.axis_size("ctx")
    return [list(range(first, devices, 2)) for first in range(2)]


def spread(block, axis, groups):
    return lax.all_to_all(
        block, axis, split_axis=0, concat_axis=0, tiled=True, axis_index_groups=groups
    )


def total_of(blocks):
    return jnp.sum(blocks.astype(f32), axis=0)


def sum_along_x(kept, sent):
    devices = lax.axis_size("dp")
    me = lax.axis_index("dp") % X_CHIPS
    got = swapped(sent)

    def piece(step):
        at = (me + step) % X_CHIPS
        return lax.dynamic_index_in_dim(kept, at, 0, keepdims=False).astype(
            f32
        ) + lax.dynamic_index_in_dim(got, at, 0, keepdims=False).astype(f32)

    total = piece(0)
    for step in range(1, X_CHIPS):
        route = [(i, i - i % X_CHIPS + (i + step) % X_CHIPS) for i in range(devices)]
        total = total + lax.ppermute(piece(step).astype(bf16), "dp", route).astype(f32)
    return total.astype(bf16)


def chips_along_z(owners):
    return [list(range(first, owners, X_CHIPS)) for first in range(X_CHIPS)]


def local(item_ids, segments, touched_rows, w_in, w_out, out_grad):
    rows_dev = segments.shape[1]
    model_width = w_in.shape[0]
    table_dev = touched_rows.shape[0]
    owners = lax.axis_size("dp")
    capacity = max(rows_dev // 4, 6 * rows_dev // owners + 2)
    slots = owners * capacity
    core = (lax.axis_index("ctx") % 2).astype(jnp.int32).reshape(1)
    piece_in = w_in.shape[1] // owners
    piece_out = model_width // owners
    block = (rows_dev, model_width)
    packed_block = (rows_dev + USER_ROWS, model_width)
    reach_block = ((REACH + 1) * rows_dev, model_width)
    chips = lax.axis_size("ctx") // 2
    weight_rows = model_width // (2 * chips)

    user = (segments + 1).astype(f32)
    grad_rows = out_grad[0]
    requests, slot = call(
        lambda *refs: route_body(table_dev, *refs),
        [((owners, capacity), jnp.int32), ((2 * rows_dev, 1), jnp.int32)],
        item_ids.reshape(2, rows_dev),
    )
    asked = lax.all_to_all(requests, "dp", split_axis=0, concat_axis=0, tiled=True)
    found, asked_row = call(
        gather_body, [((slots, model_width), bf16), ((1, slots), jnp.int32)], asked, touched_rows
    )
    fetched = lax.all_to_all(
        found.reshape(owners, capacity, model_width), "dp", split_axis=0, concat_axis=0, tiled=True
    ).reshape(slots, model_width)
    inputs, packed = call(
        embed_body, [(block, bf16), (packed_block, bf16)], slot, fetched, user
    )
    earlier_two = passed_along(packed, "ctx", 2)
    gates, values, queries, keys, mixed_grad = call(
        project_body,
        [
            (block, bf16), (block, bf16), (block, bf16), (block, bf16), (block, f32),
        ],
        packed, w_in, w_out, grad_rows,
        flops=1_500_000_000, moved=6_000_000,
    )
    packed_later, mixed_grad = lax.optimization_barrier((packed, mixed_grad))
    mate_own = swapped(packed_later)
    later_two = passed_along(packed_later, "ctx", -2)
    earlier_two, mixed_grad = lax.optimization_barrier((earlier_two, mixed_grad))
    earlier_four = passed_along(earlier_two, "ctx", 2)
    earlier_four, mate_two, mate_own = lax.optimization_barrier(
        (earlier_four, swapped(earlier_two), mate_own)
    )
    earlier = (earlier_four, mate_of_four(earlier_four, 1), earlier_two, mate_two, mate_own)
    later_four = passed_along(later_two, "ctx", -2)
    layer_out, mixed, gate_grad, att_grad, all_keys, all_values, key_user = call(
        forward_body,
        [
            (block, bf16), (block, bf16), (block, f32), (block, bf16),
            (reach_block, bf16), (reach_block, bf16), ((1, (REACH + 1) * rows_dev), f32),
        ],
        *earlier, values, keys, queries, gates, inputs, mixed_grad, w_in, w_out, user,
        core=core, flops=4_000_000_000, moved=8_000_000,
    )
    own_grad = swapped(att_grad, (1,))
    grad_two = passed_along(att_grad, "ctx", -2)
    grad_four = passed_along(grad_two, "ctx", -2)
    later_four, later_two, own_grad = lax.optimization_barrier((later_four, later_two, own_grad))
    later = (later_four, mate_of_four(later_four, -1), later_two, swapped(later_two), mate_own)
    grad_mate_two = swapped(grad_two)
    gate_grad, own_grad, grad_mate_two = lax.optimization_barrier((gate_grad, own_grad, grad_mate_two))
    gate_query, value_key_slope, all_queries, query_user = call(
        query_body,
        [
            ((rows_dev, 2 * model_width), bf16), ((rows_dev, 2 * model_width), f32), (reach_block, bf16),
            (((REACH + 1) * rows_dev, 1), f32),
        ],
        queries, all_keys, all_values, att_grad, gate_grad, packed, user, key_user, *later, w_in,
        core=core, flops=4_000_000_000, moved=8_000_000,
    )
    near_key, near_value = call(
        near_body, [(block, f32), (block, f32)],
        all_queries, query_user, att_grad, grad_two, grad_mate_two, own_grad, keys, values, user,
        core=core, flops=3_000_000_000, moved=3_000_000,
    )
    gate_query, near_key, mixed, grad_four = lax.optimization_barrier(
        (gate_query, near_key, mixed, grad_four)
    )
    grad_mate_four = mate_of_four(grad_four, -1)
    half_width = model_width // 2
    early_block = (X_CHIPS, 3 * model_width // X_CHIPS, half_width)
    early_kept, early_sent = call(
        lambda *refs: early_body(piece_in, piece_out, weight_rows, *refs),
        [(early_block, bf16), (early_block, bf16)],
        packed, gate_query, mixed, grad_rows,
        core=core, flops=2_000_000_000, moved=4_000_000,
    )
    gate_query, early_kept, early_sent = lax.optimization_barrier(
        (gate_query, early_kept, early_sent)
    )
    value_key, outgoing = call(
        key_body,
        [((rows_dev, 2 * model_width), bf16), ((slots, model_width), bf16)],
        all_queries, query_user, grad_four, grad_mate_four, grad_mate_two, keys, values,
        near_key, near_value, value_key_slope, gate_query,
        w_in, inputs, grad_rows, slot, user,
        core=core, flops=4_000_000_000, moved=8_000_000,
    )
    arrived = lax.all_to_all(
        outgoing.reshape(owners, capacity, model_width), "dp", split_axis=0, concat_axis=0, tiled=True
    ).reshape(slots, model_width)
    piece = piece_in + piece_out
    z_chips = owners // X_CHIPS
    weight_block = (X_CHIPS, z_chips * piece, half_width)
    weight_kept, weight_sent = call(
        lambda *refs: late_body(piece_in, piece_out, weight_rows, *refs),
        [(weight_block, bf16), (weight_block, bf16)],
        packed, value_key, early_kept, early_sent,
        core=core, flops=1_500_000_000, moved=3_000_000,
    )
    along_x = sum_along_x(weight_kept, weight_sent).reshape(z_chips, piece, half_width)
    arrived, along_x = lax.optimization_barrier((arrived, along_x))
    along_dp = total_of(spread(along_x, "dp", chips_along_z(owners))).astype(bf16)
    weight_terms = along_dp.T.reshape(chips, weight_rows, piece)
    table_block = (chips, model_width // (2 * chips), table_dev)
    table_kept, table_sent = call(
        table_body, [(table_block, bf16), (table_block, bf16)], asked_row, arrived, core=core
    )
    table_sum = pair_sum(table_kept, table_sent)
    last = jnp.concatenate([table_sum, weight_terms], axis=2)
    summed = total_of(spread(last, "ctx", chips_along_y()))
    table_grad = summed[:, :table_dev].T
    w_in_grad = summed[:, table_dev : table_dev + piece_in]
    w_out_grad = summed[:, table_dev + piece_in :]
    return (layer_out[None], table_grad, w_in_grad, w_out_grad)


def solution(mesh):
    return jax.shard_map(
        local,
        mesh=mesh,
        in_specs=(
            P(None, "dp", "ctx"),
            P("dp", "ctx"),
            P("dp", None),
            P(),
            P(),
            P("dp", "ctx", None),
        ),
        out_specs=(P("dp", "ctx", None), P("dp", "ctx"), P("ctx", "dp"), P("ctx", "dp")),
        check_vma=False,
    )
```
